512 devices in a mesh: grp: 4 (over x), ado: 128 (over z, y, core).
Axes of the slice: x: 4, y: 8, z: 8, core: 2. Of those that a mesh axis runs over, the one named last changes fastest.
Arguments:
- states: bfloat16 [4, 128, 128, 64, 128], P('grp', 'ado'), may hold values from -6 to 6
- send_slot: int32 [4, 128, 128, 3], P('grp', 'ado'), may hold values from -1 to 127, as said below
- window_tier_states: bfloat16 [2048, 64, 128], P('ado', 'grp'), may hold values from -6 to 6
- modes_tri: int32 [2048, 3], P('ado'), may hold values from 0 to 127, as said below
- use_up: int32 [2048, 128], P('ado', 'grp'), may hold values from 0 to 383, as said below
- use_down: int32 [2048, 3], P('ado'), may hold values from 0 to 383, as said below
- hamiltonian: bfloat16 [64, 64], replicated, may hold values from -4 to 4, as said below
- coupling: bfloat16 [128, 64, 64], P('grp'), may hold values from -1 to 1, as said below
- coup_re: float32 [128], P('grp'), may hold values from 1 to 4
- coup_im: float32 [128], P('grp'), may hold values from -6 to 6
- decay_rate: float32 [128], replicated, may hold values from 0.1 to 2
Outputs:
- increment: float32 [2048, 64, 128], P('ado', 'grp')
The draws below stay inside these ranges and needn't reach their ends.
Inputs may be any that keep to these rules, and one draw needn't show every extreme that they name: send_slot[g, j, i, c] is a slot of the stored states of the device (g, j); -1 marks an empty place. For each sending device (g, j) and receiving ado index i the live places come first, 1 to 3 of them; for every receiving device some owner fills all 3. `modes_tri`: each row lists a tier-3 multi-index in rising order, a mode repeated as often as it is occupied. use_up[w, k] names a live place, and every live place received by a device is named by some entry of use_up for that device. use_down[w, t] names a live place of the device of grp index modes_tri[w, t] // 32. `hamiltonian`: Symmetric. `coupling`: each mode's matrix is symmetric.
All inputs are finite; a program needn't handle non-finite values.
Results may differ from the reference program's by a relative error of at most 0.0003.
Values may be sent and summed in bfloat16 or wider, within the bound.
No kernel may reach another device: no remote copies, remote signals or barrier semaphores. Data moves between devices by JAX's collectives and lax.ppermute only.
A program may use at most 64 MiB of HBM per device.

```python
import math
import jax
import jax.numpy as jnp
from jax import lax

NS = 64
MODES = 128
DOWN = 3
CAP = 3
OWN_DEV = 128
WINDOW_PER_ADO = 16
MODES_G = 32
WIN = 2048
N_GRP = 4
N_ADO = 128


def layout(key):
    keys = jax.random.split(key, 7)
    counts = jax.random.randint(keys[0], (N_GRP, N_ADO, N_ADO), 1, CAP + 1)
    forced = jax.random.randint(keys[1], (N_GRP, N_ADO, 1), 0, N_ADO)
    owners = jnp.arange(N_ADO, dtype=jnp.int32)
    counts = jnp.where(owners == forced, CAP, counts)
    places = jnp.arange(CAP, dtype=jnp.int32)
    live = places < counts[..., None]
    raw_slots = jax.random.randint(keys[2], (N_GRP, N_ADO, N_ADO, CAP), 0, OWN_DEV)
    send_slot = jnp.where(jnp.transpose(live, (0, 2, 1, 3)), raw_slots, -1).astype(jnp.int32)
    live_flat = live.reshape(N_GRP, N_ADO, N_ADO * CAP)
    order = jnp.argsort(jnp.where(live_flat, 0, 1), axis=-1, stable=True).astype(jnp.int32)
    total_live = jnp.sum(live_flat.astype(jnp.int32), axis=-1)
    uses = WINDOW_PER_ADO * MODES_G
    scores = jax.random.randint(keys[3], (N_GRP, N_ADO, uses), 0, 2 ** 30)
    ranks = jnp.argsort(scores, axis=-1, stable=True).astype(jnp.int32)
    extra = jax.random.randint(keys[4], (N_GRP, N_ADO, uses), 0, 2 ** 30)
    pick = jnp.where(ranks < total_live[..., None], ranks, extra % total_live[..., None])
    up_pos = jnp.take_along_axis(order, pick, axis=-1)
    up_pos = up_pos.reshape(N_GRP, N_ADO, WINDOW_PER_ADO, MODES_G).transpose(1, 2, 0, 3).reshape(N_ADO * WINDOW_PER_ADO, MODES)
    triple = jnp.sort(jax.random.randint(keys[5], (N_ADO * WINDOW_PER_ADO, DOWN), 0, MODES), axis=-1).astype(jnp.int32)
    mode_groupings = triple // MODES_G
    receiver = (jnp.arange(N_ADO * WINDOW_PER_ADO, dtype=jnp.int32) // WINDOW_PER_ADO)[:, None]
    lows = jax.random.randint(keys[6], (N_ADO * WINDOW_PER_ADO, DOWN), 0, 2 ** 30)
    avail = total_live[mode_groupings, receiver]
    down_pos = order[mode_groupings, receiver, lows % avail]
    return (send_slot, triple, up_pos.astype(jnp.int32), down_pos.astype(jnp.int32))


def draw_send_slot(key, part):
    shared = layout(key)
    return shared[0]


def draw_modes_tri(key, part):
    shared = layout(key)
    return shared[1]


def draw_use_up(key, part):
    shared = layout(key)
    return shared[2]


def draw_use_down(key, part):
    shared = layout(key)
    return shared[3]


def draw_hamiltonian(key, part):
    key = jax.random.fold_in(key, 11)
    first, second = jax.random.split(key)
    noise = jax.random.truncated_normal(first, -4.0, 4.0, (NS, NS), jnp.float32)
    energies = jax.random.uniform(second, (NS,), jnp.float32, -2.0, 2.0)
    return ((noise + noise.T) * (2.0 * NS) ** (-0.5) + jnp.diag(energies)).astype(jnp.bfloat16)


def draw_coupling(key, part):
    key = jax.random.fold_in(key, 13)
    first, second = jax.random.split(key)
    noise = jax.random.truncated_normal(first, -4.0, 4.0, (MODES, NS, NS), jnp.float32)
    spread = jnp.exp(jax.random.uniform(second, (MODES, 1, 1), jnp.float32, -0.7, 0.7))
    paired = noise + jnp.transpose(noise, (0, 2, 1))
    return (paired * spread * (2.0 * NS * MODES) ** (-0.5)).astype(jnp.bfloat16)


def block_levels(own_key, extent, cuts, low, high):
    factor_of, own = 1.0, jax.random.fold_in(own_key, 6)
    for dim, blocks in cuts:
        steps = jnp.exp(jax.random.uniform(jax.random.fold_in(own, dim), (blocks,), jnp.float32, low / len(cuts), high / len(cuts)))
        factor_of = factor_of * jnp.repeat(steps, extent[dim] // blocks).reshape([-1 if axis == dim else 1 for axis in range(len(extent))])
    return factor_of


def gaussian(own_key, dims, deviation, most, shards=(), kind=jnp.bfloat16):
    drawn = jax.random.normal(own_key, dims, jnp.float32) * deviation
    if len(shards) > 0:
        drawn = block_levels(own_key, dims, shards, -0.22, 0.18) * drawn
    return jnp.clip(drawn, min=-most, max=most).astype(kind)


def setup_inputs(seed: int = 0) -> dict:
    key_of = jax.random.split(jax.random.key(seed), 12)
    states = gaussian(key_of[0], (N_GRP, N_ADO, OWN_DEV, NS, 2 * NS), 1.0, 6.0, ((0, 4), (1, 128)))
    send_slot = draw_send_slot(jax.random.fold_in(key_of[11], 71), 0)
    window_tier_states = gaussian(key_of[2], (WIN, NS, 2 * NS), 1.0, 6.0, ((0, 128), (1, 4)))
    modes_tri = draw_modes_tri(jax.random.fold_in(key_of[11], 71), 0)
    use_up = draw_use_up(jax.random.fold_in(key_of[11], 71), 0)
    use_down = draw_use_down(jax.random.fold_in(key_of[11], 71), 0)
    hamiltonian = draw_hamiltonian(jax.random.fold_in(key_of[11], 71), 0)
    coupling = draw_coupling(jax.random.fold_in(key_of[11], 71), 0)
    coup_re = jnp.clip(jnp.exp(math.log(4.0) - 1.3862944 * jax.random.uniform(key_of[8], (MODES,), jnp.float32) ** block_levels(key_of[8], (MODES,), ((0, 4),), -0.2, 0.2)), 1.0, 4.0)
    coup_im = gaussian(key_of[9], (MODES,), 2.0, 6.0, ((0, 4),), jnp.float32)
    decay_rate = jnp.clip(jnp.exp(jax.random.uniform(key_of[10], (MODES,), jnp.float32, math.log(0.1), math.log(2.0))), 0.1, 2.0)
    return {"states": states, "send_slot": send_slot, "window_tier_states": window_tier_states, "modes_tri": modes_tri, "use_up": use_up, "use_down": use_down, "hamiltonian": hamiltonian, "coupling": coupling, "coup_re": coup_re, "coup_im": coup_im, "decay_rate": decay_rate}


def rotate(parts, width):
    return jnp.concatenate([parts[..., width:], -parts[..., :width]], axis=-1)


def reference(states, send_slot, window_tier_states, modes_tri, use_up, use_down, hamiltonian, coupling, coup_re, coup_im, decay_rate):
    maps = coupling.astype(jnp.float32)
    ham = hamiltonian.astype(jnp.float32)
    every_mode = jnp.arange(MODES, dtype=jnp.int32)
    mode_group = every_mode // MODES_G

    def one_window(items):
        rho, up_places, triple, down_places, index = items
        receiver = index // WINDOW_PER_ADO
        owner = up_places // CAP
        slot = send_slot[mode_group, owner, receiver, up_places % CAP]
        pulled = states[mode_group, owner, slot].astype(jnp.float32)
        left = jnp.einsum("mab,mbc->ac", maps, pulled)
        right = jnp.einsum("maib,mbc->aic", pulled.reshape(MODES, NS, 2, NS), maps).reshape(NS, 2 * NS)
        upsum = rotate(left - right, NS)
        down_group = triple // MODES_G
        down_owner = down_places // CAP
        lower_tier_slot = send_slot[down_group, down_owner, receiver, down_places % CAP]
        lower_tier = states[down_group, down_owner, lower_tier_slot].astype(jnp.float32)
        lower_tier_lookup = maps[triple]
        left_factor = jnp.einsum("owi,oip->owp", lower_tier_lookup, lower_tier)
        right_d = jnp.einsum("taib,tbc->taic", lower_tier.reshape(DOWN, NS, 2, NS), lower_tier_lookup).reshape(DOWN, NS, 2 * NS)
        minus = left_factor - right_d
        plus = left_factor + right_d
        real_c = coup_re[triple][:, None, None]
        imag_c = coup_im[triple][:, None, None]
        dreal = jnp.sum(real_c * minus[..., :NS] - imag_c * plus[..., NS:], axis=0)
        dimag = jnp.sum(real_c * minus[..., NS:] + imag_c * plus[..., :NS], axis=0)
        downsum = jnp.concatenate([dimag, -dreal], axis=-1)
        rho_f = rho.astype(jnp.float32)
        left_h = jnp.dot(ham, rho_f)
        right_h = jnp.einsum("aib,bc->aic", rho_f.reshape(NS, 2, NS), ham).reshape(NS, 2 * NS)
        damping = jnp.sum(decay_rate[triple])
        local = rotate(left_h - right_h, NS) - damping * rho_f
        return 0.5 * (upsum + downsum + local)

    indices = jnp.arange(WIN, dtype=jnp.int32)
    return lax.map(one_window, (window_tier_states, use_up, modes_tri, use_down, indices))
```

```python
import jax
import jax.numpy as jnp
from jax import lax
from jax.experimental import pallas as pl
from jax.experimental.pallas import tpu as pltpu
from jax.sharding import PartitionSpec as P

STEP_WEIGHT = 0.5
F32 = jnp.float32
BF16 = jnp.bfloat16
VMEM = pl.BlockSpec(memory_space=pltpu.VMEM)
SMEM = pl.BlockSpec(memory_space=pltpu.SMEM)


def doubled(matrices):
    empty = jnp.zeros_like(matrices)
    upper_half = jnp.concatenate([matrices, empty], axis=-1)
    lower_half = jnp.concatenate([empty, matrices], axis=-1)
    return jnp.concatenate([upper_half, lower_half], axis=-2)


def rotate(parts):
    width = parts.shape[-1] // 2
    return jnp.concatenate([parts[..., width:], -parts[..., :width]], axis=-1)


def pick_kernel(slot_ref, store_ref, out_ref):
    base = pl.program_id(0) * out_ref.shape[0]
    for row in range(out_ref.shape[0]):
        out_ref[row] = store_ref[jnp.maximum(slot_ref[base + row], 0)]


def pick(slots, store, steps):
    total = slots.shape[0]
    block = total // steps
    return pl.pallas_call(
        pick_kernel,
        grid=(steps,),
        in_specs=[SMEM, pl.BlockSpec(store.shape, lambda i: (0, 0, 0))],
        out_specs=pl.BlockSpec((block,) + store.shape[1:], lambda i: (i, 0, 0)),
        out_shape=jax.ShapeDtypeStruct((total,) + store.shape[1:], store.dtype),
        compiler_params=pltpu.CompilerParams(vmem_limit_bytes=24 * 2**20),
        cost_estimate=pl.CostEstimate(flops=0, bytes_accessed=8 * 2**20, transcendentals=0),
    )(slots, store)


def terms_kernel(
    group_ref, up_ref, down_ref, tri_ref, re_ref, im_ref,
    flat_ref, left_ref, wide_ref, maps_ref, ham_ref, rho_ref,
    out_ref, tall, long,
):
    group = group_ref[0]
    windows, modes = up_ref.shape
    width = ham_ref.shape[0]

    def pair(step, carry):
        for j in range(2):
            w = step * 2 + j
            for k in range(modes):
                tile = flat_ref[up_ref[w, k]]
                tall[k * width:(k + 1) * width, j * 128:(j + 1) * 128] = tile
                long[j * width:(j + 1) * width, k * 128:(k + 1) * 128] = tile
        left = jnp.dot(left_ref[...], tall[...], preferred_element_type=F32)
        right = jnp.dot(long[...], wide_ref[...], preferred_element_type=F32)
        for j in range(2):
            w = step * 2 + j
            head = jnp.dot(ham_ref[...], rho_ref[w], preferred_element_type=F32)
            diff = left[:, j * 128:(j + 1) * 128] - right[j * width:(j + 1) * width] + head
            out_ref[w] = rotate(diff)
            for t in range(tri_ref.shape[0]):
                mode = tri_ref[t, w] - group * modes

                @pl.when((mode >= 0) & (mode < modes))
                def _():
                    state = flat_ref[down_ref[t, w]]
                    lower = jnp.dot(maps_ref[mode], state, preferred_element_type=F32)
                    start = pl.multiple_of(mode * 128, 128)
                    higher = jnp.dot(state, wide_ref[pl.ds(start, 128), :], preferred_element_type=F32)
                    out_ref[w] += re_ref[mode] * rotate(lower - higher) + im_ref[mode] * (lower + higher)
        return carry

    lax.fori_loop(0, windows // 2, pair, 0)


def on_device(
    states, send_slot, window_tier_states, modes_tri, use_up, use_down,
    hamiltonian, coupling, coup_re, coup_im, decay_rate,
):
    width = hamiltonian.shape[0]
    windows, share = window_tier_states.shape[:2]
    modes = coupling.shape[0]
    group = lax.axis_index("grp")
    slots = send_slot.reshape(-1)
    picked = pick(slots, states[0, 0], 8).reshape(send_slot.shape[2:] + states.shape[3:])
    received = lax.all_to_all(picked, "ado", split_axis=0, concat_axis=0, tiled=True)
    flat = received.reshape(-1, width, 2 * width)

    maps_wide = doubled(coupling).reshape(modes * 2 * width, 2 * width)
    maps_left = jnp.swapaxes(coupling, 0, 1).reshape(width, modes * width)
    ham_wide = doubled(hamiltonian)
    head_cols = lax.dynamic_slice_in_dim(hamiltonian, group * share, share, 1)
    right_part = jnp.einsum("wab,bc->wac", window_tier_states, ham_wide, preferred_element_type=F32)
    every_mode = jnp.arange(decay_rate.shape[0], dtype=jnp.int32)
    hits = modes_tri[:, :, None] == every_mode
    damping = jnp.sum(jnp.where(hits, decay_rate, 0.0), axis=(1, 2))
    own = rotate(right_part) + damping[:, None, None] * window_tier_states.astype(F32)

    partial_value = pl.pallas_call(
        terms_kernel,
        in_specs=[SMEM] * 6 + [VMEM] * 6,
        out_specs=VMEM,
        out_shape=jax.ShapeDtypeStruct((windows, width, 2 * width), F32),
        scratch_shapes=[
            pltpu.VMEM((modes * width, 256), BF16),
            pltpu.VMEM((2 * width, modes * 128), BF16),
        ],
        compiler_params=pltpu.CompilerParams(vmem_limit_bytes=32 * 2**20),
        cost_estimate=pl.CostEstimate(flops=2 * 10**9, bytes_accessed=10 * 2**20, transcendentals=0),
    )(
        jnp.reshape(group, (1,)).astype(jnp.int32), use_up, use_down.T, modes_tri.T, coup_re, coup_im,
        flat, maps_left, maps_wide, coupling, head_cols, window_tier_states,
    )
    blocks = partial_value.reshape(windows, width // share, share, 2 * width)
    count = width // share
    total = lax.dynamic_index_in_dim(blocks, group, 1, keepdims=False)
    for shift in (2, 1, 3):
        block = lax.dynamic_index_in_dim(blocks, lax.rem(group + shift, count), 1, keepdims=False)
        total = total + lax.ppermute(block, "grp", [(i, (i + shift) % count) for i in range(count)])
    return STEP_WEIGHT * (total - own)


def solution(mesh):
    in_specs = (
        P("grp", "ado", None, None, None),
        P("grp", "ado", None, None),
        P("ado", "grp", None),
        P("ado", None),
        P("ado", "grp"),
        P("ado", None),
        P(),
        P("grp", None, None),
        P("grp"),
        P("grp"),
        P(),
    )
    out_specs = P("ado", "grp", None)
    return jax.shard_map(
        on_device, mesh=mesh, in_specs=in_specs, out_specs=out_specs, check_vma=False
    )
```

```python
import jax
import jax.numpy as jnp
from jax import lax
from jax.experimental import pallas as pl
from jax.experimental.pallas import tpu as pltpu
from jax.sharding import PartitionSpec as P

STEP_WEIGHT = 0.5
F32 = jnp.float32
BF16 = jnp.bfloat16
LINK = jnp.float16
VMEM = pl.BlockSpec(memory_space=pltpu.VMEM)
SMEM = pl.BlockSpec(memory_space=pltpu.SMEM)


def doubled(matrices):
    empty = jnp.zeros_like(matrices)
    upper_half = jnp.concatenate([matrices, empty], axis=-1)
    lower_half = jnp.concatenate([empty, matrices], axis=-1)
    return jnp.concatenate([upper_half, lower_half], axis=-2)


def rotate(parts):
    width = parts.shape[-1] // 2
    return jnp.concatenate([parts[..., width:], -parts[..., :width]], axis=-1)

RINGS = 8
CAP = 3
LOT = 8
ROWS = 40
GRID = [(z, y, c) for z in range(RINGS) for y in range(RINGS) for c in range(2)]
COLLECT = [[z * 16 + y * 2 for z in range(RINGS)] for y in range(RINGS)] + [
    [z * 16 + y * 2 + 1 for y in range(RINGS)] for z in range(RINGS)
]
DELIVER = [[z * 16 + y * 2 for y in range(RINGS)] for z in range(RINGS)] + [
    [z * 16 + y * 2 + 1 for z in range(RINGS)] for y in range(RINGS)
]
SIBLING = [(i, i ^ 1) for i in range(2 * RINGS * RINGS)]


def pick_kernel(core_ref, own_slot, sib_slot, own_ref, sib_ref, out_ref):
    core = core_ref[0]
    target = pl.program_id(0)
    first = jnp.where(core == 0, target * 16, target * 2 + 1)
    step = jnp.where(core == 0, 2, 16)
    count = own_slot.shape[0] // CAP
    for kind, (slots, store) in enumerate(((own_slot, own_ref), (sib_slot, sib_ref))):
        for c in range(CAP):
            for r in range(RINGS):
                slot = slots[c * count + first + r * step]
                out_ref[0, kind * CAP * RINGS + c * RINGS + r] = store[jnp.maximum(slot, 0)]


def pick(core, own_slots, sib_slots, own, sib):
    tile = own.shape[1:]
    whole = pl.BlockSpec(own.shape, lambda i: (0, 0, 0))
    block = 2 * CAP * RINGS
    return pl.pallas_call(
        pick_kernel,
        grid=(RINGS,),
        in_specs=[SMEM, SMEM, SMEM, whole, whole],
        out_specs=pl.BlockSpec((1, block) + tile, lambda i: (i, 0, 0, 0)),
        out_shape=jax.ShapeDtypeStruct((RINGS, block) + tile, own.dtype),
        compiler_params=pltpu.CompilerParams(vmem_limit_bytes=24 * 2**20),
        cost_estimate=pl.CostEstimate(flops=0, bytes_accessed=10 * 2**20, transcendentals=0),
    )(core, own_slots, sib_slots, own, sib)


def terms_kernel(
    spot_ref, list_ref, re_ref, im_ref, flat_ref, wide_ref, ham_ref, rho_ref, out_ref,
):
    group, here = spot_ref[0], spot_ref[1]
    windows, share = rho_ref.shape[:2]
    width = ham_ref.shape[0]
    modes = wide_ref.shape[0] - 1
    blocks = width // share

    def add(r, w, value, fresh):
        for b in range(blocks):
            part = value[b * share:(b + 1) * share]
            index = lax.rem(b - group + blocks, blocks)
            if fresh:
                out_ref[index, r, w] = part
            else:
                out_ref[index, r, w] += part

    def lot(r, column, base):
        entries = [list_ref[r, base + n, column] for n in range(LOT)]
        maps = [lax.shift_right_logical(e, 9) for e in entries]
        tiles = [flat_ref[e & 511] for e in entries]
        rows = [
            wide_ref[maps[n], :width, :] + wide_ref[maps[n + 1], width:, :] for n in range(0, LOT, 2)
        ]
        left = jnp.dot(
            jnp.concatenate(rows, axis=1), jnp.concatenate(tiles, axis=0), preferred_element_type=F32
        )
        right = jnp.dot(
            jnp.concatenate(tiles, axis=1),
            jnp.concatenate([wide_ref[m] for m in maps], axis=0),
            preferred_element_type=F32,
        )
        return rotate(left - right)

    together = 4

    def step(index, carry):
        r = index // (windows // together)
        first = lax.rem(index, windows // together) * together
        for j in range(together):
            w = first + j
            add(r, w, lot(r, here * windows + w, 0), True)
        for j in range(together):
            w = first + j
            column = here * windows + w
            for base in range(LOT, modes, LOT):

                @pl.when(lax.shift_right_logical(list_ref[r, base, column], 9) < modes)
                def _():
                    add(r, w, lot(r, column, base), False)

            def lower(n, inner):
                entry = list_ref[r, modes + n, column]
                mode = lax.shift_right_logical(entry, 9)
                state = flat_ref[entry & 511]
                wide = wide_ref[mode]
                ahead = jnp.dot(wide[:width, :width], state, preferred_element_type=F32)
                after = jnp.dot(state, wide, preferred_element_type=F32)
                add(r, w, re_ref[mode] * rotate(ahead - after) + im_ref[mode] * (ahead + after), False)
                return inner

            lax.fori_loop(0, list_ref[r, modes + CAP, column], lower, 0)
        return carry

    lax.fori_loop(0, RINGS * (windows // together), step, 0)
    for w in range(windows):
        add(here, w, rotate(jnp.dot(ham_ref[...], rho_ref[w], preferred_element_type=F32)), False)


def use_lists(core, place, group, modes, modes_tri, use_up, use_down):
    windows = use_up.shape[0]

    def locate(places):
        owner = places // CAP
        z, y, c = owner // 16, (owner // 2) % RINGS, owner % 2
        collector = jnp.where(core == 0, y, z)
        source = jnp.where(core == 0, z, y)
        kind = jnp.where(c == core, 0, 1)
        row = ((source * 2 + kind) * CAP + places % CAP) * RINGS + place
        return collector, row

    def packed(collector, live, values, empty):
        count = values.shape[0]
        every = jnp.arange(RINGS, dtype=jnp.int32)[None, :, None]
        mask = ((collector[:, None, :] == every) & live[:, None, :]).reshape(count, RINGS * windows)
        spread = jnp.broadcast_to(values[:, None, :] - empty, (count, RINGS, windows)).reshape(count, -1)
        order = jnp.arange(count, dtype=jnp.int32)
        ranks = jnp.sum(
            jnp.where((order[:, None] > order[None, :])[:, :, None] & mask[None], 1, 0), axis=1
        )
        take = (order[:, None, None] == ranks[None]) & mask[None]
        return empty + jnp.sum(jnp.where(take, spread[None], 0), axis=1), jnp.sum(mask.astype(jnp.int32), axis=0)

    mode_ids = jnp.arange(modes, dtype=jnp.int32)[:, None]
    collector, row = locate(use_up.T)
    up, _ = packed(collector, jnp.ones(collector.shape, bool), mode_ids * 512 + row, modes * 512)
    collector, row = locate(use_down.T)
    local = modes_tri.T - group * modes
    live = (local >= 0) & (local < modes)
    down, count = packed(collector, live, local * 512 + row, 0)
    blank = jnp.zeros((ROWS - up.shape[0] - down.shape[0] - 1, up.shape[1]), jnp.int32)
    return jnp.concatenate([up, down, count[None], blank], axis=0)


def on_device(
    states, send_slot, window_tier_states, modes_tri, use_up, use_down,
    hamiltonian, coupling, coup_re, coup_im, decay_rate,
):
    width = hamiltonian.shape[0]
    windows, share = window_tier_states.shape[:2]
    modes = coupling.shape[0]
    group = lax.axis_index("grp")
    index = lax.axis_index("ado")
    core = index % 2
    place = jnp.where(core == 0, (index // 2) % RINGS, index // 16)

    slots = jnp.transpose(send_slot[0, 0]).reshape(-1)
    sib_store = lax.ppermute(states[0, 0], "ado", SIBLING)
    sib_slots = lax.ppermute(slots, "ado", SIBLING)
    lists = use_lists(core, place, group, modes, modes_tri, use_up, use_down)
    lists = lax.all_gather(lists, "ado", axis_index_groups=DELIVER, axis=0, tiled=False)
    picked = pick(jnp.reshape(core, (1,)).astype(jnp.int32), slots, sib_slots, states[0, 0], sib_store)
    received = lax.all_to_all(
        picked, "ado", split_axis=0, concat_axis=0, tiled=True, axis_index_groups=COLLECT
    )
    flat = received.reshape(-1, width, 2 * width)

    maps_wide = jnp.concatenate([doubled(coupling), jnp.zeros((1, 2 * width, 2 * width), BF16)], axis=0)
    ham_wide = doubled(hamiltonian)
    head_cols = lax.dynamic_slice_in_dim(hamiltonian, group * share, share, 1)
    right_part = jnp.einsum("wab,bc->wac", window_tier_states, ham_wide, preferred_element_type=F32)
    every_mode = jnp.arange(decay_rate.shape[0], dtype=jnp.int32)
    hits = modes_tri[:, :, None] == every_mode
    damping = jnp.sum(jnp.where(hits, decay_rate, 0.0), axis=(1, 2))
    own = rotate(right_part) + damping[:, None, None] * window_tier_states.astype(F32)

    count = width // share
    parts = pl.pallas_call(
        terms_kernel,
        in_specs=[SMEM] * 4 + [VMEM] * 4,
        out_specs=VMEM,
        out_shape=jax.ShapeDtypeStruct((count, RINGS, windows, share, 2 * width), F32),
        compiler_params=pltpu.CompilerParams(vmem_limit_bytes=32 * 2**20),
        cost_estimate=pl.CostEstimate(flops=2 * 10**9, bytes_accessed=10 * 2**20, transcendentals=0),
    )(
        jnp.stack([group, place]).astype(jnp.int32), lists, coup_re, coup_im,
        flat, maps_wide, head_cols, window_tier_states,
    )
    total = parts[0]
    for shift in (2, 1, 3):
        ring = [(i, (i + shift) % count) for i in range(count)]
        total = total + lax.ppermute(parts[shift].astype(LINK), "grp", ring).astype(F32)
    summed = lax.all_to_all(
        total.astype(LINK), "ado", split_axis=0, concat_axis=0, tiled=True, axis_index_groups=DELIVER
    )
    return STEP_WEIGHT * (jnp.sum(summed.astype(F32), axis=0) - own)


def solution(mesh):
    in_specs = (
        P("grp", "ado", None, None, None),
        P("grp", "ado", None, None),
        P("ado", "grp", None),
        P("ado", None),
        P("ado", "grp"),
        P("ado", None),
        P(),
        P("grp", None, None),
        P("grp"),
        P("grp"),
        P(),
    )
    out_specs = P("ado", "grp", None)
    return jax.shard_map(
        on_device, mesh=mesh, in_specs=in_specs, out_specs=out_specs, check_vma=False
    )
```

```python
import functools

import jax
import jax.numpy as jnp
from jax import lax
from jax.experimental import pallas as pl
from jax.experimental.pallas import tpu as pltpu
from jax.sharding import PartitionSpec as P

STEP_WEIGHT = 0.5
F32 = jnp.float32
BF16 = jnp.bfloat16
LINK = jnp.float16
VMEM = pl.BlockSpec(memory_space=pltpu.VMEM)
SMEM = pl.BlockSpec(memory_space=pltpu.SMEM)


def doubled(matrices):
    empty = jnp.zeros_like(matrices)
    upper_half = jnp.concatenate([matrices, empty], axis=-1)
    lower_half = jnp.concatenate([empty, matrices], axis=-1)
    return jnp.concatenate([upper_half, lower_half], axis=-2)


def rotate(parts):
    width = parts.shape[-1] // 2
    return jnp.concatenate([parts[..., width:], -parts[..., :width]], axis=-1)

RINGS = 8
CAP = 3
LOT = 4
SPAN = 2 * CAP * RINGS
FAR = ((4, 0), (3, -1), (-3, 1))
NEAR = ((0, 0), (1, 1), (2, 2), (-1, -1), (-2, -2))
SIBLING = [(i, i ^ 1) for i in range(2 * RINGS * RINGS)]


def device(core, along, across):
    along, across = along % RINGS, across % RINGS
    return along * 16 + across * 2 if core == 0 else across * 16 + along * 2 + 1


def onward(step):
    return [
        (device(c, a, b), device(c, a + step, b)) for c in range(2) for a in range(RINGS) for b in range(RINGS)
    ]


DELIVER = [[device(c, a, b) for b in range(RINGS)] for c in range(2) for a in range(RINGS)]
LISTENERS = [
    [device(c, a + far, b) for far in (0, 4) for b in range(RINGS)] for c in range(2) for a in range(RINGS // 2)
]


def pick_kernel(spot_ref, own_slot, sib_slot, own_ref, sib_ref, *out_refs):
    core, along = spot_ref[0], spot_ref[1]
    far = jnp.where(core == 0, 16, 2)
    near = jnp.where(core == 0, 2, 16)
    count = own_slot.shape[0] // CAP
    for (ahead, _), out_ref in zip(FAR + NEAR, out_refs, strict=True):
        first = lax.rem(along + ahead + RINGS, RINGS) * far + core
        for kind, (slots, store) in enumerate(((own_slot, own_ref), (sib_slot, sib_ref))):
            for c in range(CAP):
                for r in range(RINGS):
                    slot = slots[c * count + first + r * near]
                    out_ref[kind * CAP * RINGS + c * RINGS + r] = store[jnp.maximum(slot, 0)]


def pick(spot, own_slots, sib_slots, own, sib):
    shape = jax.ShapeDtypeStruct((SPAN,) + own.shape[1:], own.dtype)
    return pl.pallas_call(
        pick_kernel,
        in_specs=[SMEM, SMEM, SMEM, VMEM, VMEM],
        out_specs=[VMEM] * len(FAR + NEAR),
        out_shape=[shape] * len(FAR + NEAR),
        compiler_params=pltpu.CompilerParams(vmem_limit_bytes=24 * 2**20),
        cost_estimate=pl.CostEstimate(flops=0, bytes_accessed=10 * 2**20, transcendentals=0),
    )(spot, own_slots, sib_slots, own, sib)


def terms_kernel(sources, modes, windows, spot_ref, list_ref, re_ref, im_ref, *refs):
    flat_refs = refs[:sources]
    wide_ref, ham_ref, rho_ref, out_ref, flat, acc = refs[sources:]
    group, here = spot_ref[0], spot_ref[1]
    share = rho_ref.shape[1]
    width = ham_ref.shape[0]
    pairs = RINGS * windows
    blocks = width // share
    downs, extra, counts = modes, modes + CAP, modes + CAP + modes // LOT + CAP

    def gather(row, carry):
        for n, ref in enumerate(flat_refs):
            flat[n * SPAN + row] = ref[row]
        return carry

    lax.fori_loop(0, SPAN, gather, 0, unroll=8)

    def lot(pair, base):
        entries = [list_ref[base + n, pair] for n in range(LOT)]
        maps = [lax.shift_right_logical(e, 9) for e in entries]
        tiles = [flat[e & 511] for e in entries]
        rows = [
            wide_ref[maps[n], :width, :] + wide_ref[maps[n + 1], width:, :] for n in range(0, LOT, 2)
        ]
        left = jnp.dot(
            jnp.concatenate(rows, axis=1), jnp.concatenate(tiles, axis=0), preferred_element_type=F32
        )
        right = jnp.dot(
            jnp.concatenate(tiles, axis=1),
            jnp.concatenate([wide_ref[m] for m in maps], axis=0),
            preferred_element_type=F32,
        )
        return rotate(left - right)

    together = 8

    def first(index, carry):
        for j in range(together):
            pair = index * together + j
            acc[pair] = lot(pair, 0)
        return carry

    lax.fori_loop(0, pairs // together, first, 0)

    def listed(level, work):
        def some(index, carry):
            found = [list_ref[extra + level, index * 4 + j] for j in range(4)]
            values = [work(jnp.minimum(pair, pairs - 1)) for pair in found]
            for pair, value in zip(found, values, strict=True):
                acc[pair] += value
            return carry

        lax.fori_loop(0, lax.shift_right_logical(list_ref[counts, level] + 3, 2), some, 0)

    def more(level, carry):
        listed(level, lambda pair: lot(pair, level * LOT))
        return carry

    lax.fori_loop(1, modes // LOT, more, 0)

    def lower(t, carry):
        def work(pair):
            entry = list_ref[downs + t, pair]
            mode = lax.shift_right_logical(entry, 9)
            state = flat[entry & 511]
            wide = wide_ref[mode]
            ahead = jnp.dot(wide[:width, :width], state, preferred_element_type=F32)
            after = jnp.dot(state, wide, preferred_element_type=F32)
            return re_ref[mode] * rotate(ahead - after) + im_ref[mode] * (ahead + after)

        listed(modes // LOT + t, work)
        return carry

    lax.fori_loop(0, CAP, lower, 0)

    if sources == len(NEAR):

        def local(w, carry):
            acc[here * windows + w] += rotate(
                jnp.dot(ham_ref[...], rho_ref[w], preferred_element_type=F32)
            )
            return carry

        lax.fori_loop(0, windows, local, 0)

    def leave(r, carry):
        for w in range(windows):
            value = acc[r * windows + w]
            for b in range(blocks):
                out_ref[lax.rem(b - group + blocks, blocks), r, w] = value[b * share:(b + 1) * share]
        return carry

    lax.fori_loop(0, RINGS, leave, 0)


def terms(spot, lists, coup_re, coup_im, pieces, maps_wide, head_cols, rho):
    modes = maps_wide.shape[0] - 1
    windows, share, lanes = rho.shape
    width = head_cols.shape[0]
    return pl.pallas_call(
        functools.partial(terms_kernel, len(pieces), modes, windows),
        in_specs=[SMEM] * 4 + [VMEM] * (len(pieces) + 3),
        out_specs=VMEM,
        out_shape=jax.ShapeDtypeStruct((width // share, RINGS, windows, share, lanes), F32),
        scratch_shapes=[
            pltpu.VMEM((len(pieces) * SPAN, width, lanes), BF16),
            pltpu.VMEM((RINGS * windows + 1, width, lanes), F32),
        ],
        compiler_params=pltpu.CompilerParams(vmem_limit_bytes=28 * 2**20),
        cost_estimate=pl.CostEstimate(flops=10**9, bytes_accessed=10 * 2**20, transcendentals=0),
    )(spot, lists, coup_re, coup_im, *pieces, maps_wide, head_cols, rho)


def use_lists(steps, target, core, along, across, group, modes, heard):
    half = (along // 4 + target // 4) % 2
    heard = lax.dynamic_index_in_dim(heard.reshape((2, RINGS) + heard.shape[1:]), half, 0, keepdims=False)
    windows = heard.shape[-1]
    pairs = RINGS * windows
    heard = jnp.transpose(heard, (1, 0, 2)).reshape(-1, pairs)
    receiver = jnp.arange(pairs, dtype=jnp.int32) // windows

    def locate(places):
        owner = places // CAP
        z, y, c = owner // 16, (owner // 2) % RINGS, owner % 2
        off = (jnp.where(core == 0, z, y) - along) % RINGS
        source = jnp.full_like(off, -1)
        for n, (_, step) in enumerate(steps):
            source = jnp.where(off == -step % RINGS, n, source)
        mine = (jnp.where(core == 0, y, z) == across) & (source >= 0)
        kind = jnp.where(c == core, 0, 1)
        return mine, ((source * 2 + kind) * CAP + places % CAP) * RINGS + receiver

    mine, row = locate(heard[:modes])
    ids = jnp.arange(modes, dtype=jnp.int32)
    below = (ids[:, None] > ids[None, :]).astype(F32)
    rank = jnp.dot(below, mine.astype(F32), preferred_element_type=F32).astype(jnp.int32)
    count = jnp.sum(mine.astype(jnp.int32), axis=0)
    value = ids[:, None] * 512 + row - modes * 512
    hit = mine[None] & (rank[None] == ids[:, None, None])
    up = modes * 512 + jnp.sum(jnp.where(hit, value[None], 0), axis=1)

    mine, row = locate(heard[modes:modes + CAP])
    local = heard[modes + CAP:modes + 2 * CAP] - group * modes
    live = mine & (local >= 0) & (local < modes)
    down = jnp.where(live, local * 512 + row, 0)

    levels = jnp.arange(modes // LOT, dtype=jnp.int32) * LOT
    flags = jnp.concatenate([count[None, :] > levels[:, None], live], axis=0)
    lanes = jnp.arange(pairs, dtype=jnp.int32)
    ahead = (lanes[:, None] < lanes[None, :]).astype(F32)
    order = jnp.dot(flags.astype(F32), ahead, preferred_element_type=F32).astype(jnp.int32)
    hit = flags[:, None, :] & (order[:, None, :] == lanes[None, :, None])
    listed = pairs + jnp.sum(jnp.where(hit, lanes - pairs, 0), axis=2)
    totals = jnp.sum(flags.astype(jnp.int32), axis=1)
    totals = jnp.pad(totals, (0, pairs - totals.shape[0]))[None]
    return jnp.concatenate([up, down, listed, totals], axis=0)


def over_groups(parts):
    count = parts.shape[0]
    total = parts[0]
    for shift in (2, 1, 3):
        ring = [(i, (i + shift) % count) for i in range(count)]
        total = total + lax.ppermute(parts[shift].astype(LINK), "grp", ring).astype(F32)
    return total


def on_device(
    states, send_slot, window_tier_states, modes_tri, use_up, use_down,
    hamiltonian, coupling, coup_re, coup_im, decay_rate,
):
    width = hamiltonian.shape[0]
    share = window_tier_states.shape[1]
    modes = coupling.shape[0]
    group = lax.axis_index("grp").astype(jnp.int32)
    index = lax.axis_index("ado").astype(jnp.int32)
    core, z, y = index & 1, index >> 4, (index >> 1) & 7
    along = jnp.where(core == 0, z, y)
    across = jnp.where(core == 0, y, z)

    slots = jnp.transpose(send_slot[0, 0]).reshape(-1)
    sib_store = lax.ppermute(states[0, 0], "ado", SIBLING)
    sib_slots = lax.ppermute(slots, "ado", SIBLING)
    said = jnp.concatenate([use_up.T, use_down.T, modes_tri.T], axis=0)
    heard = lax.all_gather(said, "ado", axis_index_groups=LISTENERS, axis=0, tiled=False)
    slots, heard = lax.optimization_barrier((slots, heard))
    picked = pick(jnp.stack([core, along]), slots, sib_slots, states[0, 0], sib_store)

    def send(steps, blocks):
        return [
            block if step == 0 else lax.ppermute(block, "ado", onward(step))
            for (_, step), block in zip(steps, blocks, strict=True)
        ]

    far_states = send(FAR, picked[:len(FAR)])
    near_states = send(NEAR, picked[len(FAR):])
    where = (core, along, across, group, modes, heard)
    far_lists = use_lists(FAR, 4, *where)
    near_lists = use_lists(NEAR, 0, *where)

    maps_wide = jnp.concatenate([doubled(coupling), jnp.zeros((1, 2 * width, 2 * width), BF16)], axis=0)
    head_cols = lax.dynamic_slice_in_dim(hamiltonian, group * share, share, 1)
    spot = jnp.stack([group, across])
    shared = (maps_wide, head_cols, window_tier_states)
    far = over_groups(terms(spot, far_lists, coup_re, coup_im, far_states, *shared))
    far = lax.ppermute(far.astype(LINK), "ado", onward(4))
    near = over_groups(terms(spot, near_lists, coup_re, coup_im, near_states, *shared))
    summed = lax.all_to_all(
        (near + far.astype(F32)).astype(LINK), "ado", split_axis=0, concat_axis=0, tiled=True,
        axis_index_groups=DELIVER,
    )

    ham_wide = doubled(hamiltonian)
    right_part = jnp.einsum("wab,bc->wac", window_tier_states, ham_wide, preferred_element_type=F32)
    every_mode = jnp.arange(decay_rate.shape[0], dtype=jnp.int32)
    hits = modes_tri[:, :, None] == every_mode
    damping = jnp.sum(jnp.where(hits, decay_rate, 0.0), axis=(1, 2))
    own = rotate(right_part) + damping[:, None, None] * window_tier_states.astype(F32)
    return STEP_WEIGHT * (jnp.sum(summed.astype(F32), axis=0) - own)


def solution(mesh):
    in_specs = (
        P("grp", "ado", None, None, None),
        P("grp", "ado", None, None),
        P("ado", "grp", None),
        P("ado", None),
        P("ado", "grp"),
        P("ado", None),
        P(),
        P("grp", None, None),
        P("grp"),
        P("grp"),
        P(),
    )
    out_specs = P("ado", "grp", None)
    return jax.shard_map(
        on_device, mesh=mesh, in_specs=in_specs, out_specs=out_specs, check_vma=False
    )
```

```python
import functools

import jax
import jax.numpy as jnp
from jax import lax
from jax.experimental import pallas as pl
from jax.experimental.pallas import tpu as pltpu
from jax.sharding import PartitionSpec as P

STEP_WEIGHT = 0.5
F32 = jnp.float32
BF16 = jnp.bfloat16
LINK = jnp.float16
VMEM = pl.BlockSpec(memory_space=pltpu.VMEM)
SMEM = pl.BlockSpec(memory_space=pltpu.SMEM)


def doubled(matrices):
    empty = jnp.zeros_like(matrices)
    upper_half = jnp.concatenate([matrices, empty], axis=-1)
    lower_half = jnp.concatenate([empty, matrices], axis=-1)
    return jnp.concatenate([upper_half, lower_half], axis=-2)


def rotate(parts):
    width = parts.shape[-1] // 2
    return jnp.concatenate([parts[..., width:], -parts[..., :width]], axis=-1)

RINGS = 8
CAP = 3
LOT = 4
SPAN = 2 * CAP * RINGS
FAR = ((4, 0), (3, -1), (-3, 1))
NEAR = ((0, 0), (1, 1), (2, 2), (-1, -1), (-2, -2))
SIBLING = [(i, i ^ 1) for i in range(2 * RINGS * RINGS)]


def device(core, along, across):
    along, across = along % RINGS, across % RINGS
    return along * 16 + across * 2 if core == 0 else across * 16 + along * 2 + 1


def onward(step):
    return [
        (device(c, a, b), device(c, a + step, b)) for c in range(2) for a in range(RINGS) for b in range(RINGS)
    ]


DELIVER = [[device(c, a, b) for b in range(RINGS)] for c in range(2) for a in range(RINGS)]
LISTENERS = [
    [device(c, a + far, b) for far in (0, 4) for b in range(RINGS)] for c in range(2) for a in range(RINGS // 2)
]


def pick_kernel(spot_ref, own_slot, sib_slot, own_ref, sib_ref, *out_refs):
    core, along = spot_ref[0], spot_ref[1]
    far = jnp.where(core == 0, 16, 2)
    near = jnp.where(core == 0, 2, 16)
    count = own_slot.shape[0] // CAP
    for (ahead, _), out_ref in zip(FAR + NEAR, out_refs, strict=True):
        first = lax.rem(along + ahead + RINGS, RINGS) * far + core
        for kind, (slots, store) in enumerate(((own_slot, own_ref), (sib_slot, sib_ref))):
            for c in range(CAP):
                for r in range(RINGS):
                    slot = slots[c * count + first + r * near]
                    out_ref[kind * CAP * RINGS + c * RINGS + r] = store[jnp.maximum(slot, 0)]


def pick(spot, own_slots, sib_slots, own, sib):
    shape = jax.ShapeDtypeStruct((SPAN,) + own.shape[1:], own.dtype)
    return pl.pallas_call(
        pick_kernel,
        in_specs=[SMEM, SMEM, SMEM, VMEM, VMEM],
        out_specs=[VMEM] * len(FAR + NEAR),
        out_shape=[shape] * len(FAR + NEAR),
        compiler_params=pltpu.CompilerParams(vmem_limit_bytes=24 * 2**20),
        cost_estimate=pl.CostEstimate(flops=0, bytes_accessed=10 * 2**20, transcendentals=0),
    )(spot, own_slots, sib_slots, own, sib)


def terms_kernel(sources, modes, windows, spot_ref, list_ref, re_ref, im_ref, *refs):
    flat_refs = refs[:sources]
    wide_ref, ham_ref, rho_ref, out_ref, flat, acc = refs[sources:]
    group, here = spot_ref[0], spot_ref[1]
    share = rho_ref.shape[1]
    width = ham_ref.shape[0]
    pairs = RINGS * windows
    blocks = width // share
    downs, extra, counts = modes, modes + CAP, modes + CAP + modes // LOT + CAP

    def gather(row, carry):
        for n, ref in enumerate(flat_refs):
            flat[n * SPAN + row] = ref[row]
        return carry

    lax.fori_loop(0, SPAN, gather, 0, unroll=8)

    def lot(pair, base):
        entries = [list_ref[base + n, pair] for n in range(LOT)]
        maps = [lax.shift_right_logical(e, 9) for e in entries]
        tiles = [flat[e & 511] for e in entries]
        rows = [
            wide_ref[maps[n], :width, :] + wide_ref[maps[n + 1], width:, :] for n in range(0, LOT, 2)
        ]
        left = jnp.dot(
            jnp.concatenate(rows, axis=1), jnp.concatenate(tiles, axis=0), preferred_element_type=F32
        )
        right = jnp.dot(
            jnp.concatenate(tiles, axis=1),
            jnp.concatenate([wide_ref[m] for m in maps], axis=0),
            preferred_element_type=F32,
        )
        return rotate(left - right)

    together = 8

    def first(index, carry):
        for j in range(together):
            pair = index * together + j
            acc[pair] = lot(pair, 0)
        return carry

    lax.fori_loop(0, pairs // together, first, 0)

    def listed(level, work):
        def some(index, carry):
            found = [list_ref[extra + level, index * 4 + j] for j in range(4)]
            values = [work(jnp.minimum(pair, pairs - 1)) for pair in found]
            for pair, value in zip(found, values, strict=True):
                acc[pair] += value
            return carry

        lax.fori_loop(0, lax.shift_right_logical(list_ref[counts, level] + 3, 2), some, 0)

    def more(level, carry):
        listed(level, lambda pair: lot(pair, level * LOT))
        return carry

    lax.fori_loop(1, modes // LOT, more, 0)

    def lower(t, carry):
        def work(pair):
            entry = list_ref[downs + t, pair]
            mode = lax.shift_right_logical(entry, 9)
            state = flat[entry & 511]
            wide = wide_ref[mode]
            ahead = jnp.dot(wide[:width, :width], state, preferred_element_type=F32)
            after = jnp.dot(state, wide, preferred_element_type=F32)
            return re_ref[mode] * rotate(ahead - after) + im_ref[mode] * (ahead + after)

        listed(modes // LOT + t, work)
        return carry

    lax.fori_loop(0, CAP, lower, 0)

    if sources == len(NEAR):

        def local(w, carry):
            acc[here * windows + w] += rotate(
                jnp.dot(ham_ref[...], rho_ref[w], preferred_element_type=F32)
            )
            return carry

        lax.fori_loop(0, windows, local, 0)

    def leave(r, carry):
        for w in range(windows):
            value = acc[r * windows + w]
            for b in range(blocks):
                out_ref[lax.rem(b - group + blocks, blocks), r, w] = value[b * share:(b + 1) * share]
        return carry

    lax.fori_loop(0, RINGS, leave, 0)


def terms(spot, lists, coup_re, coup_im, pieces, maps_wide, head_cols, rho):
    modes = maps_wide.shape[0] - 1
    windows, share, lanes = rho.shape
    width = head_cols.shape[0]
    return pl.pallas_call(
        functools.partial(terms_kernel, len(pieces), modes, windows),
        in_specs=[SMEM] * 4 + [VMEM] * (len(pieces) + 3),
        out_specs=VMEM,
        out_shape=jax.ShapeDtypeStruct((width // share, RINGS, windows, share, lanes), F32),
        scratch_shapes=[
            pltpu.VMEM((len(pieces) * SPAN, width, lanes), BF16),
            pltpu.VMEM((RINGS * windows + 1, width, lanes), F32),
        ],
        compiler_params=pltpu.CompilerParams(vmem_limit_bytes=28 * 2**20),
        cost_estimate=pl.CostEstimate(flops=10**9, bytes_accessed=10 * 2**20, transcendentals=0),
    )(spot, lists, coup_re, coup_im, *pieces, maps_wide, head_cols, rho)


def use_lists(steps, target, core, along, across, group, modes, heard):
    half = (along // 4 + target // 4) % 2
    heard = lax.dynamic_index_in_dim(heard.reshape((2, RINGS) + heard.shape[1:]), half, 0, keepdims=False)
    windows = heard.shape[-1]
    pairs = RINGS * windows
    heard = jnp.transpose(heard, (1, 0, 2)).reshape(-1, pairs)
    receiver = jnp.arange(pairs, dtype=jnp.int32) // windows

    def locate(places):
        owner = places // CAP
        z, y, c = owner // 16, (owner // 2) % RINGS, owner % 2
        off = (jnp.where(core == 0, z, y) - along) % RINGS
        source = jnp.full_like(off, -1)
        for n, (_, step) in enumerate(steps):
            source = jnp.where(off == -step % RINGS, n, source)
        mine = (jnp.where(core == 0, y, z) == across) & (source >= 0)
        kind = jnp.where(c == core, 0, 1)
        return mine, ((source * 2 + kind) * CAP + places % CAP) * RINGS + receiver

    mine, row = locate(heard[:modes])
    ids = jnp.arange(modes, dtype=jnp.int32)
    below = (ids[:, None] > ids[None, :]).astype(F32)
    rank = jnp.dot(below, mine.astype(F32), preferred_element_type=F32).astype(jnp.int32)
    count = jnp.sum(mine.astype(jnp.int32), axis=0)
    value = ids[:, None] * 512 + row - modes * 512
    hit = mine[None] & (rank[None] == ids[:, None, None])
    up = modes * 512 + jnp.sum(jnp.where(hit, value[None], 0), axis=1)

    mine, row = locate(heard[modes:modes + CAP])
    local = heard[modes + CAP:modes + 2 * CAP] - group * modes
    live = mine & (local >= 0) & (local < modes)
    down = jnp.where(live, local * 512 + row, 0)

    levels = jnp.arange(modes // LOT, dtype=jnp.int32) * LOT
    flags = jnp.concatenate([count[None, :] > levels[:, None], live], axis=0)
    lanes = jnp.arange(pairs, dtype=jnp.int32)
    ahead = (lanes[:, None] < lanes[None, :]).astype(F32)
    order = jnp.dot(flags.astype(F32), ahead, preferred_element_type=F32).astype(jnp.int32)
    hit = flags[:, None, :] & (order[:, None, :] == lanes[None, :, None])
    listed = pairs + jnp.sum(jnp.where(hit, lanes - pairs, 0), axis=2)
    totals = jnp.sum(flags.astype(jnp.int32), axis=1)
    totals = jnp.pad(totals, (0, pairs - totals.shape[0]))[None]
    return jnp.concatenate([up, down, listed, totals], axis=0)


def over_groups(parts):
    count = parts.shape[0]
    total = parts[0]
    for shift in (2, 1, 3):
        ring = [(i, (i + shift) % count) for i in range(count)]
        total = total + lax.ppermute(parts[shift].astype(LINK), "grp", ring).astype(F32)
    return total


def on_device(
    states, send_slot, window_tier_states, modes_tri, use_up, use_down,
    hamiltonian, coupling, coup_re, coup_im, decay_rate,
):
    width = hamiltonian.shape[0]
    share = window_tier_states.shape[1]
    modes = coupling.shape[0]
    group = lax.axis_index("grp").astype(jnp.int32)
    index = lax.axis_index("ado").astype(jnp.int32)
    core, z, y = index & 1, index >> 4, (index >> 1) & 7
    along = jnp.where(core == 0, z, y)
    across = jnp.where(core == 0, y, z)

    slots = jnp.transpose(send_slot[0, 0]).reshape(-1)
    sib_store = lax.ppermute(states[0, 0], "ado", SIBLING)
    sib_slots = lax.ppermute(slots, "ado", SIBLING)
    said = jnp.concatenate([use_up.T, use_down.T, modes_tri.T], axis=0)
    said = jnp.broadcast_to(said, (2 * RINGS,) + said.shape)
    heard = lax.all_to_all(
        said, "ado", split_axis=0, concat_axis=0, tiled=True, axis_index_groups=LISTENERS
    )
    picked = pick(jnp.stack([core, along]), slots, sib_slots, states[0, 0], sib_store)

    def send(steps, blocks):
        return [
            block if step == 0 else lax.ppermute(block, "ado", onward(step))
            for (_, step), block in zip(steps, blocks, strict=True)
        ]

    far_states = send(FAR, picked[:len(FAR)])
    near_states = send(NEAR, picked[len(FAR):])
    where = (core, along, across, group, modes, heard)
    far_lists = use_lists(FAR, 4, *where)
    near_lists = use_lists(NEAR, 0, *where)

    maps_wide = jnp.concatenate([doubled(coupling), jnp.zeros((1, 2 * width, 2 * width), BF16)], axis=0)
    head_cols = lax.dynamic_slice_in_dim(hamiltonian, group * share, share, 1)
    spot = jnp.stack([group, across])
    shared = (maps_wide, head_cols, window_tier_states)
    far = over_groups(terms(spot, far_lists, coup_re, coup_im, far_states, *shared))
    far = lax.ppermute(far.astype(LINK), "ado", onward(4))
    near = over_groups(terms(spot, near_lists, coup_re, coup_im, near_states, *shared))
    summed = lax.all_to_all(
        (near + far.astype(F32)).astype(LINK), "ado", split_axis=0, concat_axis=0, tiled=True,
        axis_index_groups=DELIVER,
    )

    ham_wide = doubled(hamiltonian)
    right_part = jnp.einsum("wab,bc->wac", window_tier_states, ham_wide, preferred_element_type=F32)
    every_mode = jnp.arange(decay_rate.shape[0], dtype=jnp.int32)
    hits = modes_tri[:, :, None] == every_mode
    damping = jnp.sum(jnp.where(hits, decay_rate, 0.0), axis=(1, 2))
    own = rotate(right_part) + damping[:, None, None] * window_tier_states.astype(F32)
    return STEP_WEIGHT * (jnp.sum(summed.astype(F32), axis=0) - own)


def solution(mesh):
    in_specs = (
        P("grp", "ado", None, None, None),
        P("grp", "ado", None, None),
        P("ado", "grp", None),
        P("ado", None),
        P("ado", "grp"),
        P("ado", None),
        P(),
        P("grp", None, None),
        P("grp"),
        P("grp"),
        P(),
    )
    out_specs = P("ado", "grp", None)
    return jax.shard_map(
        on_device, mesh=mesh, in_specs=in_specs, out_specs=out_specs, check_vma=False
    )
```

```python
import functools

import jax
import jax.numpy as jnp
from jax import lax
from jax.experimental import pallas as pl
from jax.experimental.pallas import tpu as pltpu
from jax.sharding import PartitionSpec as P

STEP_WEIGHT = 0.5
F32 = jnp.float32
BF16 = jnp.bfloat16
LINK = jnp.float16
VMEM = pl.BlockSpec(memory_space=pltpu.VMEM)
SMEM = pl.BlockSpec(memory_space=pltpu.SMEM)


def doubled(matrices):
    empty = jnp.zeros_like(matrices)
    upper_half = jnp.concatenate([matrices, empty], axis=-1)
    lower_half = jnp.concatenate([empty, matrices], axis=-1)
    return jnp.concatenate([upper_half, lower_half], axis=-2)


def rotate(parts):
    width = parts.shape[-1] // 2
    return jnp.concatenate([parts[..., width:], -parts[..., :width]], axis=-1)

RINGS = 8
CAP = 3
LOT = 4
SPAN = 2 * CAP * RINGS
FAR = ((4, 0), (3, -1), (-3, 1))
NEAR = ((0, 0), (1, 1), (2, 2), (-1, -1), (-2, -2))
SIBLING = [(i, i ^ 1) for i in range(2 * RINGS * RINGS)]


def device(core, along, across):
    along, across = along % RINGS, across % RINGS
    return along * 16 + across * 2 if core == 0 else across * 16 + along * 2 + 1


def onward(step):
    return [
        (device(c, a, b), device(c, a + step, b)) for c in range(2) for a in range(RINGS) for b in range(RINGS)
    ]


DELIVER = [[device(c, a, b) for b in range(RINGS)] for c in range(2) for a in range(RINGS)]
def pick_kernel(spot_ref, own_slot, sib_slot, own_ref, sib_ref, *out_refs):
    core, along = spot_ref[0], spot_ref[1]
    far = jnp.where(core == 0, 16, 2)
    near = jnp.where(core == 0, 2, 16)
    count = own_slot.shape[0] // CAP
    for (ahead, _), out_ref in zip(FAR + NEAR, out_refs, strict=True):
        first = lax.rem(along + ahead + RINGS, RINGS) * far + core
        for kind, (slots, store) in enumerate(((own_slot, own_ref), (sib_slot, sib_ref))):
            for c in range(CAP):
                for r in range(RINGS):
                    slot = slots[c * count + first + r * near]
                    out_ref[kind * CAP * RINGS + c * RINGS + r] = store[jnp.maximum(slot, 0)]


def pick(spot, own_slots, sib_slots, own, sib):
    shape = jax.ShapeDtypeStruct((SPAN,) + own.shape[1:], own.dtype)
    return pl.pallas_call(
        pick_kernel,
        in_specs=[SMEM, SMEM, SMEM, VMEM, VMEM],
        out_specs=[VMEM] * len(FAR + NEAR),
        out_shape=[shape] * len(FAR + NEAR),
        compiler_params=pltpu.CompilerParams(vmem_limit_bytes=24 * 2**20),
        cost_estimate=pl.CostEstimate(flops=0, bytes_accessed=10 * 2**20, transcendentals=0),
    )(spot, own_slots, sib_slots, own, sib)


def terms_kernel(sources, modes, windows, part, spot_ref, list_ref, re_ref, im_ref, *refs):
    flat_refs = refs[:sources]
    wide_ref, ham_ref, rho_ref, out_ref, flat, acc = refs[sources:]
    here = spot_ref[2]
    share = rho_ref.shape[1]
    width = ham_ref.shape[0]
    pairs = RINGS * windows
    blocks = width // share
    begin, end, slot = part
    levels = modes // LOT + CAP
    downs, extra, counts = modes, modes + CAP + slot * levels, list_ref.shape[0] - 1

    def gather(row, carry):
        for n, ref in enumerate(flat_refs):
            flat[n * SPAN + row] = ref[row]
        return carry

    lax.fori_loop(0, SPAN, gather, 0, unroll=8)

    def lot(pair, base):
        entries = [list_ref[base + n, pair] for n in range(LOT)]
        maps = [lax.shift_right_logical(e, 9) for e in entries]
        tiles = [flat[e & 511] for e in entries]
        rows = [
            wide_ref[maps[n], :width, :] + wide_ref[maps[n + 1], width:, :] for n in range(0, LOT, 2)
        ]
        left = jnp.dot(
            jnp.concatenate(rows, axis=1), jnp.concatenate(tiles, axis=0), preferred_element_type=F32
        )
        right = jnp.dot(
            jnp.concatenate(tiles, axis=1),
            jnp.concatenate([wide_ref[m] for m in maps], axis=0),
            preferred_element_type=F32,
        )
        return rotate(left - right)

    together = 8

    def first(index, carry):
        for j in range(together):
            pair = index * together + j
            acc[pair] = lot(pair, 0)
        return carry

    lax.fori_loop(begin * windows // together, end * windows // together, first, 0)

    def listed(level, work):
        def some(index, carry):
            found = [list_ref[extra + level, index * 4 + j] for j in range(4)]
            values = [work(jnp.minimum(pair, pairs - 1)) for pair in found]
            for pair, value in zip(found, values, strict=True):
                acc[pair] += value
            return carry

        lax.fori_loop(0, lax.shift_right_logical(list_ref[counts, slot * levels + level] + 3, 2), some, 0)

    def more(level, carry):
        listed(level, lambda pair: lot(pair, level * LOT))
        return carry

    lax.fori_loop(1, modes // LOT, more, 0)

    def lower(t, carry):
        def work(pair):
            entry = list_ref[downs + t, pair]
            mode = lax.shift_right_logical(entry, 9)
            state = flat[entry & 511]
            wide = wide_ref[mode]
            ahead = jnp.dot(wide[:width, :width], state, preferred_element_type=F32)
            after = jnp.dot(state, wide, preferred_element_type=F32)
            return re_ref[mode] * rotate(ahead - after) + im_ref[mode] * (ahead + after)

        listed(modes // LOT + t, work)
        return carry

    lax.fori_loop(0, CAP, lower, 0)

    if sources == len(NEAR):

        def local(w, carry):
            acc[here * windows + w] += rotate(
                jnp.dot(ham_ref[...], rho_ref[w], preferred_element_type=F32)
            )
            return carry

        lax.fori_loop(0, jnp.where((here >= begin) & (here < end), windows, 0), local, 0)

    def leave(r, carry):
        for w in range(windows):
            value = acc[r * windows + w]
            for b in range(blocks):
                out_ref[b, r - begin, w] = value[b * share:(b + 1) * share]
        return carry

    lax.fori_loop(begin, end, leave, 0)


def terms(part, spot, lists, coup_re, coup_im, pieces, maps_wide, head_cols, rho):
    modes = maps_wide.shape[0] - 1
    windows, share, lanes = rho.shape
    width = head_cols.shape[0]
    return pl.pallas_call(
        functools.partial(terms_kernel, len(pieces), modes, windows, part),
        in_specs=[SMEM] * 4 + [VMEM] * (len(pieces) + 3),
        out_specs=VMEM,
        out_shape=jax.ShapeDtypeStruct((width // share, part[1] - part[0], windows, share, lanes), F32),
        scratch_shapes=[
            pltpu.VMEM((len(pieces) * SPAN, width, lanes), BF16),
            pltpu.VMEM((RINGS * windows + 1, width, lanes), F32),
        ],
        compiler_params=pltpu.CompilerParams(vmem_limit_bytes=28 * 2**20),
        cost_estimate=pl.CostEstimate(flops=10**9, bytes_accessed=10 * 2**20, transcendentals=0),
    )(spot, lists, coup_re, coup_im, *pieces, maps_wide, head_cols, rho)


def lists_kernel(steps, parts, modes, spot_ref, heard_ref, out_ref):
    core, along, across, group = spot_ref[0], spot_ref[1], spot_ref[2], spot_ref[3]
    pairs = heard_ref.shape[1]
    windows = pairs // RINGS

    def locate(places):
        owner = lax.shift_right_logical(places * 171, 9)
        z, y, c = lax.shift_right_logical(owner, 4), lax.shift_right_logical(owner, 1) & 7, owner & 1
        off = (jnp.where(core == 0, z, y) - along) & (RINGS - 1)
        source = jnp.full_like(off, -1)
        for n, (_, step) in enumerate(steps):
            source = jnp.where(off == -step % RINGS, n, source)
        mine = (jnp.where(core == 0, y, z) == across) & (source >= 0)
        kind = jnp.where(c == core, 0, 1)
        lanes = lax.broadcasted_iota(jnp.int32, places.shape, 1)
        receiver = lax.shift_right_logical(lanes, windows.bit_length() - 1)
        return mine, ((source * 2 + kind) * CAP + places - owner * CAP) * RINGS + receiver

    def square(n, axis):
        return lax.broadcasted_iota(jnp.int32, (n, n), axis)

    def ones(mask):
        return jnp.where(mask, 1.0, 0.0)

    mine, row = locate(heard_ref[:modes])
    ids = lax.broadcasted_iota(jnp.int32, mine.shape, 0)
    below = ones(square(modes, 0) > square(modes, 1))
    rank = jnp.dot(below, ones(mine), preferred_element_type=F32).astype(jnp.int32)
    rank = jnp.where(mine, rank, -1)
    count = jnp.sum(ones(mine), axis=0, keepdims=True)
    value = (ids * 512 + row - modes * 512).astype(F32)
    for n in range(modes):
        found = jnp.sum(jnp.where(rank == n, value, 0.0), axis=0, keepdims=True)
        out_ref[n:n + 1] = found.astype(jnp.int32) + modes * 512

    mine, row = locate(heard_ref[modes:modes + CAP])
    local = heard_ref[modes + CAP:modes + 2 * CAP] - group * modes
    live = mine & (local >= 0) & (local < modes)
    out_ref[modes:modes + CAP] = jnp.where(live, local * 512 + row, 0)

    first = lax.broadcasted_iota(jnp.int32, (1, pairs), 1)
    flags = []
    for begin, end in parts:
        inside = (first >= begin * windows) & (first < end * windows)
        for n in range(modes // LOT):
            flags.append(ones(inside & (count > n * LOT)))
        for t in range(CAP):
            flags.append(ones(inside & live[t:t + 1]))
    total = len(flags)
    flags = jnp.concatenate(flags + [jnp.zeros((pairs - total, pairs), F32)], axis=0)
    turned = (((1,), (1,)), ((), ()))
    down, over = square(pairs, 0), square(pairs, 1)
    chosen = lax.dot_general(ones(down == over), flags, turned, preferred_element_type=F32)
    order = lax.dot_general(ones(down > over), flags, turned, preferred_element_type=F32)
    order = jnp.where(chosen > 0.5, order, -1.0)
    numbers = (down - pairs).astype(F32)
    lanes = over.astype(F32)
    for n in range(total):
        found = jnp.sum(jnp.where(order[:, n:n + 1] == lanes, numbers, 0.0), axis=0, keepdims=True)
        out_ref[modes + CAP + n:modes + CAP + n + 1] = found.astype(jnp.int32) + pairs
    sums = lax.dot_general(jnp.ones((8, pairs), F32), flags, turned, preferred_element_type=F32)
    last = out_ref.shape[0] - 1
    out_ref[last:last + 1] = sums[:1].astype(jnp.int32)


def use_lists(steps, parts, modes, spot, heard):
    rows = modes + CAP + len(parts) * (modes // LOT + CAP) + 1
    return pl.pallas_call(
        functools.partial(lists_kernel, steps, parts, modes),
        in_specs=[SMEM, VMEM],
        out_specs=VMEM,
        out_shape=jax.ShapeDtypeStruct((rows + -rows % 8, heard.shape[1]), jnp.int32),
        compiler_params=pltpu.CompilerParams(vmem_limit_bytes=8 * 2**20),
        cost_estimate=pl.CostEstimate(flops=10**7, bytes_accessed=2**17, transcendentals=0),
    )(spot, heard)


def over_groups(parts):
    parts = lax.all_to_all(parts.astype(LINK), "grp", split_axis=0, concat_axis=0, tiled=True)
    return jnp.sum(parts.astype(F32), axis=0)


def on_device(
    states, send_slot, window_tier_states, modes_tri, use_up, use_down,
    hamiltonian, coupling, coup_re, coup_im, decay_rate,
):
    width = hamiltonian.shape[0]
    windows, share = window_tier_states.shape[:2]
    modes = coupling.shape[0]
    group = lax.axis_index("grp").astype(jnp.int32)
    index = lax.axis_index("ado").astype(jnp.int32)
    core, z, y = index & 1, index >> 4, (index >> 1) & 7
    along = jnp.where(core == 0, z, y)
    across = jnp.where(core == 0, y, z)

    spot = jnp.stack([core, along, across, group])

    slots = jnp.transpose(send_slot[0, 0]).reshape(-1)
    sib_store = lax.ppermute(states[0, 0], "ado", SIBLING)
    sib_slots = lax.ppermute(slots, "ado", SIBLING)
    said = jnp.concatenate([use_up.T, use_down.T, modes_tri.T, jnp.zeros_like(use_down.T)[:2]], axis=0)
    lane = jnp.arange(RINGS * windows, dtype=jnp.int32) // windows
    said = jnp.where(lane == across, jnp.tile(said, (1, RINGS)), 0)
    heard = lax.all_to_all(
        jnp.broadcast_to(said, (RINGS,) + said.shape), "ado", split_axis=0, concat_axis=0, tiled=True,
        axis_index_groups=DELIVER,
    )
    heard = jnp.sum(heard, axis=0)
    heard_far = lax.ppermute(heard, "ado", onward(4))
    picked = pick(spot, slots, sib_slots, states[0, 0], sib_store)
    heard, heard_far, picked = lax.optimization_barrier((heard, heard_far, picked))

    def send(steps, blocks):
        return [
            block if step == 0 else lax.ppermute(block, "ado", onward(step))
            for (_, step), block in zip(steps, blocks, strict=True)
        ]

    far_states = send(FAR, picked[:len(FAR)])
    near_states = send(NEAR, picked[len(FAR):])
    half = RINGS // 2
    far_lists = use_lists(FAR, ((0, RINGS),), modes, spot, heard_far)
    near_lists = use_lists(NEAR, ((0, half), (half, RINGS)), modes, spot, heard)

    maps_wide = jnp.concatenate([doubled(coupling), jnp.zeros((1, 2 * width, 2 * width), BF16)], axis=0)
    head_cols = lax.dynamic_slice_in_dim(hamiltonian, group * share, share, 1)
    shared = (maps_wide, head_cols, window_tier_states)
    far = over_groups(terms((0, RINGS, 0), spot, far_lists, coup_re, coup_im, far_states, *shared))
    far = lax.ppermute(far.astype(LINK), "ado", onward(4))
    near = [
        over_groups(terms(part, spot, near_lists, coup_re, coup_im, near_states, *shared))
        for part in ((0, half, 0), (half, RINGS, 1))
    ]
    summed = lax.all_to_all(
        (jnp.concatenate(near, axis=0) + far.astype(F32)).astype(LINK), "ado", split_axis=0, concat_axis=0,
        tiled=True, axis_index_groups=DELIVER,
    )

    ham_wide = doubled(hamiltonian)
    right_part = jnp.einsum("wab,bc->wac", window_tier_states, ham_wide, preferred_element_type=F32)
    every_mode = jnp.arange(decay_rate.shape[0], dtype=jnp.int32)
    hits = modes_tri[:, :, None] == every_mode
    damping = jnp.sum(jnp.where(hits, decay_rate, 0.0), axis=(1, 2))
    own = rotate(right_part) + damping[:, None, None] * window_tier_states.astype(F32)
    return STEP_WEIGHT * (jnp.sum(summed.astype(F32), axis=0) - own)


def solution(mesh):
    in_specs = (
        P("grp", "ado", None, None, None),
        P("grp", "ado", None, None),
        P("ado", "grp", None),
        P("ado", None),
        P("ado", "grp"),
        P("ado", None),
        P(),
        P("grp", None, None),
        P("grp"),
        P("grp"),
        P(),
    )
    out_specs = P("ado", "grp", None)
    return jax.shard_map(
        on_device, mesh=mesh, in_specs=in_specs, out_specs=out_specs, check_vma=False
    )
```

```python
import functools

import jax
import jax.numpy as jnp
from jax import lax
from jax.experimental import pallas as pl
from jax.experimental.pallas import tpu as pltpu
from jax.sharding import PartitionSpec as P

STEP_WEIGHT = 0.5
F32 = jnp.float32
BF16 = jnp.bfloat16
LINK = jnp.float16
VMEM = pl.BlockSpec(memory_space=pltpu.VMEM)
SMEM = pl.BlockSpec(memory_space=pltpu.SMEM)


def doubled(matrices):
    empty = jnp.zeros_like(matrices)
    upper_half = jnp.concatenate([matrices, empty], axis=-1)
    lower_half = jnp.concatenate([empty, matrices], axis=-1)
    return jnp.concatenate([upper_half, lower_half], axis=-2)


def rotate(parts):
    width = parts.shape[-1] // 2
    return jnp.concatenate([parts[..., width:], -parts[..., :width]], axis=-1)

RINGS = 8
CAP = 3
LOT = 4
SPAN = 2 * CAP * RINGS
FAR = ((4, 0), (3, -1), (-3, 1))
NEAR = ((0, 0), (1, 1), (2, 2), (-1, -1), (-2, -2))
SIBLING = [(i, i ^ 1) for i in range(2 * RINGS * RINGS)]


def device(core, along, across):
    along, across = along % RINGS, across % RINGS
    return along * 16 + across * 2 if core == 0 else across * 16 + along * 2 + 1


def onward(step):
    return [
        (device(c, a, b), device(c, a + step, b)) for c in range(2) for a in range(RINGS) for b in range(RINGS)
    ]


DELIVER = [[device(c, a, b) for b in range(RINGS)] for c in range(2) for a in range(RINGS)]
def pick_kernel(spot_ref, own_slot, sib_slot, own_ref, sib_hbm, *refs):
    out_refs, (sib_ref, sem) = refs[:-2], refs[-2:]
    copy = pltpu.make_async_copy(sib_hbm, sib_ref, sem)
    copy.start()
    core, along = spot_ref[0], spot_ref[1]
    far = jnp.where(core == 0, 16, 2)
    near = jnp.where(core == 0, 2, 16)
    count = own_slot.shape[0] // CAP
    for kind, (slots, store) in enumerate(((own_slot, own_ref), (sib_slot, sib_ref))):
        if kind == 1:
            copy.wait()
        for (ahead, _), out_ref in zip(FAR + NEAR, out_refs, strict=True):
            first = lax.rem(along + ahead + RINGS, RINGS) * far + core
            for c in range(CAP):
                for r in range(RINGS):
                    slot = slots[c * count + first + r * near]
                    out_ref[kind * CAP * RINGS + c * RINGS + r] = store[jnp.maximum(slot, 0)]


def pick(spot, own_slots, sib_slots, own, sib):
    shape = jax.ShapeDtypeStruct((SPAN,) + own.shape[1:], own.dtype)
    return pl.pallas_call(
        pick_kernel,
        in_specs=[SMEM, SMEM, SMEM, VMEM, pl.BlockSpec(memory_space=pl.ANY)],
        out_specs=[VMEM] * len(FAR + NEAR),
        out_shape=[shape] * len(FAR + NEAR),
        scratch_shapes=[pltpu.VMEM(own.shape, own.dtype), pltpu.SemaphoreType.DMA],
        compiler_params=pltpu.CompilerParams(vmem_limit_bytes=24 * 2**20),
        cost_estimate=pl.CostEstimate(flops=0, bytes_accessed=10 * 2**20, transcendentals=0),
    )(spot, own_slots, sib_slots, own, sib)


def terms_kernel(sources, modes, windows, part, spot_ref, list_ref, re_ref, im_ref, *refs):
    flat_refs = refs[:sources]
    wide_ref, ham_ref, rho_ref = refs[sources:sources + 3]
    out_refs, (flat, acc) = refs[sources + 3:-2], refs[-2:]
    here, group = spot_ref[2], spot_ref[3]
    share = rho_ref.shape[1]
    width = ham_ref.shape[0]
    pairs = RINGS * windows
    blocks = width // share
    begin, end, slot = part
    levels = modes // LOT + CAP
    downs, extra, counts = modes, modes + CAP + slot * levels, list_ref.shape[0] - 1

    def gather(row, carry):
        for n, ref in enumerate(flat_refs):
            flat[n * SPAN + row] = ref[row]
        return carry

    lax.fori_loop(0, SPAN, gather, 0, unroll=8)

    def lot(pair, base):
        entries = [list_ref[base + n, pair] for n in range(LOT)]
        maps = [lax.shift_right_logical(e, 9) for e in entries]
        tiles = [flat[e & 511] for e in entries]
        rows = [
            wide_ref[maps[n], :width, :] + wide_ref[maps[n + 1], width:, :] for n in range(0, LOT, 2)
        ]
        left = jnp.dot(
            jnp.concatenate(rows, axis=1), jnp.concatenate(tiles, axis=0), preferred_element_type=F32
        )
        right = jnp.dot(
            jnp.concatenate(tiles, axis=1),
            jnp.concatenate([wide_ref[m] for m in maps], axis=0),
            preferred_element_type=F32,
        )
        return rotate(left - right)

    together = 8

    def first(index, carry):
        for j in range(together):
            pair = index * together + j
            acc[pair] = lot(pair, 0)
        return carry

    lax.fori_loop(begin * windows // together, end * windows // together, first, 0)

    def listed(level, work):
        def some(index, carry):
            found = [list_ref[extra + level, index * 4 + j] for j in range(4)]
            values = [work(jnp.minimum(pair, pairs - 1)) for pair in found]
            for pair, value in zip(found, values, strict=True):
                acc[pair] += value
            return carry

        lax.fori_loop(0, lax.shift_right_logical(list_ref[counts, slot * levels + level] + 3, 2), some, 0)

    def more(level, carry):
        listed(level, lambda pair: lot(pair, level * LOT))
        return carry

    lax.fori_loop(1, modes // LOT, more, 0)

    def lower(t, carry):
        def work(pair):
            entry = list_ref[downs + t, pair]
            mode = lax.shift_right_logical(entry, 9)
            state = flat[entry & 511]
            wide = wide_ref[mode]
            ahead = jnp.dot(wide[:width, :width], state, preferred_element_type=F32)
            after = jnp.dot(state, wide, preferred_element_type=F32)
            return re_ref[mode] * rotate(ahead - after) + im_ref[mode] * (ahead + after)

        listed(modes // LOT + t, work)
        return carry

    lax.fori_loop(0, CAP, lower, 0)

    if sources == len(NEAR):

        def local(w, carry):
            acc[here * windows + w] += rotate(
                jnp.dot(ham_ref[...], rho_ref[w], preferred_element_type=F32)
            )
            return carry

        lax.fori_loop(0, jnp.where((here >= begin) & (here < end), windows, 0), local, 0)

    def leave(r, carry):
        for w in range(windows):
            for shift, out_ref in enumerate(out_refs):
                block = lax.rem(group + shift, blocks) * share
                out_ref[r - begin, w] = acc[r * windows + w, pl.ds(pl.multiple_of(block, share), share), :]
        return carry

    lax.fori_loop(begin, end, leave, 0)


def terms(part, spot, lists, coup_re, coup_im, pieces, maps_wide, head_cols, rho):
    modes = maps_wide.shape[0] - 1
    windows, share, lanes = rho.shape
    width = head_cols.shape[0]
    return pl.pallas_call(
        functools.partial(terms_kernel, len(pieces), modes, windows, part),
        in_specs=[SMEM] * 4 + [VMEM] * (len(pieces) + 3),
        out_specs=[VMEM] * (width // share),
        out_shape=[jax.ShapeDtypeStruct((part[1] - part[0], windows, share, lanes), F32)] * (width // share),
        scratch_shapes=[
            pltpu.VMEM((len(pieces) * SPAN, width, lanes), BF16),
            pltpu.VMEM((RINGS * windows + 1, width, lanes), F32),
        ],
        compiler_params=pltpu.CompilerParams(vmem_limit_bytes=28 * 2**20),
        cost_estimate=pl.CostEstimate(flops=10**9, bytes_accessed=10 * 2**20, transcendentals=0),
    )(spot, lists, coup_re, coup_im, *pieces, maps_wide, head_cols, rho)


def lists_of(steps, parts, modes, spot_ref, heard_ref, out_ref):
    core, along, across, group = spot_ref[0], spot_ref[1], spot_ref[2], spot_ref[3]
    pairs = heard_ref.shape[1]
    windows = pairs // RINGS

    def locate(places):
        owner = lax.shift_right_logical(places * 171, 9)
        z, y, c = lax.shift_right_logical(owner, 4), lax.shift_right_logical(owner, 1) & 7, owner & 1
        off = (jnp.where(core == 0, z, y) - along) & (RINGS - 1)
        source = jnp.full_like(off, -1)
        for n, (_, step) in enumerate(steps):
            source = jnp.where(off == -step % RINGS, n, source)
        mine = (jnp.where(core == 0, y, z) == across) & (source >= 0)
        kind = jnp.where(c == core, 0, 1)
        lanes = lax.broadcasted_iota(jnp.int32, places.shape, 1)
        receiver = lax.shift_right_logical(lanes, windows.bit_length() - 1)
        return mine, ((source * 2 + kind) * CAP + places - owner * CAP) * RINGS + receiver

    def square(n, axis):
        return lax.broadcasted_iota(jnp.int32, (n, n), axis)

    def ones(mask):
        return jnp.where(mask, 1.0, 0.0)

    mine, row = locate(heard_ref[:modes])
    ids = lax.broadcasted_iota(jnp.int32, mine.shape, 0)
    below = ones(square(modes, 0) > square(modes, 1))
    rank = jnp.dot(below, ones(mine), preferred_element_type=F32).astype(jnp.int32)
    rank = jnp.where(mine, rank, -1)
    count = jnp.sum(ones(mine), axis=0, keepdims=True)
    value = (ids * 512 + row - modes * 512).astype(F32)
    for n in range(modes):
        found = jnp.sum(jnp.where(rank == n, value, 0.0), axis=0, keepdims=True)
        out_ref[n:n + 1] = found.astype(jnp.int32) + modes * 512

    mine, row = locate(heard_ref[modes:modes + CAP])
    local = heard_ref[modes + CAP:modes + 2 * CAP] - group * modes
    live = mine & (local >= 0) & (local < modes)
    out_ref[modes:modes + CAP] = jnp.where(live, local * 512 + row, 0)

    first = lax.broadcasted_iota(jnp.int32, (1, pairs), 1)
    flags = []
    for begin, end in parts:
        inside = (first >= begin * windows) & (first < end * windows)
        for n in range(modes // LOT):
            flags.append(ones(inside & (count > n * LOT)))
        for t in range(CAP):
            flags.append(ones(inside & live[t:t + 1]))
    total = len(flags)
    flags = jnp.concatenate(flags + [jnp.zeros((pairs - total, pairs), F32)], axis=0)
    turned = (((1,), (1,)), ((), ()))
    down, over = square(pairs, 0), square(pairs, 1)
    chosen = lax.dot_general(ones(down == over), flags, turned, preferred_element_type=F32)
    order = lax.dot_general(ones(down > over), flags, turned, preferred_element_type=F32)
    order = jnp.where(chosen > 0.5, order, -1.0)
    numbers = (down - pairs).astype(F32)
    lanes = over.astype(F32)
    for n in range(total):
        found = jnp.sum(jnp.where(order[:, n:n + 1] == lanes, numbers, 0.0), axis=0, keepdims=True)
        out_ref[modes + CAP + n:modes + CAP + n + 1] = found.astype(jnp.int32) + pairs
    sums = lax.dot_general(jnp.ones((8, pairs), F32), flags, turned, preferred_element_type=F32)
    last = out_ref.shape[0] - 1
    out_ref[last:last + 1] = sums[:1].astype(jnp.int32)


def lists_kernel(kinds, modes, spot_ref, *refs):
    for (steps, parts), heard_ref, out_ref in zip(kinds, refs[:len(kinds)], refs[len(kinds):], strict=True):
        lists_of(steps, parts, modes, spot_ref, heard_ref, out_ref)


def use_lists(kinds, modes, spot, heard):
    rows = [modes + CAP + len(parts) * (modes // LOT + CAP) + 1 for _, parts in kinds]
    return pl.pallas_call(
        functools.partial(lists_kernel, kinds, modes),
        in_specs=[SMEM] + [VMEM] * len(kinds),
        out_specs=[VMEM] * len(kinds),
        out_shape=[jax.ShapeDtypeStruct((n + -n % 8, heard[0].shape[1]), jnp.int32) for n in rows],
        compiler_params=pltpu.CompilerParams(vmem_limit_bytes=8 * 2**20),
        cost_estimate=pl.CostEstimate(flops=10**7, bytes_accessed=2**18, transcendentals=0),
    )(spot, *heard)


def say_kernel(spot_ref, up_ref, down_ref, tri_ref, out_ref):
    windows, modes = up_ref.shape
    shape = (windows, out_ref.shape[2])
    lanes = lax.broadcasted_iota(jnp.int32, shape, 1)
    row = lax.broadcasted_iota(jnp.int32, shape, 0)
    place = jnp.where(lanes == spot_ref[2] * windows + row, 1.0, 0.0)

    def put(values, axis):
        def half(part):
            return lax.dot_general(
                part.astype(F32), place, (((axis,), (0,)), ((), ())), preferred_element_type=F32
            )

        high = lax.shift_right_logical(values, 5)
        return (half(high) * 32.0 + half(values & 31)).astype(jnp.int32)

    up, down, tri = put(up_ref[...], 0), put(down_ref[...], 1), put(tri_ref[...], 1)
    spare = jnp.zeros((out_ref.shape[1] - modes - 2 * CAP, shape[1]), jnp.int32)
    whole = jnp.concatenate([up, down, tri, spare], axis=0)
    for n in range(out_ref.shape[0]):
        out_ref[n] = whole


def say(spot, use_up, use_down, modes_tri):
    windows, modes = use_up.shape
    rows = modes + 2 * CAP
    return pl.pallas_call(
        say_kernel,
        in_specs=[SMEM, VMEM, VMEM, VMEM],
        out_specs=VMEM,
        out_shape=jax.ShapeDtypeStruct((RINGS, rows + -rows % 8, RINGS * windows), jnp.int32),
        cost_estimate=pl.CostEstimate(flops=10**6, bytes_accessed=2**18, transcendentals=0),
    )(spot, use_up, use_down.T, modes_tri.T)


def over_groups(parts):
    count = len(parts)
    total = parts[0]
    for shift in (2, 1, 3):
        ring = [(i, (i + shift) % count) for i in range(count)]
        total = total + lax.ppermute(parts[shift].astype(LINK), "grp", ring).astype(F32)
    return total


def on_device(
    states, send_slot, window_tier_states, modes_tri, use_up, use_down,
    hamiltonian, coupling, coup_re, coup_im, decay_rate,
):
    width = hamiltonian.shape[0]
    windows, share = window_tier_states.shape[:2]
    modes = coupling.shape[0]
    group = lax.axis_index("grp").astype(jnp.int32)
    index = lax.axis_index("ado").astype(jnp.int32)
    core, z, y = index & 1, index >> 4, (index >> 1) & 7
    along = jnp.where(core == 0, z, y)
    across = jnp.where(core == 0, y, z)

    spot = jnp.stack([core, along, across, group])

    slots = jnp.transpose(send_slot[0, 0]).reshape(-1)
    sib_store = lax.ppermute(states[0, 0], "ado", SIBLING)
    sib_slots = lax.ppermute(slots, "ado", SIBLING)
    said, slots = lax.optimization_barrier((say(spot, use_up, use_down, modes_tri), slots))
    heard = lax.all_to_all(
        said, "ado", split_axis=0, concat_axis=0, tiled=True, axis_index_groups=DELIVER
    )
    heard = jnp.sum(heard, axis=0)
    heard_far = lax.ppermute(heard, "ado", onward(4))
    picked = pick(spot, slots, sib_slots, states[0, 0], sib_store)

    def send(steps, blocks):
        return [
            block if step == 0 else lax.ppermute(block, "ado", onward(step))
            for (_, step), block in zip(steps, blocks, strict=True)
        ]

    far_states = send(FAR, picked[:len(FAR)])
    near_states = send(NEAR, picked[len(FAR):])
    half = RINGS // 2
    held, heard_far, heard = lax.optimization_barrier((picked[0], heard_far, heard))
    far_states[0] = held
    kinds = ((FAR, ((0, RINGS),)), (NEAR, ((0, half), (half, RINGS))))
    far_lists, near_lists = use_lists(kinds, modes, spot, (heard_far, heard))

    maps_wide = jnp.concatenate([doubled(coupling), jnp.zeros((1, 2 * width, 2 * width), BF16)], axis=0)
    head_cols = lax.dynamic_slice_in_dim(hamiltonian, group * share, share, 1)
    shared = (maps_wide, head_cols, window_tier_states)
    far = terms((0, RINGS, 0), spot, far_lists, coup_re, coup_im, far_states, *shared)
    far, near_lists = lax.optimization_barrier((far, near_lists))
    far = over_groups(far)
    far = lax.ppermute(far.astype(LINK), "ado", onward(4))
    first = terms((0, half, 0), spot, near_lists, coup_re, coup_im, near_states, *shared)
    first, near_lists = lax.optimization_barrier((first, near_lists))
    second = terms((half, RINGS, 1), spot, near_lists, coup_re, coup_im, near_states, *shared)
    near = [over_groups(first), over_groups(second)]
    summed = lax.all_to_all(
        (jnp.concatenate(near, axis=0) + far.astype(F32)).astype(LINK), "ado", split_axis=0, concat_axis=0,
        tiled=True, axis_index_groups=DELIVER,
    )

    ham_wide = doubled(hamiltonian)
    right_part = jnp.einsum("wab,bc->wac", window_tier_states, ham_wide, preferred_element_type=F32)
    every_mode = jnp.arange(decay_rate.shape[0], dtype=jnp.int32)
    hits = modes_tri[:, :, None] == every_mode
    damping = jnp.sum(jnp.where(hits, decay_rate, 0.0), axis=(1, 2))
    own = rotate(right_part) + damping[:, None, None] * window_tier_states.astype(F32)
    return STEP_WEIGHT * (jnp.sum(summed.astype(F32), axis=0) - own)


def solution(mesh):
    in_specs = (
        P("grp", "ado", None, None, None),
        P("grp", "ado", None, None),
        P("ado", "grp", None),
        P("ado", None),
        P("ado", "grp"),
        P("ado", None),
        P(),
        P("grp", None, None),
        P("grp"),
        P("grp"),
        P(),
    )
    out_specs = P("ado", "grp", None)
    return jax.shard_map(
        on_device, mesh=mesh, in_specs=in_specs, out_specs=out_specs, check_vma=False
    )
```

```python
import functools

import jax
import jax.numpy as jnp
from jax import lax
from jax.experimental import pallas as pl
from jax.experimental.pallas import tpu as pltpu
from jax.sharding import PartitionSpec as P

STEP_WEIGHT = 0.5
F32 = jnp.float32
BF16 = jnp.bfloat16
LINK = jnp.float16
VMEM = pl.BlockSpec(memory_space=pltpu.VMEM)
SMEM = pl.BlockSpec(memory_space=pltpu.SMEM)


def doubled(matrices):
    empty = jnp.zeros_like(matrices)
    upper_half = jnp.concatenate([matrices, empty], axis=-1)
    lower_half = jnp.concatenate([empty, matrices], axis=-1)
    return jnp.concatenate([upper_half, lower_half], axis=-2)


def rotate(parts):
    width = parts.shape[-1] // 2
    return jnp.concatenate([parts[..., width:], -parts[..., :width]], axis=-1)

RINGS = 8
CAP = 3
LOT = 4
SPAN = 2 * CAP * RINGS
FAR = ((4, 0), (3, -1), (-3, 1))
NEAR = ((0, 0), (1, 1), (2, 2), (-1, -1), (-2, -2))
SIBLING = [(i, i ^ 1) for i in range(2 * RINGS * RINGS)]


def device(core, along, across):
    along, across = along % RINGS, across % RINGS
    return along * 16 + across * 2 if core == 0 else across * 16 + along * 2 + 1


def onward(step):
    return [
        (device(c, a, b), device(c, a + step, b)) for c in range(2) for a in range(RINGS) for b in range(RINGS)
    ]


DELIVER = [[device(c, a, b) for b in range(RINGS)] for c in range(2) for a in range(RINGS)]
def pick_kernel(spot_ref, own_slot, sib_slot, own_ref, sib_hbm, *refs):
    out_refs, (sib_ref, sem) = refs[:-2], refs[-2:]
    copy = pltpu.make_async_copy(sib_hbm, sib_ref, sem)
    copy.start()
    core, along = spot_ref[0], spot_ref[1]
    far = jnp.where(core == 0, 16, 2)
    near = jnp.where(core == 0, 2, 16)
    count = own_slot.shape[0] // CAP
    for kind, (slots, store) in enumerate(((own_slot, own_ref), (sib_slot, sib_ref))):
        if kind == 1:
            copy.wait()
        for (ahead, _), out_ref in zip(FAR + NEAR, out_refs, strict=True):
            first = lax.rem(along + ahead + RINGS, RINGS) * far + core
            for c in range(CAP):
                for r in range(RINGS):
                    slot = slots[c * count + first + r * near]
                    out_ref[kind * CAP * RINGS + c * RINGS + r] = store[jnp.maximum(slot, 0)]


def pick(spot, own_slots, sib_slots, own, sib):
    shape = jax.ShapeDtypeStruct((SPAN,) + own.shape[1:], own.dtype)
    return pl.pallas_call(
        pick_kernel,
        in_specs=[SMEM, SMEM, SMEM, VMEM, pl.BlockSpec(memory_space=pl.ANY)],
        out_specs=[VMEM] * len(FAR + NEAR),
        out_shape=[shape] * len(FAR + NEAR),
        scratch_shapes=[pltpu.VMEM(own.shape, own.dtype), pltpu.SemaphoreType.DMA],
        compiler_params=pltpu.CompilerParams(vmem_limit_bytes=24 * 2**20),
        cost_estimate=pl.CostEstimate(flops=0, bytes_accessed=10 * 2**20, transcendentals=0),
    )(spot, own_slots, sib_slots, own, sib)


def terms_kernel(sources, modes, windows, part, spot_ref, list_ref, re_ref, im_ref, *refs):
    flat_refs = refs[:sources]
    wide_ref, ham_ref, rho_ref = refs[sources:sources + 3]
    out_refs, (flat, acc) = refs[sources + 3:-2], refs[-2:]
    here, group = spot_ref[2], spot_ref[3]
    share = rho_ref.shape[1]
    width = ham_ref.shape[0]
    pairs = RINGS * windows
    blocks = width // share
    begin, end, slot = part
    levels = modes // LOT + CAP
    downs, extra, counts = modes, modes + CAP + slot * levels, list_ref.shape[0] - 1

    def gather(row, carry):
        for n, ref in enumerate(flat_refs):
            flat[n * SPAN + row] = ref[row]
        return carry

    lax.fori_loop(0, SPAN, gather, 0, unroll=8)

    def lot(pair, base):
        entries = [list_ref[base + n, pair] for n in range(LOT)]
        maps = [lax.shift_right_logical(e, 9) for e in entries]
        tiles = [flat[e & 511] for e in entries]
        rows = [
            wide_ref[maps[n], :width, :] + wide_ref[maps[n + 1], width:, :] for n in range(0, LOT, 2)
        ]
        left = jnp.dot(
            jnp.concatenate(rows, axis=1), jnp.concatenate(tiles, axis=0), preferred_element_type=F32
        )
        right = jnp.dot(
            jnp.concatenate(tiles, axis=1),
            jnp.concatenate([wide_ref[m] for m in maps], axis=0),
            preferred_element_type=F32,
        )
        return rotate(left - right)

    together = 8

    def first(index, carry):
        for j in range(together):
            pair = index * together + j
            acc[pair] = lot(pair, 0)
        return carry

    lax.fori_loop(begin * windows // together, end * windows // together, first, 0)

    def listed(level, work):
        def some(index, carry):
            found = [list_ref[extra + level, index * 4 + j] for j in range(4)]
            values = [work(jnp.minimum(pair, pairs - 1)) for pair in found]
            for pair, value in zip(found, values, strict=True):
                acc[pair] += value
            return carry

        lax.fori_loop(0, lax.shift_right_logical(list_ref[counts, slot * levels + level] + 3, 2), some, 0)

    def more(level, carry):
        listed(level, lambda pair: lot(pair, level * LOT))
        return carry

    lax.fori_loop(1, modes // LOT, more, 0)

    def lower(t, carry):
        def work(pair):
            entry = list_ref[downs + t, pair]
            mode = lax.shift_right_logical(entry, 9)
            state = flat[entry & 511]
            wide = wide_ref[mode]
            ahead = jnp.dot(wide[:width, :width], state, preferred_element_type=F32)
            after = jnp.dot(state, wide, preferred_element_type=F32)
            return re_ref[mode] * rotate(ahead - after) + im_ref[mode] * (ahead + after)

        listed(modes // LOT + t, work)
        return carry

    lax.fori_loop(0, CAP, lower, 0)

    if sources == len(NEAR):

        def local(w, carry):
            acc[here * windows + w] += rotate(
                jnp.dot(ham_ref[...], rho_ref[w], preferred_element_type=F32)
            )
            return carry

        lax.fori_loop(0, jnp.where((here >= begin) & (here < end), windows, 0), local, 0)

    def leave(r, carry):
        for w in range(windows):
            for shift, out_ref in enumerate(out_refs):
                block = lax.rem(group + shift, blocks) * share
                out_ref[r - begin, w] = acc[r * windows + w, pl.ds(pl.multiple_of(block, share), share), :]
        return carry

    lax.fori_loop(begin, end, leave, 0)


def terms(part, spot, lists, coup_re, coup_im, pieces, maps_wide, head_cols, rho):
    modes = maps_wide.shape[0] - 1
    windows, share, lanes = rho.shape
    width = head_cols.shape[0]
    return pl.pallas_call(
        functools.partial(terms_kernel, len(pieces), modes, windows, part),
        in_specs=[SMEM] * 4 + [VMEM] * (len(pieces) + 3),
        out_specs=[VMEM] * (width // share),
        out_shape=[jax.ShapeDtypeStruct((part[1] - part[0], windows, share, lanes), F32)] * (width // share),
        scratch_shapes=[
            pltpu.VMEM((len(pieces) * SPAN, width, lanes), BF16),
            pltpu.VMEM((RINGS * windows + 1, width, lanes), F32),
        ],
        compiler_params=pltpu.CompilerParams(vmem_limit_bytes=28 * 2**20),
        cost_estimate=pl.CostEstimate(flops=10**9, bytes_accessed=10 * 2**20, transcendentals=0),
    )(spot, lists, coup_re, coup_im, *pieces, maps_wide, head_cols, rho)


def lists_of(steps, parts, modes, spot_ref, heard_ref, out_ref):
    core, along, across, group = spot_ref[0], spot_ref[1], spot_ref[2], spot_ref[3]
    pairs = heard_ref.shape[1]
    windows = pairs // RINGS

    def locate(places):
        owner = lax.shift_right_logical(places * 171, 9)
        z, y, c = lax.shift_right_logical(owner, 4), lax.shift_right_logical(owner, 1) & 7, owner & 1
        off = (jnp.where(core == 0, z, y) - along) & (RINGS - 1)
        source = jnp.full_like(off, -1)
        for n, (_, step) in enumerate(steps):
            source = jnp.where(off == -step % RINGS, n, source)
        mine = (jnp.where(core == 0, y, z) == across) & (source >= 0)
        kind = jnp.where(c == core, 0, 1)
        lanes = lax.broadcasted_iota(jnp.int32, places.shape, 1)
        receiver = lax.shift_right_logical(lanes, windows.bit_length() - 1)
        return mine, ((source * 2 + kind) * CAP + places - owner * CAP) * RINGS + receiver

    def square(n, axis):
        return lax.broadcasted_iota(jnp.int32, (n, n), axis)

    def ones(mask):
        return jnp.where(mask, 1.0, 0.0)

    mine, row = locate(heard_ref[:modes])
    ids = lax.broadcasted_iota(jnp.int32, mine.shape, 0)
    below = ones(square(modes, 0) > square(modes, 1))
    rank = jnp.dot(below, ones(mine), preferred_element_type=F32).astype(jnp.int32)
    rank = jnp.where(mine, rank, -1)
    count = jnp.sum(ones(mine), axis=0, keepdims=True)
    value = (ids * 512 + row - modes * 512).astype(F32)
    for n in range(modes):
        found = jnp.sum(jnp.where(rank == n, value, 0.0), axis=0, keepdims=True)
        out_ref[n:n + 1] = found.astype(jnp.int32) + modes * 512

    mine, row = locate(heard_ref[modes:modes + CAP])
    local = heard_ref[modes + CAP:modes + 2 * CAP] - group * modes
    live = mine & (local >= 0) & (local < modes)
    out_ref[modes:modes + CAP] = jnp.where(live, local * 512 + row, 0)

    first = lax.broadcasted_iota(jnp.int32, (1, pairs), 1)
    flags = []
    for begin, end in parts:
        inside = (first >= begin * windows) & (first < end * windows)
        for n in range(modes // LOT):
            flags.append(ones(inside & (count > n * LOT)))
        for t in range(CAP):
            flags.append(ones(inside & live[t:t + 1]))
    total = len(flags)
    flags = jnp.concatenate(flags + [jnp.zeros((pairs - total, pairs), F32)], axis=0)
    turned = (((1,), (1,)), ((), ()))
    down, over = square(pairs, 0), square(pairs, 1)
    chosen = lax.dot_general(ones(down == over), flags, turned, preferred_element_type=F32)
    order = lax.dot_general(ones(down > over), flags, turned, preferred_element_type=F32)
    order = jnp.where(chosen > 0.5, order, -1.0)
    numbers = (down - pairs).astype(F32)
    lanes = over.astype(F32)
    for n in range(total):
        found = jnp.sum(jnp.where(order[:, n:n + 1] == lanes, numbers, 0.0), axis=0, keepdims=True)
        out_ref[modes + CAP + n:modes + CAP + n + 1] = found.astype(jnp.int32) + pairs
    sums = lax.dot_general(jnp.ones((8, pairs), F32), flags, turned, preferred_element_type=F32)
    last = out_ref.shape[0] - 1
    out_ref[last:last + 1] = sums[:1].astype(jnp.int32)


def lists_kernel(kinds, modes, spot_ref, *refs):
    for (steps, parts), heard_ref, out_ref in zip(kinds, refs[:len(kinds)], refs[len(kinds):], strict=True):
        lists_of(steps, parts, modes, spot_ref, heard_ref, out_ref)


def use_lists(kinds, modes, spot, heard):
    rows = [modes + CAP + len(parts) * (modes // LOT + CAP) + 1 for _, parts in kinds]
    return pl.pallas_call(
        functools.partial(lists_kernel, kinds, modes),
        in_specs=[SMEM] + [VMEM] * len(kinds),
        out_specs=[VMEM] * len(kinds),
        out_shape=[jax.ShapeDtypeStruct((n + -n % 8, heard[0].shape[1]), jnp.int32) for n in rows],
        compiler_params=pltpu.CompilerParams(vmem_limit_bytes=8 * 2**20),
        cost_estimate=pl.CostEstimate(flops=10**7, bytes_accessed=2**18, transcendentals=0),
    )(spot, *heard)


def say_kernel(spot_ref, up_ref, down_ref, tri_ref, out_ref):
    windows, modes = up_ref.shape
    shape = (windows, out_ref.shape[2])
    lanes = lax.broadcasted_iota(jnp.int32, shape, 1)
    row = lax.broadcasted_iota(jnp.int32, shape, 0)
    place = jnp.where(lanes == spot_ref[2] * windows + row, 1.0, 0.0)

    def put(values, axis):
        def half(part):
            return lax.dot_general(
                part.astype(F32), place, (((axis,), (0,)), ((), ())), preferred_element_type=F32
            )

        high = lax.shift_right_logical(values, 5)
        return (half(high) * 32.0 + half(values & 31)).astype(jnp.int32)

    up, down, tri = put(up_ref[...], 0), put(down_ref[...], 1), put(tri_ref[...], 1)
    spare = jnp.zeros((out_ref.shape[1] - modes - 2 * CAP, shape[1]), jnp.int32)
    whole = jnp.concatenate([up, down, tri, spare], axis=0)
    for n in range(out_ref.shape[0]):
        out_ref[n] = whole


def say(spot, use_up, use_down, modes_tri):
    windows, modes = use_up.shape
    rows = modes + 2 * CAP
    return pl.pallas_call(
        say_kernel,
        in_specs=[SMEM, VMEM, VMEM, VMEM],
        out_specs=VMEM,
        out_shape=jax.ShapeDtypeStruct((RINGS, rows + -rows % 8, RINGS * windows), jnp.int32),
        cost_estimate=pl.CostEstimate(flops=10**6, bytes_accessed=2**18, transcendentals=0),
    )(spot, use_up, use_down.T, modes_tri.T)


def over_groups(parts):
    count = len(parts)
    total = parts[0]
    for shift in (2, 1, 3):
        ring = [(i, (i + shift) % count) for i in range(count)]
        total = total + lax.ppermute(parts[shift].astype(LINK), "grp", ring).astype(F32)
    return total


def on_device(
    states, send_slot, window_tier_states, modes_tri, use_up, use_down,
    hamiltonian, coupling, coup_re, coup_im, decay_rate,
):
    width = hamiltonian.shape[0]
    windows, share = window_tier_states.shape[:2]
    modes = coupling.shape[0]
    group = lax.axis_index("grp").astype(jnp.int32)
    index = lax.axis_index("ado").astype(jnp.int32)
    core, z, y = index & 1, index >> 4, (index >> 1) & 7
    along = jnp.where(core == 0, z, y)
    across = jnp.where(core == 0, y, z)

    spot = jnp.stack([core, along, across, group])

    slots = jnp.transpose(send_slot[0, 0]).reshape(-1)
    sib_store = lax.ppermute(states[0, 0], "ado", SIBLING)
    sib_slots = lax.ppermute(slots, "ado", SIBLING)
    heard = lax.all_to_all(
        say(spot, use_up, use_down, modes_tri), "ado", split_axis=0, concat_axis=0, tiled=True,
        axis_index_groups=DELIVER,
    )
    heard, slots = lax.optimization_barrier((jnp.sum(heard, axis=0), slots))
    heard_far = lax.ppermute(heard, "ado", onward(4))
    picked = pick(spot, slots, sib_slots, states[0, 0], sib_store)

    def send(steps, blocks):
        return [
            block if step == 0 else lax.ppermute(block, "ado", onward(step))
            for (_, step), block in zip(steps, blocks, strict=True)
        ]

    far_states = send(FAR, picked[:len(FAR)])
    near_states = send(NEAR, picked[len(FAR):])
    half = RINGS // 2
    held, heard_far, heard = lax.optimization_barrier((picked[0], heard_far, heard))
    far_states[0] = held
    kinds = ((FAR, ((0, RINGS),)), (NEAR, ((0, half), (half, RINGS))))
    far_lists, near_lists = use_lists(kinds, modes, spot, (heard_far, heard))

    maps_wide = jnp.concatenate([doubled(coupling), jnp.zeros((1, 2 * width, 2 * width), BF16)], axis=0)
    head_cols = lax.dynamic_slice_in_dim(hamiltonian, group * share, share, 1)
    shared = (maps_wide, head_cols, window_tier_states)
    far = terms((0, RINGS, 0), spot, far_lists, coup_re, coup_im, far_states, *shared)
    far, near_lists = lax.optimization_barrier((far, near_lists))
    far = over_groups(far)
    far = lax.ppermute(far.astype(LINK), "ado", onward(4))
    first = terms((0, half, 0), spot, near_lists, coup_re, coup_im, near_states, *shared)
    first, near_lists = lax.optimization_barrier((first, near_lists))
    second = terms((half, RINGS, 1), spot, near_lists, coup_re, coup_im, near_states, *shared)
    near = [over_groups(first), over_groups(second)]
    summed = lax.all_to_all(
        (jnp.concatenate(near, axis=0) + far.astype(F32)).astype(LINK), "ado", split_axis=0, concat_axis=0,
        tiled=True, axis_index_groups=DELIVER,
    )

    ham_wide = doubled(hamiltonian)
    right_part = jnp.einsum("wab,bc->wac", window_tier_states, ham_wide, preferred_element_type=F32)
    every_mode = jnp.arange(decay_rate.shape[0], dtype=jnp.int32)
    hits = modes_tri[:, :, None] == every_mode
    damping = jnp.sum(jnp.where(hits, decay_rate, 0.0), axis=(1, 2))
    own = rotate(right_part) + damping[:, None, None] * window_tier_states.astype(F32)
    return STEP_WEIGHT * (jnp.sum(summed.astype(F32), axis=0) - own)


def solution(mesh):
    in_specs = (
        P("grp", "ado", None, None, None),
        P("grp", "ado", None, None),
        P("ado", "grp", None),
        P("ado", None),
        P("ado", "grp"),
        P("ado", None),
        P(),
        P("grp", None, None),
        P("grp"),
        P("grp"),
        P(),
    )
    out_specs = P("ado", "grp", None)
    return jax.shard_map(
        on_device, mesh=mesh, in_specs=in_specs, out_specs=out_specs, check_vma=False
    )
```

```python
import functools

import jax
import jax.numpy as jnp
from jax import lax
from jax.experimental import pallas as pl
from jax.experimental.pallas import tpu as pltpu
from jax.sharding import PartitionSpec as P

STEP_WEIGHT = 0.5
F32 = jnp.float32
BF16 = jnp.bfloat16
LINK = jnp.float16
VMEM = pl.BlockSpec(memory_space=pltpu.VMEM)
SMEM = pl.BlockSpec(memory_space=pltpu.SMEM)


def doubled(matrices):
    empty = jnp.zeros_like(matrices)
    upper_half = jnp.concatenate([matrices, empty], axis=-1)
    lower_half = jnp.concatenate([empty, matrices], axis=-1)
    return jnp.concatenate([upper_half, lower_half], axis=-2)


def rotate(parts):
    width = parts.shape[-1] // 2
    return jnp.concatenate([parts[..., width:], -parts[..., :width]], axis=-1)

RINGS = 8
CAP = 3
LOT = 4
SPAN = 2 * CAP * RINGS
FAR = ((4, 0), (3, -1), (-3, 1))
NEAR = ((0, 0), (1, 1), (2, 2), (-1, -1), (-2, -2))
SIBLING = [(i, i ^ 1) for i in range(2 * RINGS * RINGS)]


def device(core, along, across):
    along, across = along % RINGS, across % RINGS
    return along * 16 + across * 2 if core == 0 else across * 16 + along * 2 + 1


def onward(step):
    return [
        (device(c, a, b), device(c, a + step, b)) for c in range(2) for a in range(RINGS) for b in range(RINGS)
    ]


DELIVER = [[device(c, a, b) for b in range(RINGS)] for c in range(2) for a in range(RINGS)]
LISTENERS = [
    [device(c, a + far, b) for far in (0, 4) for b in range(RINGS)] for c in range(2) for a in range(RINGS // 2)
]


def pick_kernel(spot_ref, own_slot, sib_slot, own_ref, sib_hbm, *refs):
    out_refs, (sib_ref, sem) = refs[:-2], refs[-2:]
    copy = pltpu.make_async_copy(sib_hbm, sib_ref, sem)
    copy.start()
    core, along = spot_ref[0], spot_ref[1]
    far = jnp.where(core == 0, 16, 2)
    near = jnp.where(core == 0, 2, 16)
    count = own_slot.shape[0] // CAP
    for kind, (slots, store) in enumerate(((own_slot, own_ref), (sib_slot, sib_ref))):
        if kind == 1:
            copy.wait()
        for (ahead, _), out_ref in zip(FAR + NEAR, out_refs, strict=True):
            first = lax.rem(along + ahead + RINGS, RINGS) * far + core
            for c in range(CAP):
                for r in range(RINGS):
                    slot = slots[c * count + first + r * near]
                    out_ref[kind * CAP * RINGS + c * RINGS + r] = store[jnp.maximum(slot, 0)]


def pick(spot, own_slots, sib_slots, own, sib):
    shape = jax.ShapeDtypeStruct((SPAN,) + own.shape[1:], own.dtype)
    return pl.pallas_call(
        pick_kernel,
        in_specs=[SMEM, SMEM, SMEM, VMEM, pl.BlockSpec(memory_space=pl.ANY)],
        out_specs=[VMEM] * len(FAR + NEAR),
        out_shape=[shape] * len(FAR + NEAR),
        scratch_shapes=[pltpu.VMEM(own.shape, own.dtype), pltpu.SemaphoreType.DMA],
        compiler_params=pltpu.CompilerParams(vmem_limit_bytes=24 * 2**20),
        cost_estimate=pl.CostEstimate(flops=0, bytes_accessed=10 * 2**20, transcendentals=0),
    )(spot, own_slots, sib_slots, own, sib)


def terms_kernel(sources, modes, windows, part, spot_ref, list_ref, re_ref, im_ref, *refs):
    flat_refs = refs[:sources]
    wide_ref, ham_ref, rho_ref = refs[sources:sources + 3]
    out_refs, (flat, acc) = refs[sources + 3:-2], refs[-2:]
    here, group = spot_ref[2], spot_ref[3]
    share = rho_ref.shape[1]
    width = ham_ref.shape[0]
    pairs = RINGS * windows
    blocks = width // share
    begin, end, slot = part
    levels = modes // LOT + CAP
    downs, extra, counts = modes, modes + CAP + slot * levels, list_ref.shape[0] - 1

    def gather(row, carry):
        for n, ref in enumerate(flat_refs):
            flat[n * SPAN + row] = ref[row]
        return carry

    lax.fori_loop(0, SPAN, gather, 0, unroll=8)

    def lot(pair, base):
        entries = [list_ref[base + n, pair] for n in range(LOT)]
        maps = [lax.shift_right_logical(e, 9) for e in entries]
        tiles = [flat[e & 511] for e in entries]
        rows = [
            wide_ref[maps[n], :width, :] + wide_ref[maps[n + 1], width:, :] for n in range(0, LOT, 2)
        ]
        left = jnp.dot(
            jnp.concatenate(rows, axis=1), jnp.concatenate(tiles, axis=0), preferred_element_type=F32
        )
        right = jnp.dot(
            jnp.concatenate(tiles, axis=1),
            jnp.concatenate([wide_ref[m] for m in maps], axis=0),
            preferred_element_type=F32,
        )
        return rotate(left - right)

    together = 16

    def first(index, carry):
        for j in range(together):
            pair = index * together + j
            acc[pair] = lot(pair, 0)
        return carry

    lax.fori_loop(begin * windows // together, end * windows // together, first, 0)

    def listed(level, work):
        def some(index, carry):
            found = [list_ref[extra + level, index * 4 + j] for j in range(4)]
            values = [work(jnp.minimum(pair, pairs - 1)) for pair in found]
            for pair, value in zip(found, values, strict=True):
                acc[pair] += value
            return carry

        lax.fori_loop(0, lax.shift_right_logical(list_ref[counts, slot * levels + level] + 3, 2), some, 0)

    def more(level, carry):
        listed(level, lambda pair: lot(pair, level * LOT))
        return carry

    lax.fori_loop(1, modes // LOT, more, 0)

    def lower(t, carry):
        def work(pair):
            entry = list_ref[downs + t, pair]
            mode = lax.shift_right_logical(entry, 9)
            state = flat[entry & 511]
            wide = wide_ref[mode]
            ahead = jnp.dot(wide[:width, :width], state, preferred_element_type=F32)
            after = jnp.dot(state, wide, preferred_element_type=F32)
            return re_ref[mode] * rotate(ahead - after) + im_ref[mode] * (ahead + after)

        listed(modes // LOT + t, work)
        return carry

    lax.fori_loop(0, CAP, lower, 0)

    if sources == len(NEAR):

        for w in range(windows):
            acc[here * windows + w] += rotate(
                jnp.dot(ham_ref[...], rho_ref[w], preferred_element_type=F32)
            )

    def leave(r, carry):
        for w in range(windows):
            for shift, out_ref in enumerate(out_refs):
                block = lax.rem(group + shift, blocks) * share
                out_ref[r - begin, w] = acc[r * windows + w, pl.ds(pl.multiple_of(block, share), share), :]
        return carry

    lax.fori_loop(begin, end, leave, 0)


def terms(part, spot, lists, coup_re, coup_im, pieces, maps_wide, head_cols, rho):
    modes = maps_wide.shape[0] - 1
    windows, share, lanes = rho.shape
    width = head_cols.shape[0]
    return pl.pallas_call(
        functools.partial(terms_kernel, len(pieces), modes, windows, part),
        in_specs=[SMEM] * 4 + [VMEM] * (len(pieces) + 3),
        out_specs=[VMEM] * (width // share),
        out_shape=[jax.ShapeDtypeStruct((part[1] - part[0], windows, share, lanes), F32)] * (width // share),
        scratch_shapes=[
            pltpu.VMEM((len(pieces) * SPAN, width, lanes), BF16),
            pltpu.VMEM((RINGS * windows + 1, width, lanes), F32),
        ],
        compiler_params=pltpu.CompilerParams(vmem_limit_bytes=28 * 2**20),
        cost_estimate=pl.CostEstimate(flops=10**9, bytes_accessed=10 * 2**20, transcendentals=0),
    )(spot, lists, coup_re, coup_im, *pieces, maps_wide, head_cols, rho)


def lists_of(steps, parts, modes, spot_ref, heard_ref, out_ref):
    core, along, across, group = spot_ref[0], spot_ref[1], spot_ref[2], spot_ref[3]
    pairs = heard_ref.shape[1]
    windows = pairs // RINGS

    def locate(places):
        owner = lax.shift_right_logical(places * 171, 9)
        z, y, c = lax.shift_right_logical(owner, 4), lax.shift_right_logical(owner, 1) & 7, owner & 1
        off = (jnp.where(core == 0, z, y) - along) & (RINGS - 1)
        source = jnp.full_like(off, -1)
        for n, (_, step) in enumerate(steps):
            source = jnp.where(off == -step % RINGS, n, source)
        mine = (jnp.where(core == 0, y, z) == across) & (source >= 0)
        kind = jnp.where(c == core, 0, 1)
        lanes = lax.broadcasted_iota(jnp.int32, places.shape, 1)
        receiver = lax.shift_right_logical(lanes, windows.bit_length() - 1)
        return mine, ((source * 2 + kind) * CAP + places - owner * CAP) * RINGS + receiver

    def square(n, axis):
        return lax.broadcasted_iota(jnp.int32, (n, n), axis)

    def ones(mask):
        return jnp.where(mask, 1.0, 0.0)

    mine, row = locate(heard_ref[:modes])
    ids = lax.broadcasted_iota(jnp.int32, mine.shape, 0)
    below = ones(square(modes, 0) > square(modes, 1))
    rank = jnp.dot(below, ones(mine), preferred_element_type=F32).astype(jnp.int32)
    rank = jnp.where(mine, rank, -1)
    count = jnp.sum(ones(mine), axis=0, keepdims=True)
    value = (ids * 512 + row - modes * 512).astype(F32)
    for n in range(modes):
        found = jnp.sum(jnp.where(rank == n, value, 0.0), axis=0, keepdims=True)
        out_ref[n:n + 1] = found.astype(jnp.int32) + modes * 512

    mine, row = locate(heard_ref[modes:modes + CAP])
    local = heard_ref[modes + CAP:modes + 2 * CAP] - group * modes
    live = mine & (local >= 0) & (local < modes)
    out_ref[modes:modes + CAP] = jnp.where(live, local * 512 + row, 0)

    first = lax.broadcasted_iota(jnp.int32, (1, pairs), 1)
    flags = []
    for begin, end in parts:
        inside = (first >= begin * windows) & (first < end * windows)
        for n in range(modes // LOT):
            flags.append(ones(inside & (count > n * LOT)))
        for t in range(CAP):
            flags.append(ones(inside & live[t:t + 1]))
    total = len(flags)
    flags = jnp.concatenate(flags + [jnp.zeros((pairs - total, pairs), F32)], axis=0)
    turned = (((1,), (1,)), ((), ()))
    down, over = square(pairs, 0), square(pairs, 1)
    chosen = lax.dot_general(ones(down == over), flags, turned, preferred_element_type=F32)
    order = lax.dot_general(ones(down > over), flags, turned, preferred_element_type=F32)
    order = jnp.where(chosen > 0.5, order, -1.0)
    numbers = (down - pairs).astype(F32)
    lanes = over.astype(F32)
    for n in range(total):
        found = jnp.sum(jnp.where(order[:, n:n + 1] == lanes, numbers, 0.0), axis=0, keepdims=True)
        out_ref[modes + CAP + n:modes + CAP + n + 1] = found.astype(jnp.int32) + pairs
    sums = lax.dot_general(jnp.ones((8, pairs), F32), flags, turned, preferred_element_type=F32)
    last = out_ref.shape[0] - 1
    out_ref[last:last + 1] = sums[:1].astype(jnp.int32)


def lists_kernel(kinds, modes, spot_ref, heard_ref, *refs):
    out_refs, sum_ref = refs[:-1], refs[-1]
    half = lax.shift_right_logical(spot_ref[1], 2)
    for (steps, parts, far), out_ref in zip(kinds, out_refs, strict=True):
        begin = (half ^ far) * RINGS
        sum_ref[...] = sum(heard_ref[begin + r] for r in range(RINGS))
        lists_of(steps, parts, modes, spot_ref, sum_ref, out_ref)


def use_lists(kinds, modes, spot, heard):
    rows = [modes + CAP + len(parts) * (modes // LOT + CAP) + 1 for _, parts, _ in kinds]
    return pl.pallas_call(
        functools.partial(lists_kernel, kinds, modes),
        in_specs=[SMEM, VMEM],
        out_specs=[VMEM] * len(kinds),
        out_shape=[jax.ShapeDtypeStruct((n + -n % 8, heard.shape[2]), jnp.int32) for n in rows],
        scratch_shapes=[pltpu.VMEM(heard.shape[1:], jnp.int32)],
        compiler_params=pltpu.CompilerParams(vmem_limit_bytes=8 * 2**20),
        cost_estimate=pl.CostEstimate(flops=10**7, bytes_accessed=2**18, transcendentals=0),
    )(spot, heard)


def say_kernel(spot_ref, up_ref, down_ref, tri_ref, out_ref):
    windows, modes = up_ref.shape
    shape = (windows, out_ref.shape[2])
    lanes = lax.broadcasted_iota(jnp.int32, shape, 1)
    row = lax.broadcasted_iota(jnp.int32, shape, 0)
    place = jnp.where(lanes == spot_ref[2] * windows + row, 1.0, 0.0)

    def put(values, axis):
        def half(part):
            return lax.dot_general(
                part.astype(F32), place, (((axis,), (0,)), ((), ())), preferred_element_type=F32
            )

        high = lax.shift_right_logical(values, 5)
        return (half(high) * 32.0 + half(values & 31)).astype(jnp.int32)

    up, down, tri = put(up_ref[...], 0), put(down_ref[...], 1), put(tri_ref[...], 1)
    spare = jnp.zeros((out_ref.shape[1] - modes - 2 * CAP, shape[1]), jnp.int32)
    whole = jnp.concatenate([up, down, tri, spare], axis=0)
    for n in range(out_ref.shape[0]):
        out_ref[n] = whole


def say(spot, use_up, use_down, modes_tri):
    windows, modes = use_up.shape
    rows = modes + 2 * CAP
    return pl.pallas_call(
        say_kernel,
        in_specs=[SMEM, VMEM, VMEM, VMEM],
        out_specs=VMEM,
        out_shape=jax.ShapeDtypeStruct((2 * RINGS, rows + -rows % 8, RINGS * windows), jnp.int32),
        cost_estimate=pl.CostEstimate(flops=10**6, bytes_accessed=2**18, transcendentals=0),
    )(spot, use_up, use_down.T, modes_tri.T)


def over_groups(parts):
    count = len(parts)
    total = parts[0]
    for shift in (2, 1, 3):
        ring = [(i, (i + shift) % count) for i in range(count)]
        total = total + lax.ppermute(parts[shift].astype(LINK), "grp", ring).astype(F32)
    return total


def on_device(
    states, send_slot, window_tier_states, modes_tri, use_up, use_down,
    hamiltonian, coupling, coup_re, coup_im, decay_rate,
):
    width = hamiltonian.shape[0]
    windows, share = window_tier_states.shape[:2]
    modes = coupling.shape[0]
    group = lax.axis_index("grp").astype(jnp.int32)
    index = lax.axis_index("ado").astype(jnp.int32)
    core, z, y = index & 1, index >> 4, (index >> 1) & 7
    along = jnp.where(core == 0, z, y)
    across = jnp.where(core == 0, y, z)

    spot = jnp.stack([core, along, across, group])

    slots = jnp.transpose(send_slot[0, 0]).reshape(-1)
    sib_store = lax.ppermute(states[0, 0], "ado", SIBLING)
    sib_slots = lax.ppermute(slots, "ado", SIBLING)
    heard = lax.all_to_all(
        say(spot, use_up, use_down, modes_tri), "ado", split_axis=0, concat_axis=0, tiled=True,
        axis_index_groups=LISTENERS,
    )
    heard, slots = lax.optimization_barrier((heard, slots))
    picked = pick(spot, slots, sib_slots, states[0, 0], sib_store)

    def send(steps, blocks):
        return [
            block if step == 0 else lax.ppermute(block, "ado", onward(step))
            for (_, step), block in zip(steps, blocks, strict=True)
        ]

    far_states = send(FAR, picked[:len(FAR)])
    near_states = send(NEAR, picked[len(FAR):])
    held, heard = lax.optimization_barrier((picked[0], heard))
    far_states[0] = held
    kinds = ((FAR, ((0, RINGS),), 1), (NEAR, ((0, RINGS),), 0))
    far_lists, near_lists = use_lists(kinds, modes, spot, heard)

    maps_wide = jnp.concatenate([doubled(coupling), jnp.zeros((1, 2 * width, 2 * width), BF16)], axis=0)
    head_cols = lax.dynamic_slice_in_dim(hamiltonian, group * share, share, 1)
    shared = (maps_wide, head_cols, window_tier_states)
    far = terms((0, RINGS, 0), spot, far_lists, coup_re, coup_im, far_states, *shared)
    far, near_lists = lax.optimization_barrier((far, near_lists))
    far = over_groups(far)
    far = lax.ppermute(far.astype(LINK), "ado", onward(4))
    near = over_groups(terms((0, RINGS, 0), spot, near_lists, coup_re, coup_im, near_states, *shared))
    summed = lax.all_to_all(
        (near + far.astype(F32)).astype(LINK), "ado", split_axis=0, concat_axis=0,
        tiled=True, axis_index_groups=DELIVER,
    )

    ham_wide = doubled(hamiltonian)
    right_part = jnp.einsum("wab,bc->wac", window_tier_states, ham_wide, preferred_element_type=F32)
    every_mode = jnp.arange(decay_rate.shape[0], dtype=jnp.int32)
    hits = modes_tri[:, :, None] == every_mode
    damping = jnp.sum(jnp.where(hits, decay_rate, 0.0), axis=(1, 2))
    own = rotate(right_part) + damping[:, None, None] * window_tier_states.astype(F32)
    return STEP_WEIGHT * (jnp.sum(summed.astype(F32), axis=0) - own)


def solution(mesh):
    in_specs = (
        P("grp", "ado", None, None, None),
        P("grp", "ado", None, None),
        P("ado", "grp", None),
        P("ado", None),
        P("ado", "grp"),
        P("ado", None),
        P(),
        P("grp", None, None),
        P("grp"),
        P("grp"),
        P(),
    )
    out_specs = P("ado", "grp", None)
    return jax.shard_map(
        on_device, mesh=mesh, in_specs=in_specs, out_specs=out_specs, check_vma=False
    )
```

```python
import functools

import jax
import jax.numpy as jnp
from jax import lax
from jax.experimental import pallas as pl
from jax.experimental.pallas import tpu as pltpu
from jax.sharding import PartitionSpec as P

STEP_WEIGHT = 0.5
F32 = jnp.float32
BF16 = jnp.bfloat16
LINK = jnp.float16
VMEM = pl.BlockSpec(memory_space=pltpu.VMEM)
SMEM = pl.BlockSpec(memory_space=pltpu.SMEM)


def doubled(matrices):
    empty = jnp.zeros_like(matrices)
    upper_half = jnp.concatenate([matrices, empty], axis=-1)
    lower_half = jnp.concatenate([empty, matrices], axis=-1)
    return jnp.concatenate([upper_half, lower_half], axis=-2)


def rotate(parts):
    width = parts.shape[-1] // 2
    return jnp.concatenate([parts[..., width:], -parts[..., :width]], axis=-1)

RINGS = 8
CAP = 3
LOT = 4
SPAN = 2 * CAP * RINGS
FAR = ((4, 0), (3, -1), (-3, 1))
NEAR = ((0, 0), (1, 1), (2, 2), (-1, -1), (-2, -2))
SIBLING = [(i, i ^ 1) for i in range(2 * RINGS * RINGS)]


def device(core, along, across):
    along, across = along % RINGS, across % RINGS
    return along * 16 + across * 2 if core == 0 else across * 16 + along * 2 + 1


def onward(step):
    return [
        (device(c, a, b), device(c, a + step, b)) for c in range(2) for a in range(RINGS) for b in range(RINGS)
    ]


DELIVER = [[device(c, a, b) for b in range(RINGS)] for c in range(2) for a in range(RINGS)]


def pick_kernel(spot_ref, own_slot, sib_slot, own_ref, sib_hbm, *refs):
    out_refs, (sib_ref, sem) = refs[:-2], refs[-2:]
    copy = pltpu.make_async_copy(sib_hbm, sib_ref, sem)
    copy.start()
    core, along = spot_ref[0], spot_ref[1]
    far = jnp.where(core == 0, 16, 2)
    near = jnp.where(core == 0, 2, 16)
    count = own_slot.shape[0] // CAP
    for kind, (slots, store) in enumerate(((own_slot, own_ref), (sib_slot, sib_ref))):
        if kind == 1:
            copy.wait()
        for (ahead, _), out_ref in zip(FAR + NEAR, out_refs, strict=True):
            first = lax.rem(along + ahead + RINGS, RINGS) * far + core
            for c in range(CAP):
                for r in range(RINGS):
                    slot = slots[c * count + first + r * near]
                    out_ref[kind * CAP * RINGS + c * RINGS + r] = store[jnp.maximum(slot, 0)]


def pick(spot, own_slots, sib_slots, own, sib):
    shape = jax.ShapeDtypeStruct((SPAN,) + own.shape[1:], own.dtype)
    return pl.pallas_call(
        pick_kernel,
        in_specs=[SMEM, SMEM, SMEM, VMEM, pl.BlockSpec(memory_space=pl.ANY)],
        out_specs=[VMEM] * len(FAR + NEAR),
        out_shape=[shape] * len(FAR + NEAR),
        scratch_shapes=[pltpu.VMEM(own.shape, own.dtype), pltpu.SemaphoreType.DMA],
        compiler_params=pltpu.CompilerParams(vmem_limit_bytes=24 * 2**20),
        cost_estimate=pl.CostEstimate(flops=0, bytes_accessed=10 * 2**20, transcendentals=0),
    )(spot, own_slots, sib_slots, own, sib)


def terms_kernel(sources, modes, windows, part, spot_ref, list_ref, re_ref, im_ref, *refs):
    flat_refs = refs[:sources]
    wide_ref, ham_ref, rho_ref = refs[sources:sources + 3]
    out_refs, (flat, acc, sems) = refs[sources + 3:-3], refs[-3:]
    here, group = spot_ref[2], spot_ref[3]
    share = rho_ref.shape[1]
    width = ham_ref.shape[0]
    pairs = RINGS * windows
    blocks = width // share
    begin, end, slot = part
    levels = modes // LOT + CAP
    downs, extra, counts = modes, modes + CAP + slot * levels, list_ref.shape[0] - 1

    copies = [
        pltpu.make_async_copy(ref, flat.at[pl.ds(n * SPAN, SPAN)], sems.at[n]) for n, ref in enumerate(flat_refs)
    ]
    for copy in copies:
        copy.start()
    for copy in copies:
        copy.wait()

    def lot(pair, base):
        entries = [list_ref[base + n, pair] for n in range(LOT)]
        maps = [lax.shift_right_logical(e, 9) for e in entries]
        tiles = [flat[e & 511] for e in entries]
        rows = [
            wide_ref[maps[n], :width, :] + wide_ref[maps[n + 1], width:, :] for n in range(0, LOT, 2)
        ]
        left = jnp.dot(
            jnp.concatenate(rows, axis=1), jnp.concatenate(tiles, axis=0), preferred_element_type=F32
        )
        right = jnp.dot(
            jnp.concatenate(tiles, axis=1),
            jnp.concatenate([wide_ref[m] for m in maps], axis=0),
            preferred_element_type=F32,
        )
        return rotate(left - right)

    together = 16

    def first(index, carry):
        for j in range(together):
            pair = index * together + j
            acc[pair] = lot(pair, 0)
        return carry

    lax.fori_loop(begin * windows // together, end * windows // together, first, 0)

    def listed(level, work):
        def some(index, carry):
            found = [list_ref[extra + level, index * 4 + j] for j in range(4)]
            values = [work(jnp.minimum(pair, pairs - 1)) for pair in found]
            for pair, value in zip(found, values, strict=True):
                acc[pair] += value
            return carry

        lax.fori_loop(0, lax.shift_right_logical(list_ref[counts, slot * levels + level] + 3, 2), some, 0)

    def more(level, carry):
        listed(level, lambda pair: lot(pair, level * LOT))
        return carry

    lax.fori_loop(1, modes // LOT, more, 0)

    def lower(t, carry):
        def work(pair):
            entry = list_ref[downs + t, pair]
            mode = lax.shift_right_logical(entry, 9)
            state = flat[entry & 511]
            wide = wide_ref[mode]
            ahead = jnp.dot(wide[:width, :width], state, preferred_element_type=F32)
            after = jnp.dot(state, wide, preferred_element_type=F32)
            return re_ref[mode] * rotate(ahead - after) + im_ref[mode] * (ahead + after)

        listed(modes // LOT + t, work)
        return carry

    lax.fori_loop(0, CAP, lower, 0)

    if sources == len(NEAR):

        for w in range(windows):
            acc[here * windows + w] += rotate(
                jnp.dot(ham_ref[...], rho_ref[w], preferred_element_type=F32)
            )

    def leave(r, carry):
        for w in range(windows):
            for shift, out_ref in enumerate(out_refs):
                block = lax.rem(group + shift, blocks) * share
                out_ref[r - begin, w] = acc[r * windows + w, pl.ds(pl.multiple_of(block, share), share), :]
        return carry

    lax.fori_loop(begin, end, leave, 0)


def terms(part, spot, lists, coup_re, coup_im, pieces, maps_wide, head_cols, rho):
    modes = maps_wide.shape[0] - 1
    windows, share, lanes = rho.shape
    width = head_cols.shape[0]
    return pl.pallas_call(
        functools.partial(terms_kernel, len(pieces), modes, windows, part),
        in_specs=[SMEM] * 4 + [pl.BlockSpec(memory_space=pl.ANY)] * len(pieces) + [VMEM] * 3,
        out_specs=[VMEM] * (width // share),
        out_shape=[jax.ShapeDtypeStruct((part[1] - part[0], windows, share, lanes), F32)] * (width // share),
        scratch_shapes=[
            pltpu.VMEM((len(pieces) * SPAN, width, lanes), BF16),
            pltpu.VMEM((RINGS * windows + 1, width, lanes), F32),
            pltpu.SemaphoreType.DMA((len(pieces),)),
        ],
        compiler_params=pltpu.CompilerParams(vmem_limit_bytes=28 * 2**20),
        cost_estimate=pl.CostEstimate(flops=10**9, bytes_accessed=10 * 2**20, transcendentals=0),
    )(spot, lists, coup_re, coup_im, *pieces, maps_wide, head_cols, rho)


def lists_of(steps, parts, modes, spot_ref, heard_ref, out_ref):
    core, along, across, group = spot_ref[0], spot_ref[1], spot_ref[2], spot_ref[3]
    pairs = heard_ref.shape[1]
    windows = pairs // RINGS

    def locate(places):
        owner = lax.shift_right_logical(places * 171, 9)
        z, y, c = lax.shift_right_logical(owner, 4), lax.shift_right_logical(owner, 1) & 7, owner & 1
        off = (jnp.where(core == 0, z, y) - along) & (RINGS - 1)
        source = jnp.full_like(off, -1)
        for n, (_, step) in enumerate(steps):
            source = jnp.where(off == -step % RINGS, n, source)
        mine = (jnp.where(core == 0, y, z) == across) & (source >= 0)
        kind = jnp.where(c == core, 0, 1)
        lanes = lax.broadcasted_iota(jnp.int32, places.shape, 1)
        receiver = lax.shift_right_logical(lanes, windows.bit_length() - 1)
        return mine, ((source * 2 + kind) * CAP + places - owner * CAP) * RINGS + receiver

    def square(n, axis):
        return lax.broadcasted_iota(jnp.int32, (n, n), axis)

    def ones(mask):
        return jnp.where(mask, 1.0, 0.0)

    mine, row = locate(heard_ref[:modes])
    ids = lax.broadcasted_iota(jnp.int32, mine.shape, 0)
    below = ones(square(modes, 0) > square(modes, 1))
    rank = jnp.dot(below, ones(mine), preferred_element_type=F32).astype(jnp.int32)
    rank = jnp.where(mine, rank, -1)
    count = jnp.sum(ones(mine), axis=0, keepdims=True)
    value = (ids * 512 + row - modes * 512).astype(F32)
    for n in range(modes):
        found = jnp.sum(jnp.where(rank == n, value, 0.0), axis=0, keepdims=True)
        out_ref[n:n + 1] = found.astype(jnp.int32) + modes * 512

    mine, row = locate(heard_ref[modes:modes + CAP])
    local = heard_ref[modes + CAP:modes + 2 * CAP] - group * modes
    live = mine & (local >= 0) & (local < modes)
    out_ref[modes:modes + CAP] = jnp.where(live, local * 512 + row, 0)

    first = lax.broadcasted_iota(jnp.int32, (1, pairs), 1)
    flags = []
    for begin, end in parts:
        inside = (first >= begin * windows) & (first < end * windows)
        for n in range(modes // LOT):
            flags.append(ones(inside & (count > n * LOT)))
        for t in range(CAP):
            flags.append(ones(inside & live[t:t + 1]))
    total = len(flags)
    flags = jnp.concatenate(flags + [jnp.zeros((pairs - total, pairs), F32)], axis=0)
    turned = (((1,), (1,)), ((), ()))
    down, over = square(pairs, 0), square(pairs, 1)
    chosen = lax.dot_general(ones(down == over), flags, turned, preferred_element_type=F32)
    order = lax.dot_general(ones(down > over), flags, turned, preferred_element_type=F32)
    order = jnp.where(chosen > 0.5, order, -1.0)
    numbers = (down - pairs).astype(F32)
    lanes = over.astype(F32)
    for n in range(total):
        found = jnp.sum(jnp.where(order[:, n:n + 1] == lanes, numbers, 0.0), axis=0, keepdims=True)
        out_ref[modes + CAP + n:modes + CAP + n + 1] = found.astype(jnp.int32) + pairs
    sums = lax.dot_general(jnp.ones((8, pairs), F32), flags, turned, preferred_element_type=F32)
    last = out_ref.shape[0] - 1
    out_ref[last:last + 1] = sums[:1].astype(jnp.int32)


def lists_kernel(kinds, modes, spot_ref, heard_ref, *refs):
    out_refs, sum_ref = refs[:-1], refs[-1]
    rows = sum_ref.shape[0]
    for (steps, parts, far), out_ref in zip(kinds, out_refs, strict=True):
        sum_ref[...] = sum(heard_ref[r, far * rows:(far + 1) * rows] for r in range(RINGS))
        lists_of(steps, parts, modes, spot_ref, sum_ref, out_ref)


def use_lists(kinds, modes, spot, heard):
    rows = [modes + CAP + len(parts) * (modes // LOT + CAP) + 1 for _, parts, _ in kinds]
    return pl.pallas_call(
        functools.partial(lists_kernel, kinds, modes),
        in_specs=[SMEM, VMEM],
        out_specs=[VMEM] * len(kinds),
        out_shape=[jax.ShapeDtypeStruct((n + -n % 8, heard.shape[2]), jnp.int32) for n in rows],
        scratch_shapes=[pltpu.VMEM((heard.shape[1] // 2, heard.shape[2]), jnp.int32)],
        compiler_params=pltpu.CompilerParams(vmem_limit_bytes=8 * 2**20),
        cost_estimate=pl.CostEstimate(flops=10**7, bytes_accessed=2**18, transcendentals=0),
    )(spot, heard)


def say_kernel(spot_ref, up_ref, down_ref, tri_ref, out_ref):
    windows, modes = up_ref.shape
    shape = (windows, out_ref.shape[1])
    lanes = lax.broadcasted_iota(jnp.int32, shape, 1)
    row = lax.broadcasted_iota(jnp.int32, shape, 0)
    place = jnp.where(lanes == spot_ref[2] * windows + row, 1.0, 0.0)

    def put(values, axis):
        def half(part):
            return lax.dot_general(
                part.astype(F32), place, (((axis,), (0,)), ((), ())), preferred_element_type=F32
            )

        high = lax.shift_right_logical(values, 5)
        return (half(high) * 32.0 + half(values & 31)).astype(jnp.int32)

    up, down, tri = put(up_ref[...], 0), put(down_ref[...], 1), put(tri_ref[...], 1)
    spare = jnp.zeros((out_ref.shape[0] - modes - 2 * CAP, shape[1]), jnp.int32)
    whole = jnp.concatenate([up, down, tri, spare], axis=0)
    out_ref[...] = whole


def say(spot, use_up, use_down, modes_tri):
    windows, modes = use_up.shape
    rows = modes + 2 * CAP
    return pl.pallas_call(
        say_kernel,
        in_specs=[SMEM, VMEM, VMEM, VMEM],
        out_specs=VMEM,
        out_shape=jax.ShapeDtypeStruct((rows + -rows % 8, RINGS * windows), jnp.int32),
        cost_estimate=pl.CostEstimate(flops=10**6, bytes_accessed=2**18, transcendentals=0),
    )(spot, use_up, use_down.T, modes_tri.T)


def over_groups(parts):
    count = len(parts)
    total = parts[0]
    for shift in (2, 1, 3):
        ring = [(i, (i + shift) % count) for i in range(count)]
        total = total + lax.ppermute(parts[shift].astype(LINK), "grp", ring).astype(F32)
    return total


def on_device(
    states, send_slot, window_tier_states, modes_tri, use_up, use_down,
    hamiltonian, coupling, coup_re, coup_im, decay_rate,
):
    width = hamiltonian.shape[0]
    windows, share = window_tier_states.shape[:2]
    modes = coupling.shape[0]
    group = lax.axis_index("grp").astype(jnp.int32)
    index = lax.axis_index("ado").astype(jnp.int32)
    core, z, y = index & 1, index >> 4, (index >> 1) & 7
    along = jnp.where(core == 0, z, y)
    across = jnp.where(core == 0, y, z)

    spot = jnp.stack([core, along, across, group])

    slots = jnp.transpose(send_slot[0, 0]).reshape(-1)
    sib_store = lax.ppermute(states[0, 0], "ado", SIBLING)
    sib_slots = lax.ppermute(slots, "ado", SIBLING)
    said = say(spot, use_up, use_down, modes_tri)
    said = jnp.concatenate([said, lax.ppermute(said, "ado", onward(4))], axis=0)
    heard = lax.all_to_all(
        jnp.broadcast_to(said, (RINGS,) + said.shape), "ado", split_axis=0, concat_axis=0, tiled=True,
        axis_index_groups=DELIVER,
    )
    picked = pick(spot, slots, sib_slots, states[0, 0], sib_store)
    maps_wide = jnp.concatenate([doubled(coupling), jnp.zeros((1, 2 * width, 2 * width), BF16)], axis=0)
    head_cols = lax.dynamic_slice_in_dim(hamiltonian, group * share, share, 1)
    shared = (maps_wide, head_cols, window_tier_states)
    picked, heard, shared = lax.optimization_barrier((picked, heard, shared))

    def send(steps, blocks):
        return [
            block if step == 0 else lax.ppermute(block, "ado", onward(step))
            for (_, step), block in zip(steps, blocks, strict=True)
        ]

    far_states = send(FAR, picked[:len(FAR)])
    near_states = send(NEAR, picked[len(FAR):])
    kinds = ((FAR, ((0, RINGS),), 1), (NEAR, ((0, RINGS),), 0))
    far_lists, near_lists = use_lists(kinds, modes, spot, heard)

    far = terms((0, RINGS, 0), spot, far_lists, coup_re, coup_im, far_states, *shared)
    far, near_lists = lax.optimization_barrier((far, near_lists))
    far = over_groups(far)
    far = lax.ppermute(far.astype(LINK), "ado", onward(4))
    near = over_groups(terms((0, RINGS, 0), spot, near_lists, coup_re, coup_im, near_states, *shared))
    summed = lax.all_to_all(
        (near + far.astype(F32)).astype(LINK), "ado", split_axis=0, concat_axis=0,
        tiled=True, axis_index_groups=DELIVER,
    )

    ham_wide = doubled(hamiltonian)
    right_part = jnp.einsum("wab,bc->wac", window_tier_states, ham_wide, preferred_element_type=F32)
    every_mode = jnp.arange(decay_rate.shape[0], dtype=jnp.int32)
    hits = modes_tri[:, :, None] == every_mode
    damping = jnp.sum(jnp.where(hits, decay_rate, 0.0), axis=(1, 2))
    own = rotate(right_part) + damping[:, None, None] * window_tier_states.astype(F32)
    return STEP_WEIGHT * (jnp.sum(summed.astype(F32), axis=0) - own)


def solution(mesh):
    in_specs = (
        P("grp", "ado", None, None, None),
        P("grp", "ado", None, None),
        P("ado", "grp", None),
        P("ado", None),
        P("ado", "grp"),
        P("ado", None),
        P(),
        P("grp", None, None),
        P("grp"),
        P("grp"),
        P(),
    )
    out_specs = P("ado", "grp", None)
    return jax.shard_map(
        on_device, mesh=mesh, in_specs=in_specs, out_specs=out_specs, check_vma=False
    )
```

```python
import functools

import jax
import jax.numpy as jnp
from jax import lax
from jax.experimental import pallas as pl
from jax.experimental.pallas import tpu as pltpu
from jax.sharding import PartitionSpec as P

STEP_WEIGHT = 0.5
F32 = jnp.float32
BF16 = jnp.bfloat16
LINK = jnp.float16
VMEM = pl.BlockSpec(memory_space=pltpu.VMEM)
SMEM = pl.BlockSpec(memory_space=pltpu.SMEM)
HBM = pl.BlockSpec(memory_space=pltpu.HBM)


def doubled(matrices):
    empty = jnp.zeros_like(matrices)
    upper_half = jnp.concatenate([matrices, empty], axis=-1)
    lower_half = jnp.concatenate([empty, matrices], axis=-1)
    return jnp.concatenate([upper_half, lower_half], axis=-2)


def rotate(parts):
    width = parts.shape[-1] // 2
    return jnp.concatenate([parts[..., width:], -parts[..., :width]], axis=-1)


RINGS = 8
CAP = 3
LOT = 4
SPAN = 2 * CAP * RINGS
SENDS = ((1, (-3, 1)), (-1, (3, -1)), (2, (2,)), (-2, (-2,)), (0, (4, 0)))
FAR = tuple((n, group.index((step + 4) % 8 - 8 * ((step + 4) % 8 > 4)), step) for n, (step, group) in enumerate(SENDS) if len(group) == 2)
NEAR = tuple((n, group.index(step), step) for n, (step, group) in enumerate(SENDS))
SIBLING = [(i, i ^ 1) for i in range(2 * RINGS * RINGS)]


def device(core, along, across):
    along, across = along % RINGS, across % RINGS
    return along * 16 + across * 2 if core == 0 else across * 16 + along * 2 + 1


def onward(step):
    return [
        (device(c, a, b), device(c, a + step, b)) for c in range(2) for a in range(RINGS) for b in range(RINGS)
    ]


DELIVER = [[device(c, a, b) for b in range(RINGS)] for c in range(2) for a in range(RINGS)]


def pick_kernel(spot_ref, own_slot, sib_slot, own_ref, sib_hbm, *refs):
    out_refs, (sib_ref, held, sem, sems) = refs[:-4], refs[-4:]
    copy = pltpu.make_async_copy(sib_hbm, sib_ref, sem)
    copy.start()
    core, along = spot_ref[0], spot_ref[1]
    far = jnp.where(core == 0, 16, 2)
    near = jnp.where(core == 0, 2, 16)
    count = own_slot.shape[0] // CAP

    def fill(ahead, place, kind):
        slots, store = ((own_slot, own_ref), (sib_slot, sib_ref))[kind]
        first = lax.rem(along + ahead + RINGS, RINGS) * far + core
        for c in range(CAP):
            for r in range(RINGS):
                slot = slots[c * count + first + r * near]
                held[place * SPAN + kind * CAP * RINGS + c * RINGS + r] = store[jnp.maximum(slot, 0)]

    aheads = [ahead for _, group in SENDS for ahead in group]
    for place, ahead in enumerate(aheads):
        fill(ahead, place, 0)
    copy.wait()
    copies, place = [], 0
    for n, ((_, group), out_ref) in enumerate(zip(SENDS, out_refs, strict=True)):
        for ahead in group:
            fill(ahead, place, 1)
            place += 1
        begin = (place - len(group)) * SPAN
        copies.append(pltpu.make_async_copy(held.at[pl.ds(begin, len(group) * SPAN)], out_ref, sems.at[n]))
        copies[-1].start()
    for copy in copies:
        copy.wait()


def pick(spot, own_slots, sib_slots, own, sib):
    tile = own.shape[1:]
    total = sum(len(group) for _, group in SENDS)
    return pl.pallas_call(
        pick_kernel,
        in_specs=[SMEM, SMEM, SMEM, VMEM, HBM],
        out_specs=[HBM] * len(SENDS),
        out_shape=[pltpu.HBM((len(group) * SPAN,) + tile, own.dtype) for _, group in SENDS],
        scratch_shapes=[
            pltpu.VMEM(own.shape, own.dtype),
            pltpu.VMEM((total * SPAN,) + tile, own.dtype),
            pltpu.SemaphoreType.DMA,
            pltpu.SemaphoreType.DMA((len(SENDS),)),
        ],
        compiler_params=pltpu.CompilerParams(vmem_limit_bytes=24 * 2**20),
        cost_estimate=pl.CostEstimate(flops=0, bytes_accessed=10 * 2**20, transcendentals=0),
    )(spot, own_slots, sib_slots, own, sib)


def terms_kernel(sources, modes, windows, part, spot_ref, list_ref, re_ref, im_ref, *refs):
    count = len(sources)
    state_refs, (wide_ref, ham_ref, rho_ref) = refs[:count], refs[count:count + 3]
    out_refs, (flat, acc, sems) = refs[count + 3:-3], refs[-3:]
    here, group = spot_ref[2], spot_ref[3]
    share = rho_ref.shape[1]
    width = ham_ref.shape[0]
    pairs = RINGS * windows
    blocks = width // share
    begin, end, slot = part
    levels = modes // LOT + CAP
    downs, extra, counts = modes, modes + CAP + slot * levels, list_ref.shape[0] - 1

    copies = [
        pltpu.make_async_copy(
            state_refs[n].at[pl.ds(place * SPAN, SPAN)], flat.at[pl.ds(n * SPAN, SPAN)], sems.at[n]
        )
        for n, (_, place, _) in enumerate(sources)
    ]
    for copy in copies:
        copy.start()
    for copy in copies:
        copy.wait()

    def lot(pair, base):
        entries = [list_ref[base + n, pair] for n in range(LOT)]
        maps = [lax.shift_right_logical(e, 9) for e in entries]
        tiles = [flat[e & 511] for e in entries]
        rows = [
            wide_ref[maps[n], :width, :] + wide_ref[maps[n + 1], width:, :] for n in range(0, LOT, 2)
        ]
        left = jnp.dot(
            jnp.concatenate(rows, axis=1), jnp.concatenate(tiles, axis=0), preferred_element_type=F32
        )
        right = jnp.dot(
            jnp.concatenate(tiles, axis=1),
            jnp.concatenate([wide_ref[m] for m in maps], axis=0),
            preferred_element_type=F32,
        )
        return rotate(left - right)

    together = 16

    def first(index, carry):
        for j in range(together):
            pair = index * together + j
            acc[pair] = lot(pair, 0)
        return carry

    lax.fori_loop(begin * windows // together, end * windows // together, first, 0)

    def listed(level, work):
        def some(index, carry):
            found = [list_ref[extra + level, index * 4 + j] for j in range(4)]
            values = [work(jnp.minimum(pair, pairs - 1)) for pair in found]
            for pair, value in zip(found, values, strict=True):
                acc[pair] += value
            return carry

        lax.fori_loop(0, lax.shift_right_logical(list_ref[counts, slot * levels + level] + 3, 2), some, 0)

    def more(level, carry):
        listed(level, lambda pair: lot(pair, level * LOT))
        return carry

    lax.fori_loop(1, modes // LOT, more, 0)

    def lower(t, carry):
        def work(pair):
            entry = list_ref[downs + t, pair]
            mode = lax.shift_right_logical(entry, 9)
            state = flat[entry & 511]
            wide = wide_ref[mode]
            ahead = jnp.dot(wide[:width, :width], state, preferred_element_type=F32)
            after = jnp.dot(state, wide, preferred_element_type=F32)
            return re_ref[mode] * rotate(ahead - after) + im_ref[mode] * (ahead + after)

        listed(modes // LOT + t, work)
        return carry

    lax.fori_loop(0, CAP, lower, 0)

    if sources is NEAR:

        for w in range(windows):
            acc[here * windows + w] += rotate(
                jnp.dot(ham_ref[...], rho_ref[w], preferred_element_type=F32)
            )

    def leave(r, carry):
        for w in range(windows):
            for shift, out_ref in enumerate(out_refs):
                block = lax.rem(group + shift, blocks) * share
                out_ref[r - begin, w] = acc[r * windows + w, pl.ds(pl.multiple_of(block, share), share), :]
        return carry

    lax.fori_loop(begin, end, leave, 0)


def terms(sources, part, spot, lists, coup_re, coup_im, states, maps_wide, head_cols, rho):
    modes = maps_wide.shape[0] - 1
    windows, share, lanes = rho.shape
    width = head_cols.shape[0]
    return pl.pallas_call(
        functools.partial(terms_kernel, sources, modes, windows, part),
        in_specs=[SMEM] * 4 + [HBM] * len(sources) + [VMEM] * 3,
        out_specs=[VMEM] * (width // share),
        out_shape=[jax.ShapeDtypeStruct((part[1] - part[0], windows, share, lanes), F32)] * (width // share),
        scratch_shapes=[
            pltpu.VMEM((len(sources) * SPAN, width, lanes), BF16),
            pltpu.VMEM((RINGS * windows + 1, width, lanes), F32),
            pltpu.SemaphoreType.DMA((len(sources),)),
        ],
        compiler_params=pltpu.CompilerParams(vmem_limit_bytes=28 * 2**20),
        cost_estimate=pl.CostEstimate(flops=10**9, bytes_accessed=10 * 2**20, transcendentals=0),
    )(spot, lists, coup_re, coup_im, *[states[n] for n, _, _ in sources], maps_wide, head_cols, rho)


def lists_of(steps, parts, modes, spot_ref, heard_ref, out_ref):
    core, along, across, group = spot_ref[0], spot_ref[1], spot_ref[2], spot_ref[3]
    pairs = heard_ref.shape[1]
    windows = pairs // RINGS

    def locate(places):
        owner = lax.shift_right_logical(places * 171, 9)
        z, y, c = lax.shift_right_logical(owner, 4), lax.shift_right_logical(owner, 1) & 7, owner & 1
        off = (jnp.where(core == 0, z, y) - along) & (RINGS - 1)
        source = jnp.full_like(off, -1)
        for n, (_, _, step) in enumerate(steps):
            source = jnp.where(off == -step % RINGS, n, source)
        mine = (jnp.where(core == 0, y, z) == across) & (source >= 0)
        kind = jnp.where(c == core, 0, 1)
        lanes = lax.broadcasted_iota(jnp.int32, places.shape, 1)
        receiver = lax.shift_right_logical(lanes, windows.bit_length() - 1)
        return mine, ((source * 2 + kind) * CAP + places - owner * CAP) * RINGS + receiver

    def square(n, axis):
        return lax.broadcasted_iota(jnp.int32, (n, n), axis)

    def ones(mask):
        return jnp.where(mask, 1.0, 0.0)

    mine, row = locate(heard_ref[:modes])
    ids = lax.broadcasted_iota(jnp.int32, mine.shape, 0)
    below = ones(square(modes, 0) > square(modes, 1))
    rank = jnp.dot(below, ones(mine), preferred_element_type=F32).astype(jnp.int32)
    rank = jnp.where(mine, rank, -1)
    count = jnp.sum(ones(mine), axis=0, keepdims=True)
    value = (ids * 512 + row - modes * 512).astype(F32)
    for n in range(modes):
        found = jnp.sum(jnp.where(rank == n, value, 0.0), axis=0, keepdims=True)
        out_ref[n:n + 1] = found.astype(jnp.int32) + modes * 512

    mine, row = locate(heard_ref[modes:modes + CAP])
    local = heard_ref[modes + CAP:modes + 2 * CAP] - group * modes
    live = mine & (local >= 0) & (local < modes)
    out_ref[modes:modes + CAP] = jnp.where(live, local * 512 + row, 0)

    first = lax.broadcasted_iota(jnp.int32, (1, pairs), 1)
    flags = []
    for begin, end in parts:
        inside = (first >= begin * windows) & (first < end * windows)
        for n in range(modes // LOT):
            flags.append(ones(inside & (count > n * LOT)))
        for t in range(CAP):
            flags.append(ones(inside & live[t:t + 1]))
    total = len(flags)
    flags = jnp.concatenate(flags + [jnp.zeros((pairs - total, pairs), F32)], axis=0)
    turned = (((1,), (1,)), ((), ()))
    down, over = square(pairs, 0), square(pairs, 1)
    chosen = lax.dot_general(ones(down == over), flags, turned, preferred_element_type=F32)
    order = lax.dot_general(ones(down > over), flags, turned, preferred_element_type=F32)
    order = jnp.where(chosen > 0.5, order, -1.0)
    numbers = (down - pairs).astype(F32)
    lanes = over.astype(F32)
    for n in range(total):
        found = jnp.sum(jnp.where(order[:, n:n + 1] == lanes, numbers, 0.0), axis=0, keepdims=True)
        out_ref[modes + CAP + n:modes + CAP + n + 1] = found.astype(jnp.int32) + pairs
    sums = lax.dot_general(jnp.ones((8, pairs), F32), flags, turned, preferred_element_type=F32)
    last = out_ref.shape[0] - 1
    out_ref[last:last + 1] = sums[:1].astype(jnp.int32)


def lists_kernel(kinds, modes, spot_ref, heard_ref, *refs):
    out_refs, sum_ref = refs[:-1], refs[-1]
    rows = sum_ref.shape[0]
    for (steps, parts, far), out_ref in zip(kinds, out_refs, strict=True):
        sum_ref[...] = sum(heard_ref[r, far * rows:(far + 1) * rows] for r in range(RINGS))
        lists_of(steps, parts, modes, spot_ref, sum_ref, out_ref)


def use_lists(kinds, modes, spot, heard):
    rows = [modes + CAP + len(parts) * (modes // LOT + CAP) + 1 for _, parts, _ in kinds]
    return pl.pallas_call(
        functools.partial(lists_kernel, kinds, modes),
        in_specs=[SMEM, VMEM],
        out_specs=[VMEM] * len(kinds),
        out_shape=[jax.ShapeDtypeStruct((n + -n % 8, heard.shape[2]), jnp.int32) for n in rows],
        scratch_shapes=[pltpu.VMEM((heard.shape[1] // 2, heard.shape[2]), jnp.int32)],
        compiler_params=pltpu.CompilerParams(vmem_limit_bytes=8 * 2**20),
        cost_estimate=pl.CostEstimate(flops=10**7, bytes_accessed=2**18, transcendentals=0),
    )(spot, heard)


def say_kernel(spot_ref, up_ref, down_ref, tri_ref, out_ref):
    windows, modes = up_ref.shape
    shape = (windows, out_ref.shape[1])
    lanes = lax.broadcasted_iota(jnp.int32, shape, 1)
    row = lax.broadcasted_iota(jnp.int32, shape, 0)
    place = jnp.where(lanes == spot_ref[2] * windows + row, 1.0, 0.0)

    def put(values, axis):
        def half(part):
            return lax.dot_general(
                part.astype(F32), place, (((axis,), (0,)), ((), ())), preferred_element_type=F32
            )

        high = lax.shift_right_logical(values, 5)
        return (half(high) * 32.0 + half(values & 31)).astype(jnp.int32)

    up, down, tri = put(up_ref[...], 0), put(down_ref[...], 1), put(tri_ref[...], 1)
    spare = jnp.zeros((out_ref.shape[0] - modes - 2 * CAP, shape[1]), jnp.int32)
    whole = jnp.concatenate([up, down, tri, spare], axis=0)
    out_ref[...] = whole


def say(spot, use_up, use_down, modes_tri):
    windows, modes = use_up.shape
    rows = modes + 2 * CAP
    return pl.pallas_call(
        say_kernel,
        in_specs=[SMEM, VMEM, VMEM, VMEM],
        out_specs=VMEM,
        out_shape=jax.ShapeDtypeStruct((rows + -rows % 8, RINGS * windows), jnp.int32),
        cost_estimate=pl.CostEstimate(flops=10**6, bytes_accessed=2**18, transcendentals=0),
    )(spot, use_up, use_down.T, modes_tri.T)


def over_groups(parts):
    count = len(parts)
    total = parts[0]
    for shift in (2, 1, 3):
        ring = [(i, (i + shift) % count) for i in range(count)]
        total = total + lax.ppermute(parts[shift].astype(LINK), "grp", ring).astype(F32)
    return total


def on_device(
    states, send_slot, window_tier_states, modes_tri, use_up, use_down,
    hamiltonian, coupling, coup_re, coup_im, decay_rate,
):
    width = hamiltonian.shape[0]
    windows, share = window_tier_states.shape[:2]
    modes = coupling.shape[0]
    group = lax.axis_index("grp").astype(jnp.int32)
    index = lax.axis_index("ado").astype(jnp.int32)
    core, z, y = index & 1, index >> 4, (index >> 1) & 7
    along = jnp.where(core == 0, z, y)
    across = jnp.where(core == 0, y, z)

    spot = jnp.stack([core, along, across, group])

    slots = jnp.transpose(send_slot[0, 0]).reshape(-1)
    sib_store = lax.ppermute(states[0, 0], "ado", SIBLING)
    sib_slots = lax.ppermute(slots, "ado", SIBLING)
    slots, use_up = lax.optimization_barrier((slots, use_up))
    said = say(spot, use_up, use_down, modes_tri)
    said = jnp.concatenate([said, lax.ppermute(said, "ado", onward(4))], axis=0)
    heard = lax.all_to_all(
        jnp.broadcast_to(said, (RINGS,) + said.shape), "ado", split_axis=0, concat_axis=0, tiled=True,
        axis_index_groups=DELIVER,
    )
    picked = pick(spot, slots, sib_slots, states[0, 0], sib_store)
    maps_wide = jnp.concatenate([doubled(coupling), jnp.zeros((1, 2 * width, 2 * width), BF16)], axis=0)
    head_cols = lax.dynamic_slice_in_dim(hamiltonian, group * share, share, 1)
    shared = (maps_wide, head_cols, window_tier_states)
    picked, heard, shared = lax.optimization_barrier((picked, heard, shared))

    sent = [
        block if step == 0 else lax.ppermute(block, "ado", onward(step))
        for (step, _), block in zip(SENDS, picked, strict=True)
    ]
    kinds = ((FAR, ((0, RINGS),), 1), (NEAR, ((0, RINGS),), 0))
    far_lists, near_lists = use_lists(kinds, modes, spot, heard)

    far = terms(FAR, (0, RINGS, 0), spot, far_lists, coup_re, coup_im, sent, *shared)
    far, near_lists = lax.optimization_barrier((far, near_lists))
    far = over_groups(far)
    far = lax.ppermute(far.astype(LINK), "ado", onward(4))
    near = over_groups(terms(NEAR, (0, RINGS, 0), spot, near_lists, coup_re, coup_im, sent, *shared))
    summed = lax.all_to_all(
        (near + far.astype(F32)).astype(LINK), "ado", split_axis=0, concat_axis=0,
        tiled=True, axis_index_groups=DELIVER,
    )

    ham_wide = doubled(hamiltonian)
    right_part = jnp.einsum("wab,bc->wac", window_tier_states, ham_wide, preferred_element_type=F32)
    every_mode = jnp.arange(decay_rate.shape[0], dtype=jnp.int32)
    hits = modes_tri[:, :, None] == every_mode
    damping = jnp.sum(jnp.where(hits, decay_rate, 0.0), axis=(1, 2))
    own = rotate(right_part) + damping[:, None, None] * window_tier_states.astype(F32)
    return STEP_WEIGHT * (jnp.sum(summed.astype(F32), axis=0) - own)


def solution(mesh):
    in_specs = (
        P("grp", "ado", None, None, None),
        P("grp", "ado", None, None),
        P("ado", "grp", None),
        P("ado", None),
        P("ado", "grp"),
        P("ado", None),
        P(),
        P("grp", None, None),
        P("grp"),
        P("grp"),
        P(),
    )
    out_specs = P("ado", "grp", None)
    return jax.shard_map(
        on_device, mesh=mesh, in_specs=in_specs, out_specs=out_specs, check_vma=False
    )
```

```python
import functools

import jax
import jax.numpy as jnp
from jax import lax
from jax.experimental import pallas as pl
from jax.experimental.pallas import tpu as pltpu
from jax.sharding import PartitionSpec as P

STEP_WEIGHT = 0.5
F32 = jnp.float32
BF16 = jnp.bfloat16
LINK = jnp.float16
VMEM = pl.BlockSpec(memory_space=pltpu.VMEM)
SMEM = pl.BlockSpec(memory_space=pltpu.SMEM)
HBM = pl.BlockSpec(memory_space=pltpu.HBM)


def doubled(matrices):
    empty = jnp.zeros_like(matrices)
    upper_half = jnp.concatenate([matrices, empty], axis=-1)
    lower_half = jnp.concatenate([empty, matrices], axis=-1)
    return jnp.concatenate([upper_half, lower_half], axis=-2)


def rotate(parts):
    width = parts.shape[-1] // 2
    return jnp.concatenate([parts[..., width:], -parts[..., :width]], axis=-1)


RINGS = 8
CAP = 3
LOT = 4
SPAN = 2 * CAP * RINGS
SENDS = ((1, (-3,)), (-1, (3,)), (1, (1,)), (-1, (-1,)), (2, (2,)), (-2, (-2,)), (0, (4, 0)))
FAR = ((0, 0, 1), (1, 0, -1), (6, 0, 0))
NEAR = ((2, 0, 1), (3, 0, -1), (4, 0, 2), (5, 0, -2), (6, 1, 0))
SIBLING = [(i, i ^ 1) for i in range(2 * RINGS * RINGS)]


def device(core, along, across):
    along, across = along % RINGS, across % RINGS
    return along * 16 + across * 2 if core == 0 else across * 16 + along * 2 + 1


def onward(step):
    return [
        (device(c, a, b), device(c, a + step, b)) for c in range(2) for a in range(RINGS) for b in range(RINGS)
    ]


DELIVER = [[device(c, a, b) for b in range(RINGS)] for c in range(2) for a in range(RINGS)]
REDUCE = [
    [g * 2 * RINGS * RINGS + member for g in range(4) for member in members] for members in DELIVER
]


def pick_kernel(spot_ref, own_slot, sib_slot, own_ref, sib_hbm, *refs):
    out_refs, (sib_ref, held, sem, sems) = refs[:-4], refs[-4:]
    copy = pltpu.make_async_copy(sib_hbm, sib_ref, sem)
    copy.start()
    core, along = spot_ref[0], spot_ref[1]
    far = jnp.where(core == 0, 16, 2)
    near = jnp.where(core == 0, 2, 16)
    count = own_slot.shape[0] // CAP

    def fill(ahead, place, kind):
        slots, store = ((own_slot, own_ref), (sib_slot, sib_ref))[kind]
        first = lax.rem(along + ahead + RINGS, RINGS) * far + core
        for c in range(CAP):
            for r in range(RINGS):
                slot = slots[c * count + first + r * near]
                held[place * SPAN + kind * CAP * RINGS + c * RINGS + r] = store[jnp.maximum(slot, 0)]

    aheads = [ahead for _, group in SENDS for ahead in group]
    for place, ahead in enumerate(aheads):
        fill(ahead, place, 0)
    copy.wait()
    copies, place = [], 0
    for n, ((_, group), out_ref) in enumerate(zip(SENDS, out_refs, strict=True)):
        for ahead in group:
            fill(ahead, place, 1)
            place += 1
        begin = (place - len(group)) * SPAN
        copies.append(pltpu.make_async_copy(held.at[pl.ds(begin, len(group) * SPAN)], out_ref, sems.at[n]))
        copies[-1].start()
    for copy in copies:
        copy.wait()


def pick(spot, own_slots, sib_slots, own, sib):
    tile = own.shape[1:]
    total = sum(len(group) for _, group in SENDS)
    return pl.pallas_call(
        pick_kernel,
        in_specs=[SMEM, SMEM, SMEM, VMEM, HBM],
        out_specs=[HBM] * len(SENDS),
        out_shape=[pltpu.HBM((len(group) * SPAN,) + tile, own.dtype) for _, group in SENDS],
        scratch_shapes=[
            pltpu.VMEM(own.shape, own.dtype),
            pltpu.VMEM((total * SPAN,) + tile, own.dtype),
            pltpu.SemaphoreType.DMA,
            pltpu.SemaphoreType.DMA((len(SENDS),)),
        ],
        compiler_params=pltpu.CompilerParams(vmem_limit_bytes=24 * 2**20),
        cost_estimate=pl.CostEstimate(flops=0, bytes_accessed=10 * 2**20, transcendentals=0),
    )(spot, own_slots, sib_slots, own, sib)


def terms_kernel(sources, modes, windows, part, spot_ref, list_ref, re_ref, im_ref, *refs):
    count = len(sources)
    state_refs, (wide_ref, ham_ref, rho_ref) = refs[:count], refs[count:count + 3]
    out_ref, flat, acc, sems = refs[count + 3:]
    here = spot_ref[2]
    share = rho_ref.shape[1]
    width = ham_ref.shape[0]
    pairs = RINGS * windows
    blocks = width // share
    begin, end, slot = part
    levels = modes // LOT + CAP
    downs, extra, counts = modes, modes + CAP + slot * levels, list_ref.shape[0] - 1

    copies = [
        pltpu.make_async_copy(
            state_refs[n].at[pl.ds(place * SPAN, SPAN)], flat.at[pl.ds(n * SPAN, SPAN)], sems.at[n]
        )
        for n, (_, place, _) in enumerate(sources)
    ]
    for copy in copies:
        copy.start()
    for copy in copies:
        copy.wait()

    def lot(pair, base):
        entries = [list_ref[base + n, pair] for n in range(LOT)]
        maps = [lax.shift_right_logical(e, 9) for e in entries]
        tiles = [flat[e & 511] for e in entries]
        rows = [
            wide_ref[maps[n], :width, :] + wide_ref[maps[n + 1], width:, :] for n in range(0, LOT, 2)
        ]
        left = jnp.dot(
            jnp.concatenate(rows, axis=1), jnp.concatenate(tiles, axis=0), preferred_element_type=F32
        )
        right = jnp.dot(
            jnp.concatenate(tiles, axis=1),
            jnp.concatenate([wide_ref[m] for m in maps], axis=0),
            preferred_element_type=F32,
        )
        return rotate(left - right)

    together = 16

    def first(index, carry):
        for j in range(together):
            pair = index * together + j
            acc[pair] = lot(pair, 0)
        return carry

    lax.fori_loop(begin * windows // together, end * windows // together, first, 0)

    def listed(level, work):
        def some(index, carry):
            found = [list_ref[extra + level, index * 4 + j] for j in range(4)]
            values = [work(jnp.minimum(pair, pairs - 1)) for pair in found]
            for pair, value in zip(found, values, strict=True):
                acc[pair] += value
            return carry

        lax.fori_loop(0, lax.shift_right_logical(list_ref[counts, slot * levels + level] + 3, 2), some, 0)

    def more(level, carry):
        listed(level, lambda pair: lot(pair, level * LOT))
        return carry

    lax.fori_loop(1, modes // LOT, more, 0)

    def lower(t, carry):
        def work(pair):
            entry = list_ref[downs + t, pair]
            mode = lax.shift_right_logical(entry, 9)
            state = flat[entry & 511]
            wide = wide_ref[mode]
            ahead = jnp.dot(wide[:width, :width], state, preferred_element_type=F32)
            after = jnp.dot(state, wide, preferred_element_type=F32)
            return re_ref[mode] * rotate(ahead - after) + im_ref[mode] * (ahead + after)

        listed(modes // LOT + t, work)
        return carry

    lax.fori_loop(0, CAP, lower, 0)

    if sources is NEAR:

        for w in range(windows):
            acc[here * windows + w] += rotate(
                jnp.dot(ham_ref[...], rho_ref[w], preferred_element_type=F32)
            )

    def leave(r, carry):
        for w in range(windows):
            value = acc[r * windows + w]
            for b in range(blocks):
                out_ref[b, r - begin, w] = value[b * share:(b + 1) * share]
        return carry

    lax.fori_loop(begin, end, leave, 0)


def terms(sources, part, spot, lists, coup_re, coup_im, states, maps_wide, head_cols, rho):
    modes = maps_wide.shape[0] - 1
    windows, share, lanes = rho.shape
    width = head_cols.shape[0]
    return pl.pallas_call(
        functools.partial(terms_kernel, sources, modes, windows, part),
        in_specs=[SMEM] * 4 + [HBM] * len(sources) + [VMEM] * 3,
        out_specs=VMEM,
        out_shape=jax.ShapeDtypeStruct((width // share, part[1] - part[0], windows, share, lanes), F32),
        scratch_shapes=[
            pltpu.VMEM((len(sources) * SPAN, width, lanes), BF16),
            pltpu.VMEM((RINGS * windows + 1, width, lanes), F32),
            pltpu.SemaphoreType.DMA((len(sources),)),
        ],
        compiler_params=pltpu.CompilerParams(vmem_limit_bytes=28 * 2**20),
        cost_estimate=pl.CostEstimate(flops=10**9, bytes_accessed=10 * 2**20, transcendentals=0),
    )(spot, lists, coup_re, coup_im, *[states[n] for n, _, _ in sources], maps_wide, head_cols, rho)


def lists_of(steps, parts, modes, spot_ref, heard_ref, out_ref):
    core, along, across, group = spot_ref[0], spot_ref[1], spot_ref[2], spot_ref[3]
    pairs = heard_ref.shape[1]
    windows = pairs // RINGS

    def locate(places):
        owner = lax.shift_right_logical(places * 171, 9)
        z, y, c = lax.shift_right_logical(owner, 4), lax.shift_right_logical(owner, 1) & 7, owner & 1
        off = (jnp.where(core == 0, z, y) - along) & (RINGS - 1)
        source = jnp.full_like(off, -1)
        for n, (_, _, step) in enumerate(steps):
            source = jnp.where(off == -step % RINGS, n, source)
        mine = (jnp.where(core == 0, y, z) == across) & (source >= 0)
        kind = jnp.where(c == core, 0, 1)
        lanes = lax.broadcasted_iota(jnp.int32, places.shape, 1)
        receiver = lax.shift_right_logical(lanes, windows.bit_length() - 1)
        return mine, ((source * 2 + kind) * CAP + places - owner * CAP) * RINGS + receiver

    def square(n, axis):
        return lax.broadcasted_iota(jnp.int32, (n, n), axis)

    def ones(mask):
        return jnp.where(mask, 1.0, 0.0)

    mine, row = locate(heard_ref[:modes])
    ids = lax.broadcasted_iota(jnp.int32, mine.shape, 0)
    below = ones(square(modes, 0) > square(modes, 1))
    rank = jnp.dot(below, ones(mine), preferred_element_type=F32).astype(jnp.int32)
    rank = jnp.where(mine, rank, -1)
    count = jnp.sum(ones(mine), axis=0, keepdims=True)
    value = (ids * 512 + row - modes * 512).astype(F32)
    for n in range(modes):
        found = jnp.sum(jnp.where(rank == n, value, 0.0), axis=0, keepdims=True)
        out_ref[n:n + 1] = found.astype(jnp.int32) + modes * 512

    mine, row = locate(heard_ref[modes:modes + CAP])
    local = heard_ref[modes + CAP:modes + 2 * CAP] - group * modes
    live = mine & (local >= 0) & (local < modes)
    out_ref[modes:modes + CAP] = jnp.where(live, local * 512 + row, 0)

    first = lax.broadcasted_iota(jnp.int32, (1, pairs), 1)
    flags = []
    for begin, end in parts:
        inside = (first >= begin * windows) & (first < end * windows)
        for n in range(modes // LOT):
            flags.append(ones(inside & (count > n * LOT)))
        for t in range(CAP):
            flags.append(ones(inside & live[t:t + 1]))
    total = len(flags)
    flags = jnp.concatenate(flags + [jnp.zeros((pairs - total, pairs), F32)], axis=0)
    turned = (((1,), (1,)), ((), ()))
    down, over = square(pairs, 0), square(pairs, 1)
    chosen = lax.dot_general(ones(down == over), flags, turned, preferred_element_type=F32)
    order = lax.dot_general(ones(down > over), flags, turned, preferred_element_type=F32)
    order = jnp.where(chosen > 0.5, order, -1.0)
    numbers = (down - pairs).astype(F32)
    lanes = over.astype(F32)
    for n in range(total):
        found = jnp.sum(jnp.where(order[:, n:n + 1] == lanes, numbers, 0.0), axis=0, keepdims=True)
        out_ref[modes + CAP + n:modes + CAP + n + 1] = found.astype(jnp.int32) + pairs
    sums = lax.dot_general(jnp.ones((8, pairs), F32), flags, turned, preferred_element_type=F32)
    last = out_ref.shape[0] - 1
    out_ref[last:last + 1] = sums[:1].astype(jnp.int32)


def lists_kernel(kinds, modes, spot_ref, heard_ref, *refs):
    out_refs, sum_ref = refs[:-1], refs[-1]
    rows = sum_ref.shape[0]
    for (steps, parts, far), out_ref in zip(kinds, out_refs, strict=True):
        sum_ref[...] = sum(heard_ref[r, far * rows:(far + 1) * rows] for r in range(RINGS))
        lists_of(steps, parts, modes, spot_ref, sum_ref, out_ref)


def use_lists(kinds, modes, spot, heard):
    rows = [modes + CAP + len(parts) * (modes // LOT + CAP) + 1 for _, parts, _ in kinds]
    return pl.pallas_call(
        functools.partial(lists_kernel, kinds, modes),
        in_specs=[SMEM, VMEM],
        out_specs=[VMEM] * len(kinds),
        out_shape=[jax.ShapeDtypeStruct((n + -n % 8, heard.shape[2]), jnp.int32) for n in rows],
        scratch_shapes=[pltpu.VMEM((heard.shape[1] // 2, heard.shape[2]), jnp.int32)],
        compiler_params=pltpu.CompilerParams(vmem_limit_bytes=8 * 2**20),
        cost_estimate=pl.CostEstimate(flops=10**7, bytes_accessed=2**18, transcendentals=0),
    )(spot, heard)


def say_kernel(spot_ref, up_ref, down_ref, tri_ref, out_ref):
    windows, modes = up_ref.shape
    shape = (windows, out_ref.shape[1])
    lanes = lax.broadcasted_iota(jnp.int32, shape, 1)
    row = lax.broadcasted_iota(jnp.int32, shape, 0)
    place = jnp.where(lanes == spot_ref[2] * windows + row, 1.0, 0.0)

    def put(values, axis):
        def half(part):
            return lax.dot_general(
                part.astype(F32), place, (((axis,), (0,)), ((), ())), preferred_element_type=F32
            )

        high = lax.shift_right_logical(values, 5)
        return (half(high) * 32.0 + half(values & 31)).astype(jnp.int32)

    up, down, tri = put(up_ref[...], 0), put(down_ref[...], 1), put(tri_ref[...], 1)
    spare = jnp.zeros((out_ref.shape[0] - modes - 2 * CAP, shape[1]), jnp.int32)
    whole = jnp.concatenate([up, down, tri, spare], axis=0)
    out_ref[...] = whole


def say(spot, use_up, use_down, modes_tri):
    windows, modes = use_up.shape
    rows = modes + 2 * CAP
    return pl.pallas_call(
        say_kernel,
        in_specs=[SMEM, VMEM, VMEM, VMEM],
        out_specs=VMEM,
        out_shape=jax.ShapeDtypeStruct((rows + -rows % 8, RINGS * windows), jnp.int32),
        cost_estimate=pl.CostEstimate(flops=10**6, bytes_accessed=2**18, transcendentals=0),
    )(spot, use_up, use_down.T, modes_tri.T)


def reduced(parts):
    parts = parts.reshape((-1,) + parts.shape[2:]).astype(LINK)
    parts = lax.all_to_all(
        parts, ("grp", "ado"), split_axis=0, concat_axis=0, tiled=True, axis_index_groups=REDUCE
    )
    return jnp.sum(parts.astype(F32), axis=0)


def on_device(
    states, send_slot, window_tier_states, modes_tri, use_up, use_down,
    hamiltonian, coupling, coup_re, coup_im, decay_rate,
):
    width = hamiltonian.shape[0]
    windows, share = window_tier_states.shape[:2]
    modes = coupling.shape[0]
    group = lax.axis_index("grp").astype(jnp.int32)
    index = lax.axis_index("ado").astype(jnp.int32)
    core, z, y = index & 1, index >> 4, (index >> 1) & 7
    along = jnp.where(core == 0, z, y)
    across = jnp.where(core == 0, y, z)

    spot = jnp.stack([core, along, across, group])

    slots = jnp.transpose(send_slot[0, 0]).reshape(-1)
    sib_store = lax.ppermute(states[0, 0], "ado", SIBLING)
    sib_slots = lax.ppermute(slots, "ado", SIBLING)
    slots, use_up = lax.optimization_barrier((slots, use_up))
    said = say(spot, use_up, use_down, modes_tri)
    said = jnp.concatenate([said, lax.ppermute(said, "ado", onward(4))], axis=0)
    heard = lax.all_to_all(
        jnp.broadcast_to(said, (RINGS,) + said.shape), "ado", split_axis=0, concat_axis=0, tiled=True,
        axis_index_groups=DELIVER,
    )
    picked = pick(spot, slots, sib_slots, states[0, 0], sib_store)
    maps_wide = jnp.concatenate([doubled(coupling), jnp.zeros((1, 2 * width, 2 * width), BF16)], axis=0)
    head_cols = lax.dynamic_slice_in_dim(hamiltonian, group * share, share, 1)
    shared = (maps_wide, head_cols, window_tier_states)
    picked, heard, shared = lax.optimization_barrier((picked, heard, shared))

    sent = [
        block if step == 0 else lax.ppermute(block, "ado", onward(step))
        for (step, _), block in zip(SENDS, picked, strict=True)
    ]
    kinds = ((FAR, ((0, RINGS),), 1), (NEAR, ((0, RINGS),), 0))
    far_lists, near_lists = use_lists(kinds, modes, spot, heard)

    far = terms(FAR, (0, RINGS, 0), spot, far_lists, coup_re, coup_im, sent, *shared)
    far, near_lists = lax.optimization_barrier((far, near_lists))
    far = lax.ppermute(reduced(far), "ado", onward(4))
    near = reduced(terms(NEAR, (0, RINGS, 0), spot, near_lists, coup_re, coup_im, sent, *shared))

    ham_wide = doubled(hamiltonian)
    right_part = jnp.einsum("wab,bc->wac", window_tier_states, ham_wide, preferred_element_type=F32)
    every_mode = jnp.arange(decay_rate.shape[0], dtype=jnp.int32)
    hits = modes_tri[:, :, None] == every_mode
    damping = jnp.sum(jnp.where(hits, decay_rate, 0.0), axis=(1, 2))
    own = rotate(right_part) + damping[:, None, None] * window_tier_states.astype(F32)
    return STEP_WEIGHT * (near + far - own)


def solution(mesh):
    in_specs = (
        P("grp", "ado", None, None, None),
        P("grp", "ado", None, None),
        P("ado", "grp", None),
        P("ado", None),
        P("ado", "grp"),
        P("ado", None),
        P(),
        P("grp", None, None),
        P("grp"),
        P("grp"),
        P(),
    )
    out_specs = P("ado", "grp", None)
    return jax.shard_map(
        on_device, mesh=mesh, in_specs=in_specs, out_specs=out_specs, check_vma=False
    )
```

```python
import functools

import jax
import jax.numpy as jnp
from jax import lax
from jax.experimental import pallas as pl
from jax.experimental.pallas import tpu as pltpu
from jax.sharding import PartitionSpec as P

STEP_WEIGHT = 0.5
F32 = jnp.float32
BF16 = jnp.bfloat16
LINK = jnp.float16
VMEM = pl.BlockSpec(memory_space=pltpu.VMEM)
SMEM = pl.BlockSpec(memory_space=pltpu.SMEM)
HBM = pl.BlockSpec(memory_space=pltpu.HBM)


def doubled(matrices):
    empty = jnp.zeros_like(matrices)
    upper_half = jnp.concatenate([matrices, empty], axis=-1)
    lower_half = jnp.concatenate([empty, matrices], axis=-1)
    return jnp.concatenate([upper_half, lower_half], axis=-2)


def rotate(parts):
    width = parts.shape[-1] // 2
    return jnp.concatenate([parts[..., width:], -parts[..., :width]], axis=-1)


RINGS = 8
CAP = 3
LOT = 4
SPAN = 2 * CAP * RINGS
SENDS = ((1, (-3,)), (-1, (3,)), (1, (1,)), (-1, (-1,)), (2, (2,)), (-2, (-2,)), (0, (4, 0)))
FAR = ((0, 0, 1), (1, 0, -1), (6, 0, 0))
NEAR = ((2, 0, 1), (3, 0, -1), (4, 0, 2), (5, 0, -2), (6, 1, 0))
SIBLING = [(i, i ^ 1) for i in range(2 * RINGS * RINGS)]


def device(core, along, across):
    along, across = along % RINGS, across % RINGS
    return along * 16 + across * 2 if core == 0 else across * 16 + along * 2 + 1


def onward(step):
    return [
        (device(c, a, b), device(c, a + step, b)) for c in range(2) for a in range(RINGS) for b in range(RINGS)
    ]


DELIVER = [[device(c, a, b) for b in range(RINGS)] for c in range(2) for a in range(RINGS)]
REDUCE = [
    [g * 2 * RINGS * RINGS + member for g in range(4) for member in members] for members in DELIVER
]


def pick_kernel(spot_ref, own_slot, sib_slot, own_ref, sib_hbm, *refs):
    out_refs, (sib_ref, held, sem, sems) = refs[:-4], refs[-4:]
    copy = pltpu.make_async_copy(sib_hbm, sib_ref, sem)
    copy.start()
    core, along = spot_ref[0], spot_ref[1]
    far = jnp.where(core == 0, 16, 2)
    near = jnp.where(core == 0, 2, 16)
    count = own_slot.shape[0] // CAP

    def fill(ahead, place, kind):
        slots, store = ((own_slot, own_ref), (sib_slot, sib_ref))[kind]
        first = lax.rem(along + ahead + RINGS, RINGS) * far + core
        for c in range(CAP):
            for r in range(RINGS):
                slot = slots[c * count + first + r * near]
                held[place * SPAN + kind * CAP * RINGS + c * RINGS + r] = store[jnp.maximum(slot, 0)]

    aheads = [ahead for _, group in SENDS for ahead in group]
    for place, ahead in enumerate(aheads):
        fill(ahead, place, 0)
    copy.wait()
    copies, place = [], 0
    for n, ((_, group), out_ref) in enumerate(zip(SENDS, out_refs, strict=True)):
        for ahead in group:
            fill(ahead, place, 1)
            place += 1
        begin = (place - len(group)) * SPAN
        copies.append(pltpu.make_async_copy(held.at[pl.ds(begin, len(group) * SPAN)], out_ref, sems.at[n]))
        copies[-1].start()
    for copy in copies:
        copy.wait()


def pick(spot, own_slots, sib_slots, own, sib):
    tile = own.shape[1:]
    total = sum(len(group) for _, group in SENDS)
    return pl.pallas_call(
        pick_kernel,
        in_specs=[SMEM, SMEM, SMEM, VMEM, HBM],
        out_specs=[HBM] * len(SENDS),
        out_shape=[pltpu.HBM((len(group) * SPAN,) + tile, own.dtype) for _, group in SENDS],
        scratch_shapes=[
            pltpu.VMEM(own.shape, own.dtype),
            pltpu.VMEM((total * SPAN,) + tile, own.dtype),
            pltpu.SemaphoreType.DMA,
            pltpu.SemaphoreType.DMA((len(SENDS),)),
        ],
        compiler_params=pltpu.CompilerParams(vmem_limit_bytes=24 * 2**20),
        cost_estimate=pl.CostEstimate(flops=0, bytes_accessed=10 * 2**20, transcendentals=0),
    )(spot, own_slots, sib_slots, own, sib)


def terms_kernel(sources, modes, windows, part, spot_ref, list_ref, re_ref, im_ref, *refs):
    count = len(sources)
    state_refs, (wide_ref, ham_ref, rho_ref) = refs[:count], refs[count:count + 3]
    out_ref, flat, acc, sems = refs[count + 3:]
    here = spot_ref[2]
    share = rho_ref.shape[1]
    width = ham_ref.shape[0]
    pairs = RINGS * windows
    blocks = width // share
    begin, end, slot = part
    levels = modes // LOT + CAP
    downs, extra, counts = modes, modes + CAP + slot * levels, list_ref.shape[0] - 1

    copies = [
        pltpu.make_async_copy(
            state_refs[n].at[pl.ds(place * SPAN, SPAN)], flat.at[pl.ds(n * SPAN, SPAN)], sems.at[n]
        )
        for n, (_, place, _) in enumerate(sources)
    ]
    for copy in copies:
        copy.start()
    for copy in copies:
        copy.wait()

    def lot(pair, base):
        entries = [list_ref[base + n, pair] for n in range(LOT)]
        maps = [lax.shift_right_logical(e, 9) for e in entries]
        tiles = [flat[e & 511] for e in entries]
        rows = [
            wide_ref[maps[n], :width, :] + wide_ref[maps[n + 1], width:, :] for n in range(0, LOT, 2)
        ]
        left = jnp.dot(
            jnp.concatenate(rows, axis=1), jnp.concatenate(tiles, axis=0), preferred_element_type=F32
        )
        right = jnp.dot(
            jnp.concatenate(tiles, axis=1),
            jnp.concatenate([wide_ref[m] for m in maps], axis=0),
            preferred_element_type=F32,
        )
        return rotate(left - right)

    together = 16

    def first(index, carry):
        for j in range(together):
            pair = index * together + j
            acc[pair] = lot(pair, 0)
        return carry

    lax.fori_loop(begin * windows // together, end * windows // together, first, 0)

    def listed(level, work):
        def some(index, carry):
            found = [list_ref[extra + level, index * 4 + j] for j in range(4)]
            values = [work(jnp.minimum(pair, pairs - 1)) for pair in found]
            for pair, value in zip(found, values, strict=True):
                acc[pair] += value
            return carry

        lax.fori_loop(0, lax.shift_right_logical(list_ref[counts, slot * levels + level] + 3, 2), some, 0)

    def more(level, carry):
        listed(level, lambda pair: lot(pair, level * LOT))
        return carry

    lax.fori_loop(1, modes // LOT, more, 0)

    def lower(t, carry):
        def work(pair):
            entry = list_ref[downs + t, pair]
            mode = lax.shift_right_logical(entry, 9)
            state = flat[entry & 511]
            wide = wide_ref[mode]
            ahead = jnp.dot(wide[:width, :width], state, preferred_element_type=F32)
            after = jnp.dot(state, wide, preferred_element_type=F32)
            return re_ref[mode] * rotate(ahead - after) + im_ref[mode] * (ahead + after)

        listed(modes // LOT + t, work)
        return carry

    lax.fori_loop(0, CAP, lower, 0)

    if sources is NEAR:

        for w in range(windows):
            acc[here * windows + w] += rotate(
                jnp.dot(ham_ref[...], rho_ref[w], preferred_element_type=F32)
            )

    def leave(r, carry):
        for w in range(windows):
            value = acc[r * windows + w]
            for b in range(blocks):
                out_ref[b, r - begin, w] = value[b * share:(b + 1) * share]
        return carry

    lax.fori_loop(begin, end, leave, 0)


def terms(sources, part, spot, lists, coup_re, coup_im, states, maps_wide, head_cols, rho):
    modes = maps_wide.shape[0] - 1
    windows, share, lanes = rho.shape
    width = head_cols.shape[0]
    return pl.pallas_call(
        functools.partial(terms_kernel, sources, modes, windows, part),
        in_specs=[SMEM] * 4 + [HBM] * len(sources) + [VMEM] * 3,
        out_specs=VMEM,
        out_shape=jax.ShapeDtypeStruct((width // share, part[1] - part[0], windows, share, lanes), F32),
        scratch_shapes=[
            pltpu.VMEM((len(sources) * SPAN, width, lanes), BF16),
            pltpu.VMEM((RINGS * windows + 1, width, lanes), F32),
            pltpu.SemaphoreType.DMA((len(sources),)),
        ],
        compiler_params=pltpu.CompilerParams(vmem_limit_bytes=28 * 2**20),
        cost_estimate=pl.CostEstimate(flops=10**9, bytes_accessed=10 * 2**20, transcendentals=0),
    )(spot, lists, coup_re, coup_im, *[states[n] for n, _, _ in sources], maps_wide, head_cols, rho)


def lists_of(steps, parts, modes, spot_ref, heard_ref, out_ref):
    core, along, across, group = spot_ref[0], spot_ref[1], spot_ref[2], spot_ref[3]
    pairs = heard_ref.shape[1]
    windows = pairs // RINGS

    def locate(places):
        owner = lax.shift_right_logical(places * 171, 9)
        z, y, c = lax.shift_right_logical(owner, 4), lax.shift_right_logical(owner, 1) & 7, owner & 1
        off = (jnp.where(core == 0, z, y) - along) & (RINGS - 1)
        source = jnp.full_like(off, -1)
        for n, (_, _, step) in enumerate(steps):
            source = jnp.where(off == -step % RINGS, n, source)
        mine = (jnp.where(core == 0, y, z) == across) & (source >= 0)
        kind = jnp.where(c == core, 0, 1)
        lanes = lax.broadcasted_iota(jnp.int32, places.shape, 1)
        receiver = lax.shift_right_logical(lanes, windows.bit_length() - 1)
        return mine, ((source * 2 + kind) * CAP + places - owner * CAP) * RINGS + receiver

    def square(n, axis):
        return lax.broadcasted_iota(jnp.int32, (n, n), axis)

    def ones(mask):
        return jnp.where(mask, 1.0, 0.0)

    mine, row = locate(heard_ref[:modes])
    ids = lax.broadcasted_iota(jnp.int32, mine.shape, 0)
    below = ones(square(modes, 0) > square(modes, 1))
    rank = jnp.dot(below, ones(mine), preferred_element_type=F32).astype(jnp.int32)
    rank = jnp.where(mine, rank, -1)
    count = jnp.sum(ones(mine), axis=0, keepdims=True)
    value = (ids * 512 + row - modes * 512).astype(F32)
    for n in range(modes):
        found = jnp.sum(jnp.where(rank == n, value, 0.0), axis=0, keepdims=True)
        out_ref[n:n + 1] = found.astype(jnp.int32) + modes * 512

    mine, row = locate(heard_ref[modes:modes + CAP])
    local = heard_ref[modes + CAP:modes + 2 * CAP] - group * modes
    live = mine & (local >= 0) & (local < modes)
    out_ref[modes:modes + CAP] = jnp.where(live, local * 512 + row, 0)

    first = lax.broadcasted_iota(jnp.int32, (1, pairs), 1)
    flags = []
    for begin, end in parts:
        inside = (first >= begin * windows) & (first < end * windows)
        for n in range(modes // LOT):
            flags.append(ones(inside & (count > n * LOT)))
        for t in range(CAP):
            flags.append(ones(inside & live[t:t + 1]))
    total = len(flags)
    flags = jnp.concatenate(flags + [jnp.zeros((pairs - total, pairs), F32)], axis=0)
    turned = (((1,), (1,)), ((), ()))
    down, over = square(pairs, 0), square(pairs, 1)
    chosen = lax.dot_general(ones(down == over), flags, turned, preferred_element_type=F32)
    order = lax.dot_general(ones(down > over), flags, turned, preferred_element_type=F32)
    order = jnp.where(chosen > 0.5, order, -1.0)
    numbers = (down - pairs).astype(F32)
    lanes = over.astype(F32)
    for n in range(total):
        found = jnp.sum(jnp.where(order[:, n:n + 1] == lanes, numbers, 0.0), axis=0, keepdims=True)
        out_ref[modes + CAP + n:modes + CAP + n + 1] = found.astype(jnp.int32) + pairs
    sums = lax.dot_general(jnp.ones((8, pairs), F32), flags, turned, preferred_element_type=F32)
    last = out_ref.shape[0] - 1
    out_ref[last:last + 1] = sums[:1].astype(jnp.int32)


def lists_kernel(kinds, modes, spot_ref, *refs):
    for (steps, parts), heard_ref, out_ref in zip(kinds, refs[:len(kinds)], refs[len(kinds):], strict=True):
        lists_of(steps, parts, modes, spot_ref, heard_ref, out_ref)


def use_lists(kinds, modes, spot, heard):
    rows = [modes + CAP + len(parts) * (modes // LOT + CAP) + 1 for _, parts in kinds]
    return pl.pallas_call(
        functools.partial(lists_kernel, kinds, modes),
        in_specs=[SMEM] + [VMEM] * len(kinds),
        out_specs=[VMEM] * len(kinds),
        out_shape=[jax.ShapeDtypeStruct((n + -n % 8, heard[0].shape[1]), jnp.int32) for n in rows],
        compiler_params=pltpu.CompilerParams(vmem_limit_bytes=8 * 2**20),
        cost_estimate=pl.CostEstimate(flops=10**7, bytes_accessed=2**18, transcendentals=0),
    )(spot, *heard)


def say_kernel(spot_ref, up_ref, down_ref, tri_ref, out_ref):
    windows, modes = up_ref.shape
    shape = (windows, out_ref.shape[1])
    lanes = lax.broadcasted_iota(jnp.int32, shape, 1)
    row = lax.broadcasted_iota(jnp.int32, shape, 0)
    place = jnp.where(lanes == spot_ref[2] * windows + row, 1.0, 0.0)

    def put(values, axis):
        def half(part):
            return lax.dot_general(
                part.astype(F32), place, (((axis,), (0,)), ((), ())), preferred_element_type=F32
            )

        high = lax.shift_right_logical(values, 5)
        return (half(high) * 32.0 + half(values & 31)).astype(jnp.int32)

    up, down, tri = put(up_ref[...], 0), put(down_ref[...], 1), put(tri_ref[...], 1)
    spare = jnp.zeros((out_ref.shape[0] - modes - 2 * CAP, shape[1]), jnp.int32)
    whole = jnp.concatenate([up, down, tri, spare], axis=0)
    out_ref[...] = whole


def say(spot, use_up, use_down, modes_tri):
    windows, modes = use_up.shape
    rows = modes + 2 * CAP
    return pl.pallas_call(
        say_kernel,
        in_specs=[SMEM, VMEM, VMEM, VMEM],
        out_specs=VMEM,
        out_shape=jax.ShapeDtypeStruct((rows + -rows % 8, RINGS * windows), jnp.int32),
        cost_estimate=pl.CostEstimate(flops=10**6, bytes_accessed=2**18, transcendentals=0),
    )(spot, use_up, use_down.T, modes_tri.T)


def reduced(parts):
    parts = parts.reshape((-1,) + parts.shape[2:]).astype(LINK)
    parts = lax.all_to_all(
        parts, ("grp", "ado"), split_axis=0, concat_axis=0, tiled=True, axis_index_groups=REDUCE
    )
    return jnp.sum(parts.astype(F32), axis=0)


def on_device(
    states, send_slot, window_tier_states, modes_tri, use_up, use_down,
    hamiltonian, coupling, coup_re, coup_im, decay_rate,
):
    width = hamiltonian.shape[0]
    windows, share = window_tier_states.shape[:2]
    modes = coupling.shape[0]
    group = lax.axis_index("grp").astype(jnp.int32)
    index = lax.axis_index("ado").astype(jnp.int32)
    core, z, y = index & 1, index >> 4, (index >> 1) & 7
    along = jnp.where(core == 0, z, y)
    across = jnp.where(core == 0, y, z)

    spot = jnp.stack([core, along, across, group])

    slots = jnp.transpose(send_slot[0, 0]).reshape(-1)
    sib_store = lax.ppermute(states[0, 0], "ado", SIBLING)
    sib_slots = lax.ppermute(slots, "ado", SIBLING)
    slots, use_up = lax.optimization_barrier((slots, use_up))
    said = say(spot, use_up, use_down, modes_tri)
    heard = lax.all_to_all(
        jnp.broadcast_to(said, (RINGS,) + said.shape), "ado", split_axis=0, concat_axis=0, tiled=True,
        axis_index_groups=DELIVER,
    )
    heard, slots = lax.optimization_barrier((jnp.sum(heard, axis=0), slots))
    heard_far = lax.ppermute(heard, "ado", onward(4))
    picked = pick(spot, slots, sib_slots, states[0, 0], sib_store)
    maps_wide = jnp.concatenate([doubled(coupling), jnp.zeros((1, 2 * width, 2 * width), BF16)], axis=0)
    head_cols = lax.dynamic_slice_in_dim(hamiltonian, group * share, share, 1)
    shared = (maps_wide, head_cols, window_tier_states)
    picked, heard, heard_far, shared = lax.optimization_barrier((picked, heard, heard_far, shared))

    sent = [
        block if step == 0 else lax.ppermute(block, "ado", onward(step))
        for (step, _), block in zip(SENDS, picked, strict=True)
    ]
    kinds = ((FAR, ((0, RINGS),)), (NEAR, ((0, RINGS),)))
    far_lists, near_lists = use_lists(kinds, modes, spot, (heard_far, heard))

    far = terms(FAR, (0, RINGS, 0), spot, far_lists, coup_re, coup_im, sent, *shared)
    far, near_lists, sent = lax.optimization_barrier((far, near_lists, sent))
    far = lax.ppermute(reduced(far), "ado", onward(4))
    near = reduced(terms(NEAR, (0, RINGS, 0), spot, near_lists, coup_re, coup_im, sent, *shared))

    ham_wide = doubled(hamiltonian)
    right_part = jnp.einsum("wab,bc->wac", window_tier_states, ham_wide, preferred_element_type=F32)
    every_mode = jnp.arange(decay_rate.shape[0], dtype=jnp.int32)
    hits = modes_tri[:, :, None] == every_mode
    damping = jnp.sum(jnp.where(hits, decay_rate, 0.0), axis=(1, 2))
    own = rotate(right_part) + damping[:, None, None] * window_tier_states.astype(F32)
    return STEP_WEIGHT * (near + far - own)


def solution(mesh):
    in_specs = (
        P("grp", "ado", None, None, None),
        P("grp", "ado", None, None),
        P("ado", "grp", None),
        P("ado", None),
        P("ado", "grp"),
        P("ado", None),
        P(),
        P("grp", None, None),
        P("grp"),
        P("grp"),
        P(),
    )
    out_specs = P("ado", "grp", None)
    return jax.shard_map(
        on_device, mesh=mesh, in_specs=in_specs, out_specs=out_specs, check_vma=False
    )
```

```python
import functools

import jax
import jax.numpy as jnp
from jax import lax
from jax.experimental import pallas as pl
from jax.experimental.pallas import tpu as pltpu
from jax.sharding import PartitionSpec as P

STEP_WEIGHT = 0.5
F32 = jnp.float32
BF16 = jnp.bfloat16
LINK = jnp.float16
VMEM = pl.BlockSpec(memory_space=pltpu.VMEM)
SMEM = pl.BlockSpec(memory_space=pltpu.SMEM)
HBM = pl.BlockSpec(memory_space=pltpu.HBM)


def doubled(matrices):
    empty = jnp.zeros_like(matrices)
    upper_half = jnp.concatenate([matrices, empty], axis=-1)
    lower_half = jnp.concatenate([empty, matrices], axis=-1)
    return jnp.concatenate([upper_half, lower_half], axis=-2)


def rotate(parts):
    width = parts.shape[-1] // 2
    return jnp.concatenate([parts[..., width:], -parts[..., :width]], axis=-1)


RINGS = 8
CAP = 3
LOT = 4
SPAN = 2 * CAP * RINGS
SENDS = ((1, (-3,)), (-1, (3,)), (2, (2,)), (-2, (-2,)), (1, (1,)), (-1, (-1,)), (0, (4, 0)))
FAR = ((0, 0, 1), (1, 0, -1), (6, 0, 0))
NEAR = ((2, 0, 2), (3, 0, -2), (4, 0, 1), (5, 0, -1), (6, 1, 0))
SIBLING = [(i, i ^ 1) for i in range(2 * RINGS * RINGS)]


def device(core, along, across):
    along, across = along % RINGS, across % RINGS
    return along * 16 + across * 2 if core == 0 else across * 16 + along * 2 + 1


def onward(step):
    return [
        (device(c, a, b), device(c, a + step, b)) for c in range(2) for a in range(RINGS) for b in range(RINGS)
    ]


DELIVER = [[device(c, a, b) for b in range(RINGS)] for c in range(2) for a in range(RINGS)]


def pick_kernel(spot_ref, own_slot, sib_slot, own_ref, sib_hbm, *refs):
    out_refs, (sib_ref, held, sem, sems) = refs[:-4], refs[-4:]
    copy = pltpu.make_async_copy(sib_hbm, sib_ref, sem)
    copy.start()
    core, along = spot_ref[0], spot_ref[1]
    far = jnp.where(core == 0, 16, 2)
    near = jnp.where(core == 0, 2, 16)
    count = own_slot.shape[0] // CAP

    def fill(ahead, place, kind):
        slots, store = ((own_slot, own_ref), (sib_slot, sib_ref))[kind]
        first = lax.rem(along + ahead + RINGS, RINGS) * far + core
        for c in range(CAP):
            for r in range(RINGS):
                slot = slots[c * count + first + r * near]
                held[place * SPAN + kind * CAP * RINGS + c * RINGS + r] = store[jnp.maximum(slot, 0)]

    aheads = [ahead for _, group in SENDS for ahead in group]
    for place, ahead in enumerate(aheads):
        fill(ahead, place, 0)
    copy.wait()
    copies, place = [], 0
    for n, ((_, group), out_ref) in enumerate(zip(SENDS, out_refs, strict=True)):
        for ahead in group:
            fill(ahead, place, 1)
            place += 1
        begin = (place - len(group)) * SPAN
        copies.append(pltpu.make_async_copy(held.at[pl.ds(begin, len(group) * SPAN)], out_ref, sems.at[n]))
        copies[-1].start()
    for copy in copies:
        copy.wait()


def pick(spot, own_slots, sib_slots, own, sib):
    tile = own.shape[1:]
    total = sum(len(group) for _, group in SENDS)
    return pl.pallas_call(
        pick_kernel,
        in_specs=[SMEM, SMEM, SMEM, VMEM, HBM],
        out_specs=[HBM] * len(SENDS),
        out_shape=[pltpu.HBM((len(group) * SPAN,) + tile, own.dtype) for _, group in SENDS],
        scratch_shapes=[
            pltpu.VMEM(own.shape, own.dtype),
            pltpu.VMEM((total * SPAN,) + tile, own.dtype),
            pltpu.SemaphoreType.DMA,
            pltpu.SemaphoreType.DMA((len(SENDS),)),
        ],
        compiler_params=pltpu.CompilerParams(vmem_limit_bytes=24 * 2**20),
        cost_estimate=pl.CostEstimate(flops=0, bytes_accessed=10 * 2**20, transcendentals=0),
    )(spot, own_slots, sib_slots, own, sib)


def terms_kernel(sources, modes, windows, part, spot_ref, list_ref, re_ref, im_ref, *refs):
    count = len(sources)
    state_refs, (wide_ref, ham_ref, rho_ref) = refs[:count], refs[count:count + 3]
    out_refs, (flat, acc, sems) = refs[count + 3:-3], refs[-3:]
    here, group = spot_ref[2], spot_ref[3]
    share = rho_ref.shape[1]
    width = ham_ref.shape[0]
    pairs = RINGS * windows
    blocks = width // share
    begin, end, slot = part
    levels = modes // LOT + CAP
    downs, extra, counts = modes, modes + CAP + slot * levels, list_ref.shape[0] - 1

    copies = [
        pltpu.make_async_copy(
            state_refs[n].at[pl.ds(place * SPAN, SPAN)], flat.at[pl.ds(n * SPAN, SPAN)], sems.at[n]
        )
        for n, (_, place, _) in enumerate(sources)
    ]
    for copy in copies:
        copy.start()
    for copy in copies:
        copy.wait()

    def lot(pair, base):
        entries = [list_ref[base + n, pair] for n in range(LOT)]
        maps = [lax.shift_right_logical(e, 9) for e in entries]
        tiles = [flat[e & 511] for e in entries]
        rows = [
            wide_ref[maps[n], :width, :] + wide_ref[maps[n + 1], width:, :] for n in range(0, LOT, 2)
        ]
        left = jnp.dot(
            jnp.concatenate(rows, axis=1), jnp.concatenate(tiles, axis=0), preferred_element_type=F32
        )
        right = jnp.dot(
            jnp.concatenate(tiles, axis=1),
            jnp.concatenate([wide_ref[m] for m in maps], axis=0),
            preferred_element_type=F32,
        )
        return rotate(left - right)

    together = 16

    def first(index, carry):
        for j in range(together):
            pair = index * together + j
            acc[pair] = lot(pair, 0)
        return carry

    lax.fori_loop(begin * windows // together, end * windows // together, first, 0)

    def listed(level, work):
        def some(index, carry):
            found = [list_ref[extra + level, index * 4 + j] for j in range(4)]
            values = [work(jnp.minimum(pair, pairs - 1)) for pair in found]
            for pair, value in zip(found, values, strict=True):
                acc[pair] += value
            return carry

        lax.fori_loop(0, lax.shift_right_logical(list_ref[counts, slot * levels + level] + 3, 2), some, 0)

    def more(level, carry):
        listed(level, lambda pair: lot(pair, level * LOT))
        return carry

    lax.fori_loop(1, modes // LOT, more, 0)

    def lower(t, carry):
        def work(pair):
            entry = list_ref[downs + t, pair]
            mode = lax.shift_right_logical(entry, 9)
            state = flat[entry & 511]
            wide = wide_ref[mode]
            ahead = jnp.dot(wide[:width, :width], state, preferred_element_type=F32)
            after = jnp.dot(state, wide, preferred_element_type=F32)
            return re_ref[mode] * rotate(ahead - after) + im_ref[mode] * (ahead + after)

        listed(modes // LOT + t, work)
        return carry

    lax.fori_loop(0, CAP, lower, 0)

    if sources is NEAR:

        for w in range(windows):
            acc[here * windows + w] += rotate(
                jnp.dot(ham_ref[...], rho_ref[w], preferred_element_type=F32)
            )

    def leave(r, carry):
        for w in range(windows):
            for shift, out_ref in enumerate(out_refs):
                block = lax.rem(group + shift, blocks) * share
                out_ref[r - begin, w] = acc[r * windows + w, pl.ds(pl.multiple_of(block, share), share), :]
        return carry

    lax.fori_loop(begin, end, leave, 0)


def terms(sources, part, spot, lists, coup_re, coup_im, states, maps_wide, head_cols, rho):
    modes = maps_wide.shape[0] - 1
    windows, share, lanes = rho.shape
    width = head_cols.shape[0]
    return pl.pallas_call(
        functools.partial(terms_kernel, sources, modes, windows, part),
        in_specs=[SMEM] * 4 + [HBM] * len(sources) + [VMEM] * 3,
        out_specs=[VMEM] * (width // share),
        out_shape=[jax.ShapeDtypeStruct((part[1] - part[0], windows, share, lanes), F32)] * (width // share),
        scratch_shapes=[
            pltpu.VMEM((len(sources) * SPAN, width, lanes), BF16),
            pltpu.VMEM((RINGS * windows + 1, width, lanes), F32),
            pltpu.SemaphoreType.DMA((len(sources),)),
        ],
        compiler_params=pltpu.CompilerParams(vmem_limit_bytes=28 * 2**20),
        cost_estimate=pl.CostEstimate(flops=10**9, bytes_accessed=10 * 2**20, transcendentals=0),
    )(spot, lists, coup_re, coup_im, *[states[n] for n, _, _ in sources], maps_wide, head_cols, rho)


def lists_of(steps, parts, modes, spot_ref, heard_ref, out_ref):
    core, along, across, group = spot_ref[0], spot_ref[1], spot_ref[2], spot_ref[3]
    pairs = heard_ref.shape[1]
    windows = pairs // RINGS

    def locate(places):
        owner = lax.shift_right_logical(places * 171, 9)
        z, y, c = lax.shift_right_logical(owner, 4), lax.shift_right_logical(owner, 1) & 7, owner & 1
        off = (jnp.where(core == 0, z, y) - along) & (RINGS - 1)
        source = jnp.full_like(off, -1)
        for n, (_, _, step) in enumerate(steps):
            source = jnp.where(off == -step % RINGS, n, source)
        mine = (jnp.where(core == 0, y, z) == across) & (source >= 0)
        kind = jnp.where(c == core, 0, 1)
        lanes = lax.broadcasted_iota(jnp.int32, places.shape, 1)
        receiver = lax.shift_right_logical(lanes, windows.bit_length() - 1)
        return mine, ((source * 2 + kind) * CAP + places - owner * CAP) * RINGS + receiver

    def square(n, axis):
        return lax.broadcasted_iota(jnp.int32, (n, n), axis)

    def ones(mask):
        return jnp.where(mask, 1.0, 0.0)

    mine, row = locate(heard_ref[:modes])
    ids = lax.broadcasted_iota(jnp.int32, mine.shape, 0)
    below = ones(square(modes, 0) > square(modes, 1))
    rank = jnp.dot(below, ones(mine), preferred_element_type=F32).astype(jnp.int32)
    rank = jnp.where(mine, rank, -1)
    count = jnp.sum(ones(mine), axis=0, keepdims=True)
    value = (ids * 512 + row - modes * 512).astype(F32)
    for n in range(modes):
        found = jnp.sum(jnp.where(rank == n, value, 0.0), axis=0, keepdims=True)
        out_ref[n:n + 1] = found.astype(jnp.int32) + modes * 512

    mine, row = locate(heard_ref[modes:modes + CAP])
    local = heard_ref[modes + CAP:modes + 2 * CAP] - group * modes
    live = mine & (local >= 0) & (local < modes)
    out_ref[modes:modes + CAP] = jnp.where(live, local * 512 + row, 0)

    first = lax.broadcasted_iota(jnp.int32, (1, pairs), 1)
    flags = []
    for begin, end in parts:
        inside = (first >= begin * windows) & (first < end * windows)
        for n in range(modes // LOT):
            flags.append(ones(inside & (count > n * LOT)))
        for t in range(CAP):
            flags.append(ones(inside & live[t:t + 1]))
    total = len(flags)
    flags = jnp.concatenate(flags + [jnp.zeros((pairs - total, pairs), F32)], axis=0)
    turned = (((1,), (1,)), ((), ()))
    down, over = square(pairs, 0), square(pairs, 1)
    chosen = lax.dot_general(ones(down == over), flags, turned, preferred_element_type=F32)
    order = lax.dot_general(ones(down > over), flags, turned, preferred_element_type=F32)
    order = jnp.where(chosen > 0.5, order, -1.0)
    numbers = (down - pairs).astype(F32)
    lanes = over.astype(F32)
    for n in range(total):
        found = jnp.sum(jnp.where(order[:, n:n + 1] == lanes, numbers, 0.0), axis=0, keepdims=True)
        out_ref[modes + CAP + n:modes + CAP + n + 1] = found.astype(jnp.int32) + pairs
    sums = lax.dot_general(jnp.ones((8, pairs), F32), flags, turned, preferred_element_type=F32)
    last = out_ref.shape[0] - 1
    out_ref[last:last + 1] = sums[:1].astype(jnp.int32)


def lists_kernel(kinds, modes, spot_ref, *refs):
    for (steps, parts), heard_ref, out_ref in zip(kinds, refs[:len(kinds)], refs[len(kinds):], strict=True):
        lists_of(steps, parts, modes, spot_ref, heard_ref, out_ref)


def use_lists(kinds, modes, spot, heard):
    rows = [modes + CAP + len(parts) * (modes // LOT + CAP) + 1 for _, parts in kinds]
    return pl.pallas_call(
        functools.partial(lists_kernel, kinds, modes),
        in_specs=[SMEM] + [VMEM] * len(kinds),
        out_specs=[VMEM] * len(kinds),
        out_shape=[jax.ShapeDtypeStruct((n + -n % 8, heard[0].shape[1]), jnp.int32) for n in rows],
        compiler_params=pltpu.CompilerParams(vmem_limit_bytes=8 * 2**20),
        cost_estimate=pl.CostEstimate(flops=10**7, bytes_accessed=2**18, transcendentals=0),
    )(spot, *heard)


def say_kernel(spot_ref, up_ref, down_ref, tri_ref, out_ref):
    windows, modes = up_ref.shape
    shape = (windows, out_ref.shape[1])
    lanes = lax.broadcasted_iota(jnp.int32, shape, 1)
    row = lax.broadcasted_iota(jnp.int32, shape, 0)
    place = jnp.where(lanes == spot_ref[2] * windows + row, 1.0, 0.0)

    def put(values, axis):
        def half(part):
            return lax.dot_general(
                part.astype(F32), place, (((axis,), (0,)), ((), ())), preferred_element_type=F32
            )

        high = lax.shift_right_logical(values, 5)
        return (half(high) * 32.0 + half(values & 31)).astype(jnp.int32)

    up, down, tri = put(up_ref[...], 0), put(down_ref[...], 1), put(tri_ref[...], 1)
    spare = jnp.zeros((out_ref.shape[0] - modes - 2 * CAP, shape[1]), jnp.int32)
    whole = jnp.concatenate([up, down, tri, spare], axis=0)
    out_ref[...] = whole


def say(spot, use_up, use_down, modes_tri):
    windows, modes = use_up.shape
    rows = modes + 2 * CAP
    return pl.pallas_call(
        say_kernel,
        in_specs=[SMEM, VMEM, VMEM, VMEM],
        out_specs=VMEM,
        out_shape=jax.ShapeDtypeStruct((rows + -rows % 8, RINGS * windows), jnp.int32),
        cost_estimate=pl.CostEstimate(flops=10**6, bytes_accessed=2**18, transcendentals=0),
    )(spot, use_up, use_down.T, modes_tri.T)


def over_groups(parts):
    count = len(parts)
    total = parts[0]
    for shift in (2, 1, 3):
        ring = [(i, (i + shift) % count) for i in range(count)]
        total = total + lax.ppermute(parts[shift].astype(LINK), "grp", ring).astype(F32)
    return total


def on_device(
    states, send_slot, window_tier_states, modes_tri, use_up, use_down,
    hamiltonian, coupling, coup_re, coup_im, decay_rate,
):
    width = hamiltonian.shape[0]
    windows, share = window_tier_states.shape[:2]
    modes = coupling.shape[0]
    group = lax.axis_index("grp").astype(jnp.int32)
    index = lax.axis_index("ado").astype(jnp.int32)
    core, z, y = index & 1, index >> 4, (index >> 1) & 7
    along = jnp.where(core == 0, z, y)
    across = jnp.where(core == 0, y, z)

    spot = jnp.stack([core, along, across, group])

    slots = jnp.transpose(send_slot[0, 0]).reshape(-1)
    sib_store = lax.ppermute(states[0, 0], "ado", SIBLING)
    sib_slots = lax.ppermute(slots, "ado", SIBLING)
    slots, use_up = lax.optimization_barrier((slots, use_up))
    said = say(spot, use_up, use_down, modes_tri)
    heard = lax.all_to_all(
        jnp.broadcast_to(said, (RINGS,) + said.shape), "ado", split_axis=0, concat_axis=0, tiled=True,
        axis_index_groups=DELIVER,
    )
    heard, slots = lax.optimization_barrier((jnp.sum(heard, axis=0), slots))
    heard_far = lax.ppermute(heard, "ado", onward(4))
    picked = pick(spot, slots, sib_slots, states[0, 0], sib_store)
    maps_wide = jnp.concatenate([doubled(coupling), jnp.zeros((1, 2 * width, 2 * width), BF16)], axis=0)
    head_cols = lax.dynamic_slice_in_dim(hamiltonian, group * share, share, 1)
    shared = (maps_wide, head_cols, window_tier_states)
    picked, heard, heard_far, shared = lax.optimization_barrier((picked, heard, heard_far, shared))

    sent = [
        block if step == 0 else lax.ppermute(block, "ado", onward(step))
        for (step, _), block in zip(SENDS, picked, strict=True)
    ]
    kinds = ((FAR, ((0, RINGS),)), (NEAR, ((0, RINGS),)))
    far_lists, near_lists = use_lists(kinds, modes, spot, (heard_far, heard))

    far = terms(FAR, (0, RINGS, 0), spot, far_lists, coup_re, coup_im, sent, *shared)
    far, near_lists = lax.optimization_barrier((far, near_lists))
    far = lax.ppermute(over_groups(far).astype(LINK), "ado", onward(4))
    near = over_groups(terms(NEAR, (0, RINGS, 0), spot, near_lists, coup_re, coup_im, sent, *shared))
    summed = lax.all_to_all(
        (near + far.astype(F32)).astype(LINK), "ado", split_axis=0, concat_axis=0, tiled=True,
        axis_index_groups=DELIVER,
    )

    ham_wide = doubled(hamiltonian)
    right_part = jnp.einsum("wab,bc->wac", window_tier_states, ham_wide, preferred_element_type=F32)
    every_mode = jnp.arange(decay_rate.shape[0], dtype=jnp.int32)
    hits = modes_tri[:, :, None] == every_mode
    damping = jnp.sum(jnp.where(hits, decay_rate, 0.0), axis=(1, 2))
    own = rotate(right_part) + damping[:, None, None] * window_tier_states.astype(F32)
    return STEP_WEIGHT * (jnp.sum(summed.astype(F32), axis=0) - own)


def solution(mesh):
    in_specs = (
        P("grp", "ado", None, None, None),
        P("grp", "ado", None, None),
        P("ado", "grp", None),
        P("ado", None),
        P("ado", "grp"),
        P("ado", None),
        P(),
        P("grp", None, None),
        P("grp"),
        P("grp"),
        P(),
    )
    out_specs = P("ado", "grp", None)
    return jax.shard_map(
        on_device, mesh=mesh, in_specs=in_specs, out_specs=out_specs, check_vma=False
    )
```

```python
import functools

import jax
import jax.numpy as jnp
from jax import lax
from jax.experimental import pallas as pl
from jax.experimental.pallas import tpu as pltpu
from jax.sharding import PartitionSpec as P

STEP_WEIGHT = 0.5
F32 = jnp.float32
BF16 = jnp.bfloat16
LINK = jnp.float16
VMEM = pl.BlockSpec(memory_space=pltpu.VMEM)
SMEM = pl.BlockSpec(memory_space=pltpu.SMEM)
HBM = pl.BlockSpec(memory_space=pltpu.HBM)


def doubled(matrices):
    empty = jnp.zeros_like(matrices)
    upper_half = jnp.concatenate([matrices, empty], axis=-1)
    lower_half = jnp.concatenate([empty, matrices], axis=-1)
    return jnp.concatenate([upper_half, lower_half], axis=-2)


def rotate(parts):
    width = parts.shape[-1] // 2
    return jnp.concatenate([parts[..., width:], -parts[..., :width]], axis=-1)


RINGS = 8
CAP = 3
LOT = 4
SPAN = 2 * CAP * RINGS
SENDS = ((1, (-3,)), (-1, (3,)), (2, (2,)), (-2, (-2,)), (1, (1,)), (-1, (-1,)), (0, (4, 0)))
FAR = ((0, 0, 1), (1, 0, -1), (6, 0, 0))
NEAR = ((2, 0, 2), (3, 0, -2), (4, 0, 1), (5, 0, -1), (6, 1, 0))
SIBLING = [(i, i ^ 1) for i in range(2 * RINGS * RINGS)]


def device(core, along, across):
    along, across = along % RINGS, across % RINGS
    return along * 16 + across * 2 if core == 0 else across * 16 + along * 2 + 1


def onward(step):
    return [
        (device(c, a, b), device(c, a + step, b)) for c in range(2) for a in range(RINGS) for b in range(RINGS)
    ]


DELIVER = [[device(c, a, b) for b in range(RINGS)] for c in range(2) for a in range(RINGS)]


def pick_kernel(spot_ref, own_slot, sib_slot, own_ref, sib_hbm, *refs):
    out_refs, (sib_ref, sem) = refs[:-2], refs[-2:]
    copy = pltpu.make_async_copy(sib_hbm, sib_ref, sem)
    copy.start()
    core, along = spot_ref[0], spot_ref[1]
    far = jnp.where(core == 0, 16, 2)
    near = jnp.where(core == 0, 2, 16)
    count = own_slot.shape[0] // CAP
    for kind, (slots, store) in enumerate(((own_slot, own_ref), (sib_slot, sib_ref))):
        if kind == 1:
            copy.wait()
        for (_, group), out_ref in zip(SENDS, out_refs, strict=True):
            for place, ahead in enumerate(group):
                first = lax.rem(along + ahead + RINGS, RINGS) * far + core
                for c in range(CAP):
                    for r in range(RINGS):
                        slot = slots[c * count + first + r * near]
                        row = place * SPAN + kind * CAP * RINGS + c * RINGS + r
                        out_ref[row] = store[jnp.maximum(slot, 0)]


def pick(spot, own_slots, sib_slots, own, sib):
    tile = own.shape[1:]
    return pl.pallas_call(
        pick_kernel,
        in_specs=[SMEM, SMEM, SMEM, VMEM, HBM],
        out_specs=[VMEM] * len(SENDS),
        out_shape=[jax.ShapeDtypeStruct((len(group) * SPAN,) + tile, own.dtype) for _, group in SENDS],
        scratch_shapes=[pltpu.VMEM(own.shape, own.dtype), pltpu.SemaphoreType.DMA],
        compiler_params=pltpu.CompilerParams(vmem_limit_bytes=24 * 2**20),
        cost_estimate=pl.CostEstimate(flops=0, bytes_accessed=10 * 2**20, transcendentals=0),
    )(spot, own_slots, sib_slots, own, sib)


def terms_kernel(sources, modes, windows, part, spot_ref, list_ref, re_ref, im_ref, *refs):
    count = len(sources)
    state_refs, (wide_ref, ham_ref, rho_ref) = refs[:count], refs[count:count + 3]
    out_refs, (flat, acc, sems) = refs[count + 3:-3], refs[-3:]
    here, group = spot_ref[2], spot_ref[3]
    share = rho_ref.shape[1]
    width = ham_ref.shape[0]
    pairs = RINGS * windows
    blocks = width // share
    begin, end, slot = part
    levels = modes // LOT + CAP
    downs, extra, counts = modes, modes + CAP + slot * levels, list_ref.shape[0] - 1

    copies = [
        pltpu.make_async_copy(
            state_refs[n].at[pl.ds(place * SPAN, SPAN)], flat.at[pl.ds(n * SPAN, SPAN)], sems.at[n]
        )
        for n, (_, place, _) in enumerate(sources)
    ]
    for copy in copies:
        copy.start()
    for copy in copies:
        copy.wait()

    def lot(pair, base):
        entries = [list_ref[base + n, pair] for n in range(LOT)]
        maps = [lax.shift_right_logical(e, 9) for e in entries]
        tiles = [flat[e & 511] for e in entries]
        rows = [
            wide_ref[maps[n], :width, :] + wide_ref[maps[n + 1], width:, :] for n in range(0, LOT, 2)
        ]
        left = jnp.dot(
            jnp.concatenate(rows, axis=1), jnp.concatenate(tiles, axis=0), preferred_element_type=F32
        )
        right = jnp.dot(
            jnp.concatenate(tiles, axis=1),
            jnp.concatenate([wide_ref[m] for m in maps], axis=0),
            preferred_element_type=F32,
        )
        return rotate(left - right)

    together = 16

    def first(index, carry):
        for j in range(together):
            pair = index * together + j
            acc[pair] = lot(pair, 0)
        return carry

    lax.fori_loop(begin * windows // together, end * windows // together, first, 0)

    def listed(level, work):
        def some(index, carry):
            found = [list_ref[extra + level, index * 4 + j] for j in range(4)]
            values = [work(jnp.minimum(pair, pairs - 1)) for pair in found]
            for pair, value in zip(found, values, strict=True):
                acc[pair] += value
            return carry

        lax.fori_loop(0, lax.shift_right_logical(list_ref[counts, slot * levels + level] + 3, 2), some, 0)

    def more(level, carry):
        listed(level, lambda pair: lot(pair, level * LOT))
        return carry

    lax.fori_loop(1, modes // LOT, more, 0)

    def lower(t, carry):
        def work(pair):
            entry = list_ref[downs + t, pair]
            mode = lax.shift_right_logical(entry, 9)
            state = flat[entry & 511]
            wide = wide_ref[mode]
            ahead = jnp.dot(wide[:width, :width], state, preferred_element_type=F32)
            after = jnp.dot(state, wide, preferred_element_type=F32)
            return re_ref[mode] * rotate(ahead - after) + im_ref[mode] * (ahead + after)

        listed(modes // LOT + t, work)
        return carry

    lax.fori_loop(0, CAP, lower, 0)

    if sources is NEAR:

        for w in range(windows):
            acc[here * windows + w] += rotate(
                jnp.dot(ham_ref[...], rho_ref[w], preferred_element_type=F32)
            )

    def leave(r, carry):
        for w in range(windows):
            for shift, out_ref in enumerate(out_refs):
                block = lax.rem(group + shift, blocks) * share
                out_ref[r - begin, w] = acc[r * windows + w, pl.ds(pl.multiple_of(block, share), share), :]
        return carry

    lax.fori_loop(begin, end, leave, 0)


def terms(sources, part, spot, lists, coup_re, coup_im, states, maps_wide, head_cols, rho):
    modes = maps_wide.shape[0] - 1
    windows, share, lanes = rho.shape
    width = head_cols.shape[0]
    return pl.pallas_call(
        functools.partial(terms_kernel, sources, modes, windows, part),
        in_specs=[SMEM] * 4 + [HBM] * len(sources) + [VMEM] * 3,
        out_specs=[VMEM] * (width // share),
        out_shape=[jax.ShapeDtypeStruct((part[1] - part[0], windows, share, lanes), F32)] * (width // share),
        scratch_shapes=[
            pltpu.VMEM((len(sources) * SPAN, width, lanes), BF16),
            pltpu.VMEM((RINGS * windows + 1, width, lanes), F32),
            pltpu.SemaphoreType.DMA((len(sources),)),
        ],
        compiler_params=pltpu.CompilerParams(vmem_limit_bytes=28 * 2**20),
        cost_estimate=pl.CostEstimate(flops=10**9, bytes_accessed=10 * 2**20, transcendentals=0),
    )(spot, lists, coup_re, coup_im, *[states[n] for n, _, _ in sources], maps_wide, head_cols, rho)


def lists_of(steps, parts, modes, spot_ref, heard_ref, out_ref):
    core, along, across, group = spot_ref[0], spot_ref[1], spot_ref[2], spot_ref[3]
    pairs = heard_ref.shape[1]
    windows = pairs // RINGS

    def locate(places):
        owner = lax.shift_right_logical(places * 171, 9)
        z, y, c = lax.shift_right_logical(owner, 4), lax.shift_right_logical(owner, 1) & 7, owner & 1
        off = (jnp.where(core == 0, z, y) - along) & (RINGS - 1)
        source = jnp.full_like(off, -1)
        for n, (_, _, step) in enumerate(steps):
            source = jnp.where(off == -step % RINGS, n, source)
        mine = (jnp.where(core == 0, y, z) == across) & (source >= 0)
        kind = jnp.where(c == core, 0, 1)
        lanes = lax.broadcasted_iota(jnp.int32, places.shape, 1)
        receiver = lax.shift_right_logical(lanes, windows.bit_length() - 1)
        return mine, ((source * 2 + kind) * CAP + places - owner * CAP) * RINGS + receiver

    def square(n, axis):
        return lax.broadcasted_iota(jnp.int32, (n, n), axis)

    def ones(mask):
        return jnp.where(mask, 1.0, 0.0)

    mine, row = locate(heard_ref[:modes])
    ids = lax.broadcasted_iota(jnp.int32, mine.shape, 0)
    below = ones(square(modes, 0) > square(modes, 1))
    rank = jnp.dot(below, ones(mine), preferred_element_type=F32).astype(jnp.int32)
    rank = jnp.where(mine, rank, -1)
    count = jnp.sum(ones(mine), axis=0, keepdims=True)
    value = (ids * 512 + row - modes * 512).astype(F32)
    for n in range(modes):
        found = jnp.sum(jnp.where(rank == n, value, 0.0), axis=0, keepdims=True)
        out_ref[n:n + 1] = found.astype(jnp.int32) + modes * 512

    mine, row = locate(heard_ref[modes:modes + CAP])
    local = heard_ref[modes + CAP:modes + 2 * CAP] - group * modes
    live = mine & (local >= 0) & (local < modes)
    out_ref[modes:modes + CAP] = jnp.where(live, local * 512 + row, 0)

    first = lax.broadcasted_iota(jnp.int32, (1, pairs), 1)
    flags = []
    for begin, end in parts:
        inside = (first >= begin * windows) & (first < end * windows)
        for n in range(modes // LOT):
            flags.append(ones(inside & (count > n * LOT)))
        for t in range(CAP):
            flags.append(ones(inside & live[t:t + 1]))
    total = len(flags)
    flags = jnp.concatenate(flags + [jnp.zeros((pairs - total, pairs), F32)], axis=0)
    turned = (((1,), (1,)), ((), ()))
    down, over = square(pairs, 0), square(pairs, 1)
    chosen = lax.dot_general(ones(down == over), flags, turned, preferred_element_type=F32)
    order = lax.dot_general(ones(down > over), flags, turned, preferred_element_type=F32)
    order = jnp.where(chosen > 0.5, order, -1.0)
    numbers = (down - pairs).astype(F32)
    lanes = over.astype(F32)
    for n in range(total):
        found = jnp.sum(jnp.where(order[:, n:n + 1] == lanes, numbers, 0.0), axis=0, keepdims=True)
        out_ref[modes + CAP + n:modes + CAP + n + 1] = found.astype(jnp.int32) + pairs
    sums = lax.dot_general(jnp.ones((8, pairs), F32), flags, turned, preferred_element_type=F32)
    last = out_ref.shape[0] - 1
    out_ref[last:last + 1] = sums[:1].astype(jnp.int32)


def lists_kernel(kinds, modes, spot_ref, *refs):
    for (steps, parts), heard_ref, out_ref in zip(kinds, refs[:len(kinds)], refs[len(kinds):], strict=True):
        lists_of(steps, parts, modes, spot_ref, heard_ref, out_ref)


def use_lists(kinds, modes, spot, heard):
    rows = [modes + CAP + len(parts) * (modes // LOT + CAP) + 1 for _, parts in kinds]
    return pl.pallas_call(
        functools.partial(lists_kernel, kinds, modes),
        in_specs=[SMEM] + [VMEM] * len(kinds),
        out_specs=[VMEM] * len(kinds),
        out_shape=[jax.ShapeDtypeStruct((n + -n % 8, heard[0].shape[1]), jnp.int32) for n in rows],
        compiler_params=pltpu.CompilerParams(vmem_limit_bytes=8 * 2**20),
        cost_estimate=pl.CostEstimate(flops=10**7, bytes_accessed=2**18, transcendentals=0),
    )(spot, *heard)


def say_kernel(spot_ref, up_ref, down_ref, tri_ref, out_ref):
    windows, modes = up_ref.shape
    shape = (windows, out_ref.shape[2])
    lanes = lax.broadcasted_iota(jnp.int32, shape, 1)
    row = lax.broadcasted_iota(jnp.int32, shape, 0)
    place = jnp.where(lanes == spot_ref[2] * windows + row, 1.0, 0.0)

    def put(values, axis):
        def half(part):
            return lax.dot_general(
                part.astype(F32), place, (((axis,), (0,)), ((), ())), preferred_element_type=F32
            )

        high = lax.shift_right_logical(values, 5)
        return (half(high) * 32.0 + half(values & 31)).astype(jnp.int32)

    up, down, tri = put(up_ref[...], 0), put(down_ref[...], 1), put(tri_ref[...], 1)
    spare = jnp.zeros((out_ref.shape[1] - modes - 2 * CAP, shape[1]), jnp.int32)
    whole = jnp.concatenate([up, down, tri, spare], axis=0)
    for n in range(RINGS):
        out_ref[n] = whole


def say(spot, use_up, use_down, modes_tri):
    windows, modes = use_up.shape
    rows = modes + 2 * CAP
    return pl.pallas_call(
        say_kernel,
        in_specs=[SMEM, VMEM, VMEM, VMEM],
        out_specs=VMEM,
        out_shape=jax.ShapeDtypeStruct((RINGS, rows + -rows % 8, RINGS * windows), jnp.int32),
        cost_estimate=pl.CostEstimate(flops=10**6, bytes_accessed=2**18, transcendentals=0),
    )(spot, use_up, use_down.T, modes_tri.T)


def over_groups(parts):
    count = len(parts)
    total = parts[0]
    for shift in (2, 1, 3):
        ring = [(i, (i + shift) % count) for i in range(count)]
        total = total + lax.ppermute(parts[shift].astype(LINK), "grp", ring).astype(F32)
    return total


def on_device(
    states, send_slot, window_tier_states, modes_tri, use_up, use_down,
    hamiltonian, coupling, coup_re, coup_im, decay_rate,
):
    width = hamiltonian.shape[0]
    windows, share = window_tier_states.shape[:2]
    modes = coupling.shape[0]
    group = lax.axis_index("grp").astype(jnp.int32)
    index = lax.axis_index("ado").astype(jnp.int32)
    core, z, y = index & 1, index >> 4, (index >> 1) & 7
    along = jnp.where(core == 0, z, y)
    across = jnp.where(core == 0, y, z)

    spot = jnp.stack([core, along, across, group])

    said = say(spot, use_up, use_down, modes_tri)
    said, slots, store = lax.optimization_barrier((said, send_slot[0, 0], states[0, 0]))
    heard = lax.all_to_all(
        said, "ado", split_axis=0, concat_axis=0, tiled=True, axis_index_groups=DELIVER
    )
    slots = jnp.transpose(slots).reshape(-1)
    sib_store = lax.ppermute(store, "ado", SIBLING)
    sib_slots = lax.ppermute(slots, "ado", SIBLING)
    heard, slots = lax.optimization_barrier((jnp.sum(heard, axis=0), slots))
    heard_far = lax.ppermute(heard, "ado", onward(4))
    picked = pick(spot, slots, sib_slots, store, sib_store)
    maps_wide = jnp.concatenate([doubled(coupling), jnp.zeros((1, 2 * width, 2 * width), BF16)], axis=0)
    head_cols = lax.dynamic_slice_in_dim(hamiltonian, group * share, share, 1)
    shared = (maps_wide, head_cols, window_tier_states)
    picked, heard, heard_far, shared = lax.optimization_barrier((picked, heard, heard_far, shared))

    sent = [
        block if step == 0 else lax.ppermute(block, "ado", onward(step))
        for (step, _), block in zip(SENDS, picked, strict=True)
    ]
    kinds = ((FAR, ((0, RINGS),)), (NEAR, ((0, RINGS),)))
    far_lists, near_lists = use_lists(kinds, modes, spot, (heard_far, heard))

    far = terms(FAR, (0, RINGS, 0), spot, far_lists, coup_re, coup_im, sent, *shared)
    far, near_lists = lax.optimization_barrier((far, near_lists))
    far = lax.ppermute(over_groups(far).astype(LINK), "ado", onward(4))
    near = over_groups(terms(NEAR, (0, RINGS, 0), spot, near_lists, coup_re, coup_im, sent, *shared))
    summed = lax.all_to_all(
        (near + far.astype(F32)).astype(LINK), "ado", split_axis=0, concat_axis=0, tiled=True,
        axis_index_groups=DELIVER,
    )

    ham_wide = doubled(hamiltonian)
    right_part = jnp.einsum("wab,bc->wac", window_tier_states, ham_wide, preferred_element_type=F32)
    every_mode = jnp.arange(decay_rate.shape[0], dtype=jnp.int32)
    hits = modes_tri[:, :, None] == every_mode
    damping = jnp.sum(jnp.where(hits, decay_rate, 0.0), axis=(1, 2))
    own = rotate(right_part) + damping[:, None, None] * window_tier_states.astype(F32)
    return STEP_WEIGHT * (jnp.sum(summed.astype(F32), axis=0) - own)


def solution(mesh):
    in_specs = (
        P("grp", "ado", None, None, None),
        P("grp", "ado", None, None),
        P("ado", "grp", None),
        P("ado", None),
        P("ado", "grp"),
        P("ado", None),
        P(),
        P("grp", None, None),
        P("grp"),
        P("grp"),
        P(),
    )
    out_specs = P("ado", "grp", None)
    return jax.shard_map(
        on_device, mesh=mesh, in_specs=in_specs, out_specs=out_specs, check_vma=False
    )
```

```python
import functools

import jax
import jax.numpy as jnp
from jax import lax
from jax.experimental import pallas as pl
from jax.experimental.pallas import tpu as pltpu
from jax.sharding import PartitionSpec as P

STEP_WEIGHT = 0.5
F32 = jnp.float32
BF16 = jnp.bfloat16
LINK = jnp.float16
VMEM = pl.BlockSpec(memory_space=pltpu.VMEM)
SMEM = pl.BlockSpec(memory_space=pltpu.SMEM)
HBM = pl.BlockSpec(memory_space=pltpu.HBM)


def doubled(matrices):
    empty = jnp.zeros_like(matrices)
    upper_half = jnp.concatenate([matrices, empty], axis=-1)
    lower_half = jnp.concatenate([empty, matrices], axis=-1)
    return jnp.concatenate([upper_half, lower_half], axis=-2)


def rotate(parts):
    width = parts.shape[-1] // 2
    return jnp.concatenate([parts[..., width:], -parts[..., :width]], axis=-1)


RINGS = 8
CAP = 3
LOT = 4
SPAN = 2 * CAP * RINGS
SENDS = ((1, (-3,)), (-1, (3,)), (2, (2,)), (-2, (-2,)), (1, (1,)), (-1, (-1,)), (0, (4, 0)))
FAR = ((0, 0, 1), (1, 0, -1), (6, 0, 0))
NEAR = ((2, 0, 2), (3, 0, -2), (4, 0, 1), (5, 0, -1), (6, 1, 0))
SIBLING = [(i, i ^ 1) for i in range(2 * RINGS * RINGS)]


def device(core, along, across):
    along, across = along % RINGS, across % RINGS
    return along * 16 + across * 2 if core == 0 else across * 16 + along * 2 + 1


def onward(step):
    return [
        (device(c, a, b), device(c, a + step, b)) for c in range(2) for a in range(RINGS) for b in range(RINGS)
    ]


DELIVER = [[device(c, a, b) for b in range(RINGS)] for c in range(2) for a in range(RINGS)]


def pick_kernel(spot_ref, own_slot, sib_slot, own_ref, sib_hbm, *refs):
    out_refs, (sib_ref, sem) = refs[:-2], refs[-2:]
    copy = pltpu.make_async_copy(sib_hbm, sib_ref, sem)
    copy.start()
    core, along = spot_ref[0], spot_ref[1]
    far = jnp.where(core == 0, 16, 2)
    near = jnp.where(core == 0, 2, 16)
    count = own_slot.shape[0] // CAP
    for kind, (slots, store) in enumerate(((own_slot, own_ref), (sib_slot, sib_ref))):
        if kind == 1:
            copy.wait()
        for (_, group), out_ref in zip(SENDS, out_refs, strict=True):
            for place, ahead in enumerate(group):
                first = lax.rem(along + ahead + RINGS, RINGS) * far + core
                for c in range(CAP):
                    for r in range(RINGS):
                        slot = slots[c * count + first + r * near]
                        row = place * SPAN + kind * CAP * RINGS + c * RINGS + r
                        out_ref[row] = store[jnp.maximum(slot, 0)]


def pick(spot, own_slots, sib_slots, own, sib):
    tile = own.shape[1:]
    return pl.pallas_call(
        pick_kernel,
        in_specs=[SMEM, SMEM, SMEM, VMEM, HBM],
        out_specs=[VMEM] * len(SENDS),
        out_shape=[jax.ShapeDtypeStruct((len(group) * SPAN,) + tile, own.dtype) for _, group in SENDS],
        scratch_shapes=[pltpu.VMEM(own.shape, own.dtype), pltpu.SemaphoreType.DMA],
        compiler_params=pltpu.CompilerParams(vmem_limit_bytes=24 * 2**20),
        cost_estimate=pl.CostEstimate(flops=0, bytes_accessed=10 * 2**20, transcendentals=0),
    )(spot, own_slots, sib_slots, own, sib)


def terms_kernel(sources, modes, windows, part, spot_ref, list_ref, re_ref, im_ref, *refs):
    count = len(sources)
    state_refs, (wide_ref, ham_ref, rho_ref) = refs[:count], refs[count:count + 3]
    out_refs, (flat, acc, sems) = refs[count + 3:-3], refs[-3:]
    here, group = spot_ref[2], spot_ref[3]
    share = rho_ref.shape[1]
    width = ham_ref.shape[0]
    pairs = RINGS * windows
    blocks = width // share
    begin, end, slot = part
    levels = modes // LOT + CAP
    downs, extra, counts = modes, modes + CAP + slot * levels, list_ref.shape[0] - 1

    copies = [
        pltpu.make_async_copy(
            state_refs[n].at[pl.ds(place * SPAN, SPAN)], flat.at[pl.ds(n * SPAN, SPAN)], sems.at[n]
        )
        for n, (_, place, _) in enumerate(sources)
    ]
    for copy in copies:
        copy.start()
    for copy in copies:
        copy.wait()

    def lot(pair, base):
        entries = [list_ref[base + n, pair] for n in range(LOT)]
        maps = [lax.shift_right_logical(e, 9) for e in entries]
        tiles = [flat[e & 511] for e in entries]
        rows = [
            wide_ref[maps[n], :width, :] + wide_ref[maps[n + 1], width:, :] for n in range(0, LOT, 2)
        ]
        left = jnp.dot(
            jnp.concatenate(rows, axis=1), jnp.concatenate(tiles, axis=0), preferred_element_type=F32
        )
        right = jnp.dot(
            jnp.concatenate(tiles, axis=1),
            jnp.concatenate([wide_ref[m] for m in maps], axis=0),
            preferred_element_type=F32,
        )
        return rotate(left - right)

    together = 16

    def first(index, carry):
        for j in range(together):
            pair = index * together + j
            acc[pair] = lot(pair, 0)
        return carry

    lax.fori_loop(begin * windows // together, end * windows // together, first, 0)

    def listed(level, work):
        def some(index, carry):
            found = [list_ref[extra + level, index * 4 + j] for j in range(4)]
            values = [work(jnp.minimum(pair, pairs - 1)) for pair in found]
            for pair, value in zip(found, values, strict=True):
                acc[pair] += value
            return carry

        lax.fori_loop(0, lax.shift_right_logical(list_ref[counts, slot * levels + level] + 3, 2), some, 0)

    def more(level, carry):
        listed(level, lambda pair: lot(pair, level * LOT))
        return carry

    lax.fori_loop(1, modes // LOT, more, 0)

    def lower(t, carry):
        def work(pair):
            entry = list_ref[downs + t, pair]
            mode = lax.shift_right_logical(entry, 9)
            state = flat[entry & 511]
            wide = wide_ref[mode]
            ahead = jnp.dot(wide[:width, :width], state, preferred_element_type=F32)
            after = jnp.dot(state, wide, preferred_element_type=F32)
            return re_ref[mode] * rotate(ahead - after) + im_ref[mode] * (ahead + after)

        listed(modes // LOT + t, work)
        return carry

    lax.fori_loop(0, CAP, lower, 0)

    if sources is NEAR:

        for w in range(windows):
            acc[here * windows + w] += rotate(
                jnp.dot(ham_ref[...], rho_ref[w], preferred_element_type=F32)
            )

    def leave(r, carry):
        for w in range(windows):
            for shift, out_ref in enumerate(out_refs):
                block = lax.rem(group + shift, blocks) * share
                out_ref[r - begin, w] = acc[r * windows + w, pl.ds(pl.multiple_of(block, share), share), :]
        return carry

    lax.fori_loop(begin, end, leave, 0)


def terms(sources, part, spot, lists, coup_re, coup_im, states, maps_wide, head_cols, rho):
    modes = maps_wide.shape[0] - 1
    windows, share, lanes = rho.shape
    width = head_cols.shape[0]
    return pl.pallas_call(
        functools.partial(terms_kernel, sources, modes, windows, part),
        in_specs=[SMEM] * 4 + [HBM] * len(sources) + [VMEM] * 3,
        out_specs=[VMEM] * (width // share),
        out_shape=[jax.ShapeDtypeStruct((part[1] - part[0], windows, share, lanes), F32)] * (width // share),
        scratch_shapes=[
            pltpu.VMEM((len(sources) * SPAN, width, lanes), BF16),
            pltpu.VMEM((RINGS * windows + 1, width, lanes), F32),
            pltpu.SemaphoreType.DMA((len(sources),)),
        ],
        compiler_params=pltpu.CompilerParams(vmem_limit_bytes=28 * 2**20),
        cost_estimate=pl.CostEstimate(flops=10**9, bytes_accessed=10 * 2**20, transcendentals=0),
    )(spot, lists, coup_re, coup_im, *[states[n] for n, _, _ in sources], maps_wide, head_cols, rho)


def lists_of(steps, parts, modes, spot_ref, heard_ref, out_ref):
    core, along, across, group = spot_ref[0], spot_ref[1], spot_ref[2], spot_ref[3]
    pairs = heard_ref.shape[1]
    windows = pairs // RINGS

    def locate(places):
        owner = lax.shift_right_logical(places * 171, 9)
        z, y, c = lax.shift_right_logical(owner, 4), lax.shift_right_logical(owner, 1) & 7, owner & 1
        off = (jnp.where(core == 0, z, y) - along) & (RINGS - 1)
        source = jnp.full_like(off, -1)
        for n, (_, _, step) in enumerate(steps):
            source = jnp.where(off == -step % RINGS, n, source)
        mine = (jnp.where(core == 0, y, z) == across) & (source >= 0)
        kind = jnp.where(c == core, 0, 1)
        lanes = lax.broadcasted_iota(jnp.int32, places.shape, 1)
        receiver = lax.shift_right_logical(lanes, windows.bit_length() - 1)
        return mine, ((source * 2 + kind) * CAP + places - owner * CAP) * RINGS + receiver

    def square(n, axis):
        return lax.broadcasted_iota(jnp.int32, (n, n), axis)

    def ones(mask):
        return jnp.where(mask, 1.0, 0.0)

    mine, row = locate(heard_ref[:modes])
    ids = lax.broadcasted_iota(jnp.int32, mine.shape, 0)
    below = ones(square(modes, 0) > square(modes, 1))
    rank = jnp.dot(below, ones(mine), preferred_element_type=F32).astype(jnp.int32)
    rank = jnp.where(mine, rank, -1)
    count = jnp.sum(ones(mine), axis=0, keepdims=True)
    value = (ids * 512 + row - modes * 512).astype(F32)
    for n in range(modes):
        found = jnp.sum(jnp.where(rank == n, value, 0.0), axis=0, keepdims=True)
        out_ref[n:n + 1] = found.astype(jnp.int32) + modes * 512

    mine, row = locate(heard_ref[modes:modes + CAP])
    local = heard_ref[modes + CAP:modes + 2 * CAP] - group * modes
    live = mine & (local >= 0) & (local < modes)
    out_ref[modes:modes + CAP] = jnp.where(live, local * 512 + row, 0)

    first = lax.broadcasted_iota(jnp.int32, (1, pairs), 1)
    flags = []
    for begin, end in parts:
        inside = (first >= begin * windows) & (first < end * windows)
        for n in range(modes // LOT):
            flags.append(ones(inside & (count > n * LOT)))
        for t in range(CAP):
            flags.append(ones(inside & live[t:t + 1]))
    total = len(flags)
    flags = jnp.concatenate(flags + [jnp.zeros((pairs - total, pairs), F32)], axis=0)
    turned = (((1,), (1,)), ((), ()))
    down, over = square(pairs, 0), square(pairs, 1)
    chosen = lax.dot_general(ones(down == over), flags, turned, preferred_element_type=F32)
    order = lax.dot_general(ones(down > over), flags, turned, preferred_element_type=F32)
    order = jnp.where(chosen > 0.5, order, -1.0)
    numbers = (down - pairs).astype(F32)
    lanes = over.astype(F32)
    for n in range(total):
        found = jnp.sum(jnp.where(order[:, n:n + 1] == lanes, numbers, 0.0), axis=0, keepdims=True)
        out_ref[modes + CAP + n:modes + CAP + n + 1] = found.astype(jnp.int32) + pairs
    sums = lax.dot_general(jnp.ones((8, pairs), F32), flags, turned, preferred_element_type=F32)
    last = out_ref.shape[0] - 1
    out_ref[last:last + 1] = sums[:1].astype(jnp.int32)


def lists_kernel(kinds, modes, spot_ref, *refs):
    for (steps, parts), heard_ref, out_ref in zip(kinds, refs[:len(kinds)], refs[len(kinds):], strict=True):
        lists_of(steps, parts, modes, spot_ref, heard_ref, out_ref)


def use_lists(kinds, modes, spot, heard):
    rows = [modes + CAP + len(parts) * (modes // LOT + CAP) + 1 for _, parts in kinds]
    return pl.pallas_call(
        functools.partial(lists_kernel, kinds, modes),
        in_specs=[SMEM] + [VMEM] * len(kinds),
        out_specs=[VMEM] * len(kinds),
        out_shape=[jax.ShapeDtypeStruct((n + -n % 8, heard[0].shape[1]), jnp.int32) for n in rows],
        compiler_params=pltpu.CompilerParams(vmem_limit_bytes=8 * 2**20),
        cost_estimate=pl.CostEstimate(flops=10**7, bytes_accessed=2**18, transcendentals=0),
    )(spot, *heard)


def say_kernel(spot_ref, up_ref, down_ref, tri_ref, out_ref):
    windows, modes = up_ref.shape
    shape = (windows, out_ref.shape[2])
    lanes = lax.broadcasted_iota(jnp.int32, shape, 1)
    row = lax.broadcasted_iota(jnp.int32, shape, 0)
    place = jnp.where(lanes == spot_ref[2] * windows + row, 1.0, 0.0)

    def put(values, axis):
        def half(part):
            return lax.dot_general(
                part.astype(F32), place, (((axis,), (0,)), ((), ())), preferred_element_type=F32
            )

        high = lax.shift_right_logical(values, 5)
        return (half(high) * 32.0 + half(values & 31)).astype(jnp.int32)

    up, down, tri = put(up_ref[...], 0), put(down_ref[...], 1), put(tri_ref[...], 1)
    spare = jnp.zeros((out_ref.shape[1] - modes - 2 * CAP, shape[1]), jnp.int32)
    whole = jnp.concatenate([up, down, tri, spare], axis=0)
    for n in range(RINGS):
        out_ref[n] = whole


def say(spot, use_up, use_down, modes_tri):
    windows, modes = use_up.shape
    rows = modes + 2 * CAP
    return pl.pallas_call(
        say_kernel,
        in_specs=[SMEM, VMEM, VMEM, VMEM],
        out_specs=VMEM,
        out_shape=jax.ShapeDtypeStruct((RINGS, rows + -rows % 8, RINGS * windows), jnp.int32),
        cost_estimate=pl.CostEstimate(flops=10**6, bytes_accessed=2**18, transcendentals=0),
    )(spot, use_up, use_down.T, modes_tri.T)


def over_groups(parts):
    count = len(parts)
    total = parts[0]
    for shift in (1, 3, 2):
        ring = [(i, (i + shift) % count) for i in range(count)]
        total = total + lax.ppermute(parts[shift].astype(LINK), "grp", ring).astype(F32)
    return total


def on_device(
    states, send_slot, window_tier_states, modes_tri, use_up, use_down,
    hamiltonian, coupling, coup_re, coup_im, decay_rate,
):
    width = hamiltonian.shape[0]
    windows, share = window_tier_states.shape[:2]
    modes = coupling.shape[0]
    group = lax.axis_index("grp").astype(jnp.int32)
    index = lax.axis_index("ado").astype(jnp.int32)
    core, z, y = index & 1, index >> 4, (index >> 1) & 7
    along = jnp.where(core == 0, z, y)
    across = jnp.where(core == 0, y, z)

    spot = jnp.stack([core, along, across, group])

    said = say(spot, use_up, use_down, modes_tri)
    said, slots, store = lax.optimization_barrier((said, send_slot[0, 0], states[0, 0]))
    heard = lax.all_to_all(
        said, "ado", split_axis=0, concat_axis=0, tiled=True, axis_index_groups=DELIVER
    )
    slots = jnp.transpose(slots).reshape(-1)
    sib_store = lax.ppermute(store, "ado", SIBLING)
    sib_slots = lax.ppermute(slots, "ado", SIBLING)
    heard, slots = lax.optimization_barrier((jnp.sum(heard, axis=0), slots))
    heard_far = lax.ppermute(heard, "ado", onward(4))
    picked = pick(spot, slots, sib_slots, store, sib_store)
    maps_wide = jnp.concatenate([doubled(coupling), jnp.zeros((1, 2 * width, 2 * width), BF16)], axis=0)
    head_cols = lax.dynamic_slice_in_dim(hamiltonian, group * share, share, 1)
    shared = (maps_wide, head_cols, window_tier_states)
    picked, heard, heard_far, shared = lax.optimization_barrier((picked, heard, heard_far, shared))

    sent = [
        block if step == 0 else lax.ppermute(block, "ado", onward(step))
        for (step, _), block in zip(SENDS, picked, strict=True)
    ]
    kinds = ((FAR, ((0, RINGS),)), (NEAR, ((0, RINGS),)))
    far_lists, near_lists = use_lists(kinds, modes, spot, (heard_far, heard))

    far = terms(FAR, (0, RINGS, 0), spot, far_lists, coup_re, coup_im, sent, *shared)
    far, near_lists = lax.optimization_barrier((far, near_lists))
    far = lax.ppermute(over_groups(far).astype(LINK), "ado", onward(4))
    near = over_groups(terms(NEAR, (0, RINGS, 0), spot, near_lists, coup_re, coup_im, sent, *shared))
    summed = lax.all_to_all(
        (near + far.astype(F32)).astype(LINK), "ado", split_axis=0, concat_axis=0, tiled=True,
        axis_index_groups=DELIVER,
    )

    ham_wide = doubled(hamiltonian)
    right_part = jnp.einsum("wab,bc->wac", window_tier_states, ham_wide, preferred_element_type=F32)
    every_mode = jnp.arange(decay_rate.shape[0], dtype=jnp.int32)
    hits = modes_tri[:, :, None] == every_mode
    damping = jnp.sum(jnp.where(hits, decay_rate, 0.0), axis=(1, 2))
    own = rotate(right_part) + damping[:, None, None] * window_tier_states.astype(F32)
    return STEP_WEIGHT * (jnp.sum(summed.astype(F32), axis=0) - own)


def solution(mesh):
    in_specs = (
        P("grp", "ado", None, None, None),
        P("grp", "ado", None, None),
        P("ado", "grp", None),
        P("ado", None),
        P("ado", "grp"),
        P("ado", None),
        P(),
        P("grp", None, None),
        P("grp"),
        P("grp"),
        P(),
    )
    out_specs = P("ado", "grp", None)
    return jax.shard_map(
        on_device, mesh=mesh, in_specs=in_specs, out_specs=out_specs, check_vma=False
    )
```

```python
import functools

import jax
import jax.numpy as jnp
from jax import lax
from jax.experimental import pallas as pl
from jax.experimental.pallas import tpu as pltpu
from jax.sharding import PartitionSpec as P

STEP_WEIGHT = 0.5
F32 = jnp.float32
BF16 = jnp.bfloat16
LINK = jnp.float16
VMEM = pl.BlockSpec(memory_space=pltpu.VMEM)
SMEM = pl.BlockSpec(memory_space=pltpu.SMEM)
HBM = pl.BlockSpec(memory_space=pltpu.HBM)


def doubled(matrices):
    empty = jnp.zeros_like(matrices)
    upper_half = jnp.concatenate([matrices, empty], axis=-1)
    lower_half = jnp.concatenate([empty, matrices], axis=-1)
    return jnp.concatenate([upper_half, lower_half], axis=-2)


def rotate(parts):
    width = parts.shape[-1] // 2
    return jnp.concatenate([parts[..., width:], -parts[..., :width]], axis=-1)


RINGS = 8
CAP = 3
LOT = 4
SPAN = 2 * CAP * RINGS
SENDS = ((1, (-3,)), (-1, (3,)), (2, (2,)), (-2, (-2,)), (1, (1,)), (-1, (-1,)), (0, (4, 0)))
FAR = ((0, 0, 1), (1, 0, -1), (6, 0, 0))
NEAR = ((2, 0, 2), (3, 0, -2), (4, 0, 1), (5, 0, -1), (6, 1, 0))
SIBLING = [(i, i ^ 1) for i in range(2 * RINGS * RINGS)]


def device(core, along, across):
    along, across = along % RINGS, across % RINGS
    return along * 16 + across * 2 if core == 0 else across * 16 + along * 2 + 1


def onward(step):
    return [
        (device(c, a, b), device(c, a + step, b)) for c in range(2) for a in range(RINGS) for b in range(RINGS)
    ]


DELIVER = [[device(c, a, b) for b in range(RINGS)] for c in range(2) for a in range(RINGS)]


def pick_kernel(spot_ref, own_slot, sib_slot, own_ref, sib_hbm, *refs):
    out_refs, (sib_ref, sem) = refs[:-2], refs[-2:]
    copy = pltpu.make_async_copy(sib_hbm, sib_ref, sem)
    copy.start()
    core, along = spot_ref[0], spot_ref[1]
    far = jnp.where(core == 0, 16, 2)
    near = jnp.where(core == 0, 2, 16)
    count = own_slot.shape[0] // CAP
    for kind, (slots, store) in enumerate(((own_slot, own_ref), (sib_slot, sib_ref))):
        if kind == 1:
            copy.wait()
        for (_, group), out_ref in zip(SENDS, out_refs, strict=True):
            for place, ahead in enumerate(group):
                first = lax.rem(along + ahead + RINGS, RINGS) * far + core
                for c in range(CAP):
                    for r in range(RINGS):
                        slot = slots[c * count + first + r * near]
                        row = place * SPAN + kind * CAP * RINGS + c * RINGS + r
                        out_ref[row] = store[jnp.maximum(slot, 0)]


def pick(spot, own_slots, sib_slots, own, sib):
    tile = own.shape[1:]
    return pl.pallas_call(
        pick_kernel,
        in_specs=[SMEM, SMEM, SMEM, VMEM, HBM],
        out_specs=[VMEM] * len(SENDS),
        out_shape=[jax.ShapeDtypeStruct((len(group) * SPAN,) + tile, own.dtype) for _, group in SENDS],
        scratch_shapes=[pltpu.VMEM(own.shape, own.dtype), pltpu.SemaphoreType.DMA],
        compiler_params=pltpu.CompilerParams(vmem_limit_bytes=24 * 2**20),
        cost_estimate=pl.CostEstimate(flops=0, bytes_accessed=10 * 2**20, transcendentals=0),
    )(spot, own_slots, sib_slots, own, sib)


def terms_kernel(sources, modes, windows, part, spot_ref, list_ref, re_ref, im_ref, *refs):
    count = len(sources)
    state_refs, (wide_ref, ham_ref, rho_ref) = refs[:count], refs[count:count + 3]
    out_refs, (flat, acc, sems) = refs[count + 3:-3], refs[-3:]
    here, group = spot_ref[2], spot_ref[3]
    share = rho_ref.shape[1]
    width = ham_ref.shape[0]
    pairs = RINGS * windows
    blocks = width // share
    begin, end, slot = part
    levels = modes // LOT + CAP
    downs, extra, counts = modes, modes + CAP + slot * levels, list_ref.shape[0] - 1

    copies = [
        pltpu.make_async_copy(
            state_refs[n].at[pl.ds(place * SPAN, SPAN)], flat.at[pl.ds(n * SPAN, SPAN)], sems.at[n]
        )
        for n, (_, place, _) in enumerate(sources)
    ]
    for copy in copies:
        copy.start()
    for copy in copies:
        copy.wait()

    def lot(pair, base):
        entries = [list_ref[base + n, pair] for n in range(LOT)]
        maps = [lax.shift_right_logical(e, 9) for e in entries]
        tiles = [flat[e & 511] for e in entries]
        rows = [
            wide_ref[maps[n], :width, :] + wide_ref[maps[n + 1], width:, :] for n in range(0, LOT, 2)
        ]
        left = jnp.dot(
            jnp.concatenate(rows, axis=1), jnp.concatenate(tiles, axis=0), preferred_element_type=F32
        )
        right = jnp.dot(
            jnp.concatenate(tiles, axis=1),
            jnp.concatenate([wide_ref[m] for m in maps], axis=0),
            preferred_element_type=F32,
        )
        return rotate(left - right)

    together = 16

    def first(index, carry):
        for j in range(together):
            pair = index * together + j
            acc[pair] = lot(pair, 0)
        return carry

    lax.fori_loop(begin * windows // together, end * windows // together, first, 0)

    def listed(level, work):
        def some(index, carry):
            found = [list_ref[extra + level, index * 4 + j] for j in range(4)]
            values = [work(jnp.minimum(pair, pairs - 1)) for pair in found]
            for pair, value in zip(found, values, strict=True):
                acc[pair] += value
            return carry

        lax.fori_loop(0, lax.shift_right_logical(list_ref[counts, slot * levels + level] + 3, 2), some, 0)

    def more(level, carry):
        listed(level, lambda pair: lot(pair, level * LOT))
        return carry

    lax.fori_loop(1, modes // LOT, more, 0)

    def lower(t, carry):
        def work(pair):
            entry = list_ref[downs + t, pair]
            mode = lax.shift_right_logical(entry, 9)
            state = flat[entry & 511]
            wide = wide_ref[mode]
            ahead = jnp.dot(wide[:width, :width], state, preferred_element_type=F32)
            after = jnp.dot(state, wide, preferred_element_type=F32)
            return re_ref[mode] * rotate(ahead - after) + im_ref[mode] * (ahead + after)

        listed(modes // LOT + t, work)
        return carry

    lax.fori_loop(0, CAP, lower, 0)

    if sources is NEAR:

        for w in range(windows):
            acc[here * windows + w] += rotate(
                jnp.dot(ham_ref[...], rho_ref[w], preferred_element_type=F32)
            )

    def leave(r, carry):
        for w in range(windows):
            for shift, out_ref in enumerate(out_refs):
                block = lax.rem(group + shift, blocks) * share
                out_ref[r - begin, w] = acc[r * windows + w, pl.ds(pl.multiple_of(block, share), share), :]
        return carry

    lax.fori_loop(begin, end, leave, 0)


def terms(sources, part, spot, lists, coup_re, coup_im, states, maps_wide, head_cols, rho):
    modes = maps_wide.shape[0] - 1
    windows, share, lanes = rho.shape
    width = head_cols.shape[0]
    return pl.pallas_call(
        functools.partial(terms_kernel, sources, modes, windows, part),
        in_specs=[SMEM] * 4 + [HBM] * len(sources) + [VMEM] * 3,
        out_specs=[VMEM] * (width // share),
        out_shape=[jax.ShapeDtypeStruct((part[1] - part[0], windows, share, lanes), F32)] * (width // share),
        scratch_shapes=[
            pltpu.VMEM((len(sources) * SPAN, width, lanes), BF16),
            pltpu.VMEM((RINGS * windows + 1, width, lanes), F32),
            pltpu.SemaphoreType.DMA((len(sources),)),
        ],
        compiler_params=pltpu.CompilerParams(vmem_limit_bytes=28 * 2**20),
        cost_estimate=pl.CostEstimate(flops=10**9, bytes_accessed=10 * 2**20, transcendentals=0),
    )(spot, lists, coup_re, coup_im, *[states[n] for n, _, _ in sources], maps_wide, head_cols, rho)


def lists_of(steps, parts, modes, spot_ref, heard_ref, out_ref):
    core, along, across, group = spot_ref[0], spot_ref[1], spot_ref[2], spot_ref[3]
    pairs = heard_ref.shape[1]
    windows = pairs // RINGS

    def locate(places):
        owner = lax.shift_right_logical(places * 171, 9)
        z, y, c = lax.shift_right_logical(owner, 4), lax.shift_right_logical(owner, 1) & 7, owner & 1
        off = (jnp.where(core == 0, z, y) - along) & (RINGS - 1)
        source = jnp.full_like(off, -1)
        for n, (_, _, step) in enumerate(steps):
            source = jnp.where(off == -step % RINGS, n, source)
        mine = (jnp.where(core == 0, y, z) == across) & (source >= 0)
        kind = jnp.where(c == core, 0, 1)
        lanes = lax.broadcasted_iota(jnp.int32, places.shape, 1)
        receiver = lax.shift_right_logical(lanes, windows.bit_length() - 1)
        return mine, ((source * 2 + kind) * CAP + places - owner * CAP) * RINGS + receiver

    def square(n, axis):
        return lax.broadcasted_iota(jnp.int32, (n, n), axis)

    def ones(mask):
        return jnp.where(mask, 1.0, 0.0)

    mine, row = locate(heard_ref[:modes])
    ids = lax.broadcasted_iota(jnp.int32, mine.shape, 0)
    below = ones(square(modes, 0) > square(modes, 1))
    rank = jnp.dot(below, ones(mine), preferred_element_type=F32).astype(jnp.int32)
    rank = jnp.where(mine, rank, -1)
    count = jnp.sum(ones(mine), axis=0, keepdims=True)
    value = (ids * 512 + row - modes * 512).astype(F32)
    for n in range(modes):
        found = jnp.sum(jnp.where(rank == n, value, 0.0), axis=0, keepdims=True)
        out_ref[n:n + 1] = found.astype(jnp.int32) + modes * 512

    mine, row = locate(heard_ref[modes:modes + CAP])
    local = heard_ref[modes + CAP:modes + 2 * CAP] - group * modes
    live = mine & (local >= 0) & (local < modes)
    out_ref[modes:modes + CAP] = jnp.where(live, local * 512 + row, 0)

    first = lax.broadcasted_iota(jnp.int32, (1, pairs), 1)
    flags = []
    for begin, end in parts:
        inside = (first >= begin * windows) & (first < end * windows)
        for n in range(modes // LOT):
            flags.append(ones(inside & (count > n * LOT)))
        for t in range(CAP):
            flags.append(ones(inside & live[t:t + 1]))
    total = len(flags)
    flags = jnp.concatenate(flags + [jnp.zeros((pairs - total, pairs), F32)], axis=0)
    turned = (((1,), (1,)), ((), ()))
    down, over = square(pairs, 0), square(pairs, 1)
    chosen = lax.dot_general(ones(down == over), flags, turned, preferred_element_type=F32)
    order = lax.dot_general(ones(down > over), flags, turned, preferred_element_type=F32)
    order = jnp.where(chosen > 0.5, order, -1.0)
    numbers = (down - pairs).astype(F32)
    lanes = over.astype(F32)
    for n in range(total):
        found = jnp.sum(jnp.where(order[:, n:n + 1] == lanes, numbers, 0.0), axis=0, keepdims=True)
        out_ref[modes + CAP + n:modes + CAP + n + 1] = found.astype(jnp.int32) + pairs
    sums = lax.dot_general(jnp.ones((8, pairs), F32), flags, turned, preferred_element_type=F32)
    last = out_ref.shape[0] - 1
    out_ref[last:last + 1] = sums[:1].astype(jnp.int32)


def lists_kernel(kinds, modes, spot_ref, *refs):
    for (steps, parts), heard_ref, out_ref in zip(kinds, refs[:len(kinds)], refs[len(kinds):], strict=True):
        lists_of(steps, parts, modes, spot_ref, heard_ref, out_ref)


def use_lists(kinds, modes, spot, heard):
    rows = [modes + CAP + len(parts) * (modes // LOT + CAP) + 1 for _, parts in kinds]
    return pl.pallas_call(
        functools.partial(lists_kernel, kinds, modes),
        in_specs=[SMEM] + [VMEM] * len(kinds),
        out_specs=[VMEM] * len(kinds),
        out_shape=[jax.ShapeDtypeStruct((n + -n % 8, heard[0].shape[1]), jnp.int32) for n in rows],
        compiler_params=pltpu.CompilerParams(vmem_limit_bytes=8 * 2**20),
        cost_estimate=pl.CostEstimate(flops=10**7, bytes_accessed=2**18, transcendentals=0),
    )(spot, *heard)


def say_kernel(spot_ref, up_ref, down_ref, tri_ref, out_ref):
    windows, modes = up_ref.shape
    shape = (windows, out_ref.shape[2])
    lanes = lax.broadcasted_iota(jnp.int32, shape, 1)
    row = lax.broadcasted_iota(jnp.int32, shape, 0)
    place = jnp.where(lanes == spot_ref[2] * windows + row, 1.0, 0.0)

    def put(values, axis):
        def half(part):
            return lax.dot_general(
                part.astype(F32), place, (((axis,), (0,)), ((), ())), preferred_element_type=F32
            )

        high = lax.shift_right_logical(values, 5)
        return (half(high) * 32.0 + half(values & 31)).astype(jnp.int32)

    up, down, tri = put(up_ref[...], 0), put(down_ref[...], 1), put(tri_ref[...], 1)
    spare = jnp.zeros((out_ref.shape[1] - modes - 2 * CAP, shape[1]), jnp.int32)
    whole = jnp.concatenate([up, down, tri, spare], axis=0)
    for n in range(RINGS):
        out_ref[n] = whole


def say(spot, use_up, use_down, modes_tri):
    windows, modes = use_up.shape
    rows = modes + 2 * CAP
    return pl.pallas_call(
        say_kernel,
        in_specs=[SMEM, VMEM, VMEM, VMEM],
        out_specs=VMEM,
        out_shape=jax.ShapeDtypeStruct((RINGS, rows + -rows % 8, RINGS * windows), jnp.int32),
        cost_estimate=pl.CostEstimate(flops=10**6, bytes_accessed=2**18, transcendentals=0),
    )(spot, use_up, use_down.T, modes_tri.T)


def over_groups(parts):
    count = len(parts)
    total = parts[0]
    for shift in (1, 3, 2):
        ring = [(i, (i + shift) % count) for i in range(count)]
        total = total + lax.ppermute(parts[shift].astype(LINK), "grp", ring).astype(F32)
    return total


def along_row(sums):
    sums = lax.all_to_all(
        sums.astype(LINK), "ado", split_axis=0, concat_axis=0, tiled=True, axis_index_groups=DELIVER
    )
    return jnp.sum(sums.astype(F32), axis=0)


def on_device(
    states, send_slot, window_tier_states, modes_tri, use_up, use_down,
    hamiltonian, coupling, coup_re, coup_im, decay_rate,
):
    width = hamiltonian.shape[0]
    windows, share = window_tier_states.shape[:2]
    modes = coupling.shape[0]
    group = lax.axis_index("grp").astype(jnp.int32)
    index = lax.axis_index("ado").astype(jnp.int32)
    core, z, y = index & 1, index >> 4, (index >> 1) & 7
    along = jnp.where(core == 0, z, y)
    across = jnp.where(core == 0, y, z)

    spot = jnp.stack([core, along, across, group])

    said = say(spot, use_up, use_down, modes_tri)
    said, slots, store = lax.optimization_barrier((said, send_slot[0, 0], states[0, 0]))
    heard = lax.all_to_all(
        said, "ado", split_axis=0, concat_axis=0, tiled=True, axis_index_groups=DELIVER
    )
    slots = jnp.transpose(slots).reshape(-1)
    sib_store = lax.ppermute(store, "ado", SIBLING)
    sib_slots = lax.ppermute(slots, "ado", SIBLING)
    heard, slots = lax.optimization_barrier((jnp.sum(heard, axis=0), slots))
    heard_far = lax.ppermute(heard, "ado", onward(4))
    picked = pick(spot, slots, sib_slots, store, sib_store)
    maps_wide = jnp.concatenate([doubled(coupling), jnp.zeros((1, 2 * width, 2 * width), BF16)], axis=0)
    head_cols = lax.dynamic_slice_in_dim(hamiltonian, group * share, share, 1)
    shared = (maps_wide, head_cols, window_tier_states)
    picked, heard, heard_far, shared = lax.optimization_barrier((picked, heard, heard_far, shared))

    sent = [
        block if step == 0 else lax.ppermute(block, "ado", onward(step))
        for (step, _), block in zip(SENDS, picked, strict=True)
    ]
    kinds = ((FAR, ((0, RINGS),)), (NEAR, ((0, RINGS),)))
    far_lists, near_lists = use_lists(kinds, modes, spot, (heard_far, heard))

    far = terms(FAR, (0, RINGS, 0), spot, far_lists, coup_re, coup_im, sent, *shared)
    far, near_lists = lax.optimization_barrier((far, near_lists))
    far = lax.ppermute(along_row(over_groups(far)), "ado", onward(4))
    near = terms(NEAR, (0, RINGS, 0), spot, near_lists, coup_re, coup_im, sent, *shared)
    near = along_row(over_groups(near))

    ham_wide = doubled(hamiltonian)
    right_part = jnp.einsum("wab,bc->wac", window_tier_states, ham_wide, preferred_element_type=F32)
    every_mode = jnp.arange(decay_rate.shape[0], dtype=jnp.int32)
    hits = modes_tri[:, :, None] == every_mode
    damping = jnp.sum(jnp.where(hits, decay_rate, 0.0), axis=(1, 2))
    own = rotate(right_part) + damping[:, None, None] * window_tier_states.astype(F32)
    return STEP_WEIGHT * (near + far - own)


def solution(mesh):
    in_specs = (
        P("grp", "ado", None, None, None),
        P("grp", "ado", None, None),
        P("ado", "grp", None),
        P("ado", None),
        P("ado", "grp"),
        P("ado", None),
        P(),
        P("grp", None, None),
        P("grp"),
        P("grp"),
        P(),
    )
    out_specs = P("ado", "grp", None)
    return jax.shard_map(
        on_device, mesh=mesh, in_specs=in_specs, out_specs=out_specs, check_vma=False
    )
```

```python
import functools

import jax
import jax.numpy as jnp
from jax import lax
from jax.experimental import pallas as pl
from jax.experimental.pallas import tpu as pltpu
from jax.sharding import PartitionSpec as P

STEP_WEIGHT = 0.5
F32 = jnp.float32
BF16 = jnp.bfloat16
LINK = jnp.float16
VMEM = pl.BlockSpec(memory_space=pltpu.VMEM)
SMEM = pl.BlockSpec(memory_space=pltpu.SMEM)
HBM = pl.BlockSpec(memory_space=pltpu.HBM)


def doubled(matrices):
    empty = jnp.zeros_like(matrices)
    upper_half = jnp.concatenate([matrices, empty], axis=-1)
    lower_half = jnp.concatenate([empty, matrices], axis=-1)
    return jnp.concatenate([upper_half, lower_half], axis=-2)


def rotate(parts):
    width = parts.shape[-1] // 2
    return jnp.concatenate([parts[..., width:], -parts[..., :width]], axis=-1)


RINGS = 8
CAP = 3
LOT = 4
SPAN = 2 * CAP * RINGS
SENDS = ((1, (-3,)), (-1, (3,)), (2, (2,)), (-2, (-2,)), (1, (1,)), (-1, (-1,)), (0, (4, 0)))
FAR = ((0, 0, 1), (1, 0, -1), (6, 0, 0))
NEAR = ((2, 0, 2), (3, 0, -2), (4, 0, 1), (5, 0, -1), (6, 1, 0))
SIBLING = [(i, i ^ 1) for i in range(2 * RINGS * RINGS)]


def device(core, along, across):
    along, across = along % RINGS, across % RINGS
    return along * 16 + across * 2 if core == 0 else across * 16 + along * 2 + 1


def onward(step):
    return [
        (device(c, a, b), device(c, a + step, b)) for c in range(2) for a in range(RINGS) for b in range(RINGS)
    ]


DELIVER = [[device(c, a, b) for b in range(RINGS)] for c in range(2) for a in range(RINGS)]


def pick_kernel(spot_ref, own_slot, sib_slot, own_ref, sib_hbm, *refs):
    out_refs, (sib_ref, sem) = refs[:-2], refs[-2:]
    copy = pltpu.make_async_copy(sib_hbm, sib_ref, sem)
    copy.start()
    core, along = spot_ref[0], spot_ref[1]
    far = jnp.where(core == 0, 16, 2)
    near = jnp.where(core == 0, 2, 16)
    count = own_slot.shape[0] // CAP
    for kind, (slots, store) in enumerate(((own_slot, own_ref), (sib_slot, sib_ref))):
        if kind == 1:
            copy.wait()
        for (_, group), out_ref in zip(SENDS, out_refs, strict=True):
            for place, ahead in enumerate(group):
                first = lax.rem(along + ahead + RINGS, RINGS) * far + core
                for c in range(CAP):
                    for r in range(RINGS):
                        slot = slots[c * count + first + r * near]
                        row = place * SPAN + kind * CAP * RINGS + c * RINGS + r
                        out_ref[row] = store[jnp.maximum(slot, 0)]


def pick(spot, own_slots, sib_slots, own, sib):
    tile = own.shape[1:]
    return pl.pallas_call(
        pick_kernel,
        in_specs=[SMEM, SMEM, SMEM, VMEM, HBM],
        out_specs=[VMEM] * len(SENDS),
        out_shape=[jax.ShapeDtypeStruct((len(group) * SPAN,) + tile, own.dtype) for _, group in SENDS],
        scratch_shapes=[pltpu.VMEM(own.shape, own.dtype), pltpu.SemaphoreType.DMA],
        compiler_params=pltpu.CompilerParams(vmem_limit_bytes=24 * 2**20),
        cost_estimate=pl.CostEstimate(flops=0, bytes_accessed=10 * 2**20, transcendentals=0),
    )(spot, own_slots, sib_slots, own, sib)


def terms_kernel(sources, modes, windows, part, spot_ref, list_ref, re_ref, im_ref, *refs):
    count = len(sources)
    state_refs, (wide_ref, ham_ref, rho_ref) = refs[:count], refs[count:count + 3]
    out_refs, (flat, acc, sems) = refs[count + 3:-3], refs[-3:]
    here, group = spot_ref[2], spot_ref[3]
    share = rho_ref.shape[1]
    width = ham_ref.shape[0]
    pairs = RINGS * windows
    blocks = width // share
    begin, end, slot = part
    levels = modes // LOT + CAP
    downs, extra, counts = modes, modes + CAP + slot * levels, list_ref.shape[0] - 1

    copies = [
        pltpu.make_async_copy(
            state_refs[n].at[pl.ds(place * SPAN, SPAN)], flat.at[pl.ds(n * SPAN, SPAN)], sems.at[n]
        )
        for n, (_, place, _) in enumerate(sources)
    ]
    for copy in copies:
        copy.start()
    for copy in copies:
        copy.wait()

    def lot(pair, base):
        entries = [list_ref[base + n, pair] for n in range(LOT)]
        maps = [lax.shift_right_logical(e, 9) for e in entries]
        tiles = [flat[e & 511] for e in entries]
        rows = [
            wide_ref[maps[n], :width, :] + wide_ref[maps[n + 1], width:, :] for n in range(0, LOT, 2)
        ]
        left = jnp.dot(
            jnp.concatenate(rows, axis=1), jnp.concatenate(tiles, axis=0), preferred_element_type=F32
        )
        right = jnp.dot(
            jnp.concatenate(tiles, axis=1),
            jnp.concatenate([wide_ref[m] for m in maps], axis=0),
            preferred_element_type=F32,
        )
        return rotate(left - right)

    together = 16

    def first(index, carry):
        for j in range(together):
            pair = index * together + j
            acc[pair] = lot(pair, 0)
        return carry

    lax.fori_loop(begin * windows // together, end * windows // together, first, 0)

    def listed(level, work):
        def some(index, carry):
            found = [list_ref[extra + level, index * 4 + j] for j in range(4)]
            values = [work(jnp.minimum(pair, pairs - 1)) for pair in found]
            for pair, value in zip(found, values, strict=True):
                acc[pair] += value
            return carry

        lax.fori_loop(0, lax.shift_right_logical(list_ref[counts, slot * levels + level] + 3, 2), some, 0)

    def more(level, carry):
        listed(level, lambda pair: lot(pair, level * LOT))
        return carry

    lax.fori_loop(1, modes // LOT, more, 0)

    def lower(t, carry):
        def work(pair):
            entry = list_ref[downs + t, pair]
            mode = lax.shift_right_logical(entry, 9)
            state = flat[entry & 511]
            wide = wide_ref[mode]
            ahead = jnp.dot(wide[:width, :width], state, preferred_element_type=F32)
            after = jnp.dot(state, wide, preferred_element_type=F32)
            return re_ref[mode] * rotate(ahead - after) + im_ref[mode] * (ahead + after)

        listed(modes // LOT + t, work)
        return carry

    lax.fori_loop(0, CAP, lower, 0)

    if sources is NEAR:

        for w in range(windows):
            acc[here * windows + w] += rotate(
                jnp.dot(ham_ref[...], rho_ref[w], preferred_element_type=F32)
            )

    def leave(r, carry):
        for w in range(windows):
            for shift, out_ref in enumerate(out_refs):
                block = lax.rem(group + shift, blocks) * share
                out_ref[r - begin, w] = acc[r * windows + w, pl.ds(pl.multiple_of(block, share), share), :]
        return carry

    lax.fori_loop(begin, end, leave, 0)


def terms(sources, part, spot, lists, coup_re, coup_im, states, maps_wide, head_cols, rho):
    modes = maps_wide.shape[0] - 1
    windows, share, lanes = rho.shape
    width = head_cols.shape[0]
    return pl.pallas_call(
        functools.partial(terms_kernel, sources, modes, windows, part),
        in_specs=[SMEM] * 4 + [HBM] * len(sources) + [VMEM] * 3,
        out_specs=[VMEM] * (width // share),
        out_shape=[jax.ShapeDtypeStruct((part[1] - part[0], windows, share, lanes), F32)] * (width // share),
        scratch_shapes=[
            pltpu.VMEM((len(sources) * SPAN, width, lanes), BF16),
            pltpu.VMEM((RINGS * windows + 1, width, lanes), F32),
            pltpu.SemaphoreType.DMA((len(sources),)),
        ],
        compiler_params=pltpu.CompilerParams(vmem_limit_bytes=28 * 2**20),
        cost_estimate=pl.CostEstimate(flops=10**9, bytes_accessed=10 * 2**20, transcendentals=0),
    )(spot, lists, coup_re, coup_im, *[states[n] for n, _, _ in sources], maps_wide, head_cols, rho)


def lists_of(steps, parts, modes, spot_ref, heard_ref, out_ref):
    core, along, across, group = spot_ref[0], spot_ref[1], spot_ref[2], spot_ref[3]
    pairs = heard_ref.shape[1]
    windows = pairs // RINGS

    def locate(places):
        owner = lax.shift_right_logical(places * 171, 9)
        z, y, c = lax.shift_right_logical(owner, 4), lax.shift_right_logical(owner, 1) & 7, owner & 1
        off = (jnp.where(core == 0, z, y) - along) & (RINGS - 1)
        source = jnp.full_like(off, -1)
        for n, (_, _, step) in enumerate(steps):
            source = jnp.where(off == -step % RINGS, n, source)
        mine = (jnp.where(core == 0, y, z) == across) & (source >= 0)
        kind = jnp.where(c == core, 0, 1)
        lanes = lax.broadcasted_iota(jnp.int32, places.shape, 1)
        receiver = lax.shift_right_logical(lanes, windows.bit_length() - 1)
        return mine, ((source * 2 + kind) * CAP + places - owner * CAP) * RINGS + receiver

    def square(n, axis):
        return lax.broadcasted_iota(jnp.int32, (n, n), axis)

    def ones(mask):
        return jnp.where(mask, 1.0, 0.0)

    mine, row = locate(heard_ref[:modes])
    ids = lax.broadcasted_iota(jnp.int32, mine.shape, 0)
    below = ones(square(modes, 0) > square(modes, 1))
    rank = jnp.dot(below, ones(mine), preferred_element_type=F32).astype(jnp.int32)
    rank = jnp.where(mine, rank, -1)
    count = jnp.sum(ones(mine), axis=0, keepdims=True)
    value = (ids * 512 + row - modes * 512).astype(F32)
    for n in range(modes):
        found = jnp.sum(jnp.where(rank == n, value, 0.0), axis=0, keepdims=True)
        out_ref[n:n + 1] = found.astype(jnp.int32) + modes * 512

    mine, row = locate(heard_ref[modes:modes + CAP])
    local = heard_ref[modes + CAP:modes + 2 * CAP] - group * modes
    live = mine & (local >= 0) & (local < modes)
    out_ref[modes:modes + CAP] = jnp.where(live, local * 512 + row, 0)

    first = lax.broadcasted_iota(jnp.int32, (1, pairs), 1)
    flags = []
    for begin, end in parts:
        inside = (first >= begin * windows) & (first < end * windows)
        for n in range(modes // LOT):
            flags.append(ones(inside & (count > n * LOT)))
        for t in range(CAP):
            flags.append(ones(inside & live[t:t + 1]))
    total = len(flags)
    flags = jnp.concatenate(flags + [jnp.zeros((pairs - total, pairs), F32)], axis=0)
    turned = (((1,), (1,)), ((), ()))
    down, over = square(pairs, 0), square(pairs, 1)
    chosen = lax.dot_general(ones(down == over), flags, turned, preferred_element_type=F32)
    order = lax.dot_general(ones(down > over), flags, turned, preferred_element_type=F32)
    order = jnp.where(chosen > 0.5, order, -1.0)
    numbers = (down - pairs).astype(F32)
    lanes = over.astype(F32)
    for n in range(total):
        found = jnp.sum(jnp.where(order[:, n:n + 1] == lanes, numbers, 0.0), axis=0, keepdims=True)
        out_ref[modes + CAP + n:modes + CAP + n + 1] = found.astype(jnp.int32) + pairs
    sums = lax.dot_general(jnp.ones((8, pairs), F32), flags, turned, preferred_element_type=F32)
    last = out_ref.shape[0] - 1
    out_ref[last:last + 1] = sums[:1].astype(jnp.int32)


def lists_kernel(kinds, modes, spot_ref, *refs):
    for (steps, parts), heard_ref, out_ref in zip(kinds, refs[:len(kinds)], refs[len(kinds):], strict=True):
        lists_of(steps, parts, modes, spot_ref, heard_ref, out_ref)


def use_lists(kinds, modes, spot, heard):
    rows = [modes + CAP + len(parts) * (modes // LOT + CAP) + 1 for _, parts in kinds]
    return pl.pallas_call(
        functools.partial(lists_kernel, kinds, modes),
        in_specs=[SMEM] + [VMEM] * len(kinds),
        out_specs=[VMEM] * len(kinds),
        out_shape=[jax.ShapeDtypeStruct((n + -n % 8, heard[0].shape[1]), jnp.int32) for n in rows],
        compiler_params=pltpu.CompilerParams(vmem_limit_bytes=8 * 2**20),
        cost_estimate=pl.CostEstimate(flops=10**7, bytes_accessed=2**18, transcendentals=0),
    )(spot, *heard)


def say_kernel(spot_ref, up_ref, down_ref, tri_ref, out_ref):
    windows, modes = up_ref.shape
    shape = (windows, out_ref.shape[2])
    lanes = lax.broadcasted_iota(jnp.int32, shape, 1)
    row = lax.broadcasted_iota(jnp.int32, shape, 0)
    place = jnp.where(lanes == spot_ref[2] * windows + row, 1.0, 0.0)

    def put(values, axis):
        def half(part):
            return lax.dot_general(
                part.astype(F32), place, (((axis,), (0,)), ((), ())), preferred_element_type=F32
            )

        high = lax.shift_right_logical(values, 5)
        return (half(high) * 32.0 + half(values & 31)).astype(jnp.int32)

    up, down, tri = put(up_ref[...], 0), put(down_ref[...], 1), put(tri_ref[...], 1)
    spare = jnp.zeros((out_ref.shape[1] - modes - 2 * CAP, shape[1]), jnp.int32)
    whole = jnp.concatenate([up, down, tri, spare], axis=0)
    for n in range(RINGS):
        out_ref[n] = whole


def say(spot, use_up, use_down, modes_tri):
    windows, modes = use_up.shape
    rows = modes + 2 * CAP
    return pl.pallas_call(
        say_kernel,
        in_specs=[SMEM, VMEM, VMEM, VMEM],
        out_specs=VMEM,
        out_shape=jax.ShapeDtypeStruct((RINGS, rows + -rows % 8, RINGS * windows), jnp.int32),
        cost_estimate=pl.CostEstimate(flops=10**6, bytes_accessed=2**18, transcendentals=0),
    )(spot, use_up, use_down.T, modes_tri.T)


def over_groups(parts, shifts):
    count = len(parts)
    total = parts[0]
    for shift in shifts:
        ring = [(i, (i + shift) % count) for i in range(count)]
        total = total + lax.ppermute(parts[shift].astype(LINK), "grp", ring).astype(F32)
    return total


def on_device(
    states, send_slot, window_tier_states, modes_tri, use_up, use_down,
    hamiltonian, coupling, coup_re, coup_im, decay_rate,
):
    width = hamiltonian.shape[0]
    windows, share = window_tier_states.shape[:2]
    modes = coupling.shape[0]
    group = lax.axis_index("grp").astype(jnp.int32)
    index = lax.axis_index("ado").astype(jnp.int32)
    core, z, y = index & 1, index >> 4, (index >> 1) & 7
    along = jnp.where(core == 0, z, y)
    across = jnp.where(core == 0, y, z)

    spot = jnp.stack([core, along, across, group])

    said = say(spot, use_up, use_down, modes_tri)
    said, slots, store = lax.optimization_barrier((said, send_slot[0, 0], states[0, 0]))
    heard = lax.all_to_all(
        said, "ado", split_axis=0, concat_axis=0, tiled=True, axis_index_groups=DELIVER
    )
    slots = jnp.transpose(slots).reshape(-1)
    sib_store = lax.ppermute(store, "ado", SIBLING)
    sib_slots = lax.ppermute(slots, "ado", SIBLING)
    heard, slots = lax.optimization_barrier((jnp.sum(heard, axis=0), slots))
    heard_far = lax.ppermute(heard, "ado", onward(4))
    picked = pick(spot, slots, sib_slots, store, sib_store)
    maps_wide = jnp.concatenate([doubled(coupling), jnp.zeros((1, 2 * width, 2 * width), BF16)], axis=0)
    head_cols = lax.dynamic_slice_in_dim(hamiltonian, group * share, share, 1)
    shared = (maps_wide, head_cols, window_tier_states)
    picked, heard, heard_far, shared = lax.optimization_barrier((picked, heard, heard_far, shared))

    sent = [
        block if step == 0 else lax.ppermute(block, "ado", onward(step))
        for (step, _), block in zip(SENDS, picked, strict=True)
    ]
    kinds = ((FAR, ((0, RINGS),)), (NEAR, ((0, RINGS),)))
    far_lists, near_lists = use_lists(kinds, modes, spot, (heard_far, heard))

    far = terms(FAR, (0, RINGS, 0), spot, far_lists, coup_re, coup_im, sent, *shared)
    far, near_lists = lax.optimization_barrier((far, near_lists))
    far = lax.ppermute(over_groups(far, (2, 1, 3)).astype(LINK), "ado", onward(4))
    near = terms(NEAR, (0, RINGS, 0), spot, near_lists, coup_re, coup_im, sent, *shared)
    near = over_groups(near, (1, 3, 2))
    summed = lax.all_to_all(
        (near + far.astype(F32)).astype(LINK), "ado", split_axis=0, concat_axis=0, tiled=True,
        axis_index_groups=DELIVER,
    )

    ham_wide = doubled(hamiltonian)
    right_part = jnp.einsum("wab,bc->wac", window_tier_states, ham_wide, preferred_element_type=F32)
    every_mode = jnp.arange(decay_rate.shape[0], dtype=jnp.int32)
    hits = modes_tri[:, :, None] == every_mode
    damping = jnp.sum(jnp.where(hits, decay_rate, 0.0), axis=(1, 2))
    own = rotate(right_part) + damping[:, None, None] * window_tier_states.astype(F32)
    return STEP_WEIGHT * (jnp.sum(summed.astype(F32), axis=0) - own)


def solution(mesh):
    in_specs = (
        P("grp", "ado", None, None, None),
        P("grp", "ado", None, None),
        P("ado", "grp", None),
        P("ado", None),
        P("ado", "grp"),
        P("ado", None),
        P(),
        P("grp", None, None),
        P("grp"),
        P("grp"),
        P(),
    )
    out_specs = P("ado", "grp", None)
    return jax.shard_map(
        on_device, mesh=mesh, in_specs=in_specs, out_specs=out_specs, check_vma=False
    )
```

```python
import functools

import jax
import jax.numpy as jnp
from jax import lax
from jax.experimental import pallas as pl
from jax.experimental.pallas import tpu as pltpu
from jax.sharding import PartitionSpec as P

STEP_WEIGHT = 0.5
F32 = jnp.float32
BF16 = jnp.bfloat16
LINK = jnp.float16
VMEM = pl.BlockSpec(memory_space=pltpu.VMEM)
SMEM = pl.BlockSpec(memory_space=pltpu.SMEM)
HBM = pl.BlockSpec(memory_space=pltpu.HBM)


def doubled(matrices):
    empty = jnp.zeros_like(matrices)
    upper_half = jnp.concatenate([matrices, empty], axis=-1)
    lower_half = jnp.concatenate([empty, matrices], axis=-1)
    return jnp.concatenate([upper_half, lower_half], axis=-2)


def rotate(parts):
    width = parts.shape[-1] // 2
    return jnp.concatenate([parts[..., width:], -parts[..., :width]], axis=-1)


RINGS = 8
CAP = 3
LOT = 4
SPAN = 2 * CAP * RINGS
SENDS = ((1, (-3,)), (-1, (3,)), (2, (2,)), (-2, (-2,)), (1, (1,)), (-1, (-1,)), (0, (4, 0)))
FAR = ((0, 0, 1), (1, 0, -1), (6, 0, 0))
NEAR = ((2, 0, 2), (3, 0, -2), (4, 0, 1), (5, 0, -1), (6, 1, 0))
SIBLING = [(i, i ^ 1) for i in range(2 * RINGS * RINGS)]


def device(core, along, across):
    along, across = along % RINGS, across % RINGS
    return along * 16 + across * 2 if core == 0 else across * 16 + along * 2 + 1


def onward(step):
    return [
        (device(c, a, b), device(c, a + step, b)) for c in range(2) for a in range(RINGS) for b in range(RINGS)
    ]


DELIVER = [[device(c, a, b) for b in range(RINGS)] for c in range(2) for a in range(RINGS)]


def pick_kernel(spot_ref, own_slot, sib_slot, own_ref, sib_hbm, *refs):
    out_refs, (sib_ref, sem) = refs[:-2], refs[-2:]
    copy = pltpu.make_async_copy(sib_hbm, sib_ref, sem)
    copy.start()
    core, along = spot_ref[0], spot_ref[1]
    far = jnp.where(core == 0, 16, 2)
    near = jnp.where(core == 0, 2, 16)
    count = own_slot.shape[0] // CAP
    for kind, (slots, store) in enumerate(((own_slot, own_ref), (sib_slot, sib_ref))):
        if kind == 1:
            copy.wait()
        for (_, group), out_ref in zip(SENDS, out_refs, strict=True):
            for place, ahead in enumerate(group):
                first = lax.rem(along + ahead + RINGS, RINGS) * far + core
                for c in range(CAP):
                    for r in range(RINGS):
                        slot = slots[c * count + first + r * near]
                        row = place * SPAN + kind * CAP * RINGS + c * RINGS + r
                        out_ref[row] = store[jnp.maximum(slot, 0)]


def pick(spot, own_slots, sib_slots, own, sib):
    tile = own.shape[1:]
    return pl.pallas_call(
        pick_kernel,
        in_specs=[SMEM, SMEM, SMEM, VMEM, HBM],
        out_specs=[VMEM] * len(SENDS),
        out_shape=[jax.ShapeDtypeStruct((len(group) * SPAN,) + tile, own.dtype) for _, group in SENDS],
        scratch_shapes=[pltpu.VMEM(own.shape, own.dtype), pltpu.SemaphoreType.DMA],
        compiler_params=pltpu.CompilerParams(vmem_limit_bytes=24 * 2**20),
        cost_estimate=pl.CostEstimate(flops=0, bytes_accessed=10 * 2**20, transcendentals=0),
    )(spot, own_slots, sib_slots, own, sib)


def terms_kernel(sources, modes, windows, part, spot_ref, list_ref, re_ref, im_ref, *refs):
    count = len(sources)
    state_refs, (wide_ref, ham_ref, rho_ref) = refs[:count], refs[count:count + 3]
    out_refs, (flat, acc, sems) = refs[count + 3:-3], refs[-3:]
    here, group = spot_ref[2], spot_ref[3]
    share = rho_ref.shape[1]
    width = ham_ref.shape[0]
    pairs = RINGS * windows
    blocks = width // share
    begin, end, slot = part
    levels = modes // LOT + CAP
    downs, extra, counts = modes, modes + CAP + slot * levels, list_ref.shape[0] - 1

    copies = [
        pltpu.make_async_copy(
            state_refs[n].at[pl.ds(place * SPAN, SPAN)], flat.at[pl.ds(n * SPAN, SPAN)], sems.at[n]
        )
        for n, (_, place, _) in enumerate(sources)
    ]
    for copy in copies:
        copy.start()
    for copy in copies:
        copy.wait()

    def lot(pair, base):
        entries = [list_ref[base + n, pair] for n in range(LOT)]
        maps = [lax.shift_right_logical(e, 9) for e in entries]
        tiles = [flat[e & 511] for e in entries]
        rows = [
            wide_ref[maps[n], :width, :] + wide_ref[maps[n + 1], width:, :] for n in range(0, LOT, 2)
        ]
        left = jnp.dot(
            jnp.concatenate(rows, axis=1), jnp.concatenate(tiles, axis=0), preferred_element_type=F32
        )
        right = jnp.dot(
            jnp.concatenate(tiles, axis=1),
            jnp.concatenate([wide_ref[m] for m in maps], axis=0),
            preferred_element_type=F32,
        )
        return rotate(left - right)

    together = 32

    def first(index, carry):
        for j in range(together):
            pair = index * together + j
            acc[pair] = lot(pair, 0)
        return carry

    lax.fori_loop(begin * windows // together, end * windows // together, first, 0)

    def listed(level, work):
        def some(index, carry):
            found = [list_ref[extra + level, index * 4 + j] for j in range(4)]
            values = [work(jnp.minimum(pair, pairs - 1)) for pair in found]
            for pair, value in zip(found, values, strict=True):
                acc[pair] += value
            return carry

        lax.fori_loop(0, lax.shift_right_logical(list_ref[counts, slot * levels + level] + 3, 2), some, 0)

    def more(level, carry):
        listed(level, lambda pair: lot(pair, level * LOT))
        return carry

    lax.fori_loop(1, modes // LOT, more, 0)

    def lower(t, carry):
        def work(pair):
            entry = list_ref[downs + t, pair]
            mode = lax.shift_right_logical(entry, 9)
            state = flat[entry & 511]
            wide = wide_ref[mode]
            ahead = jnp.dot(wide[:width, :width], state, preferred_element_type=F32)
            after = jnp.dot(state, wide, preferred_element_type=F32)
            return re_ref[mode] * rotate(ahead - after) + im_ref[mode] * (ahead + after)

        listed(modes // LOT + t, work)
        return carry

    lax.fori_loop(0, CAP, lower, 0)

    if sources is NEAR:

        for w in range(windows):
            acc[here * windows + w] += rotate(
                jnp.dot(ham_ref[...], rho_ref[w], preferred_element_type=F32)
            )

    def leave(r, carry):
        for w in range(windows):
            for shift, out_ref in enumerate(out_refs):
                block = lax.rem(group + shift, blocks) * share
                out_ref[r - begin, w] = acc[r * windows + w, pl.ds(pl.multiple_of(block, share), share), :]
        return carry

    lax.fori_loop(begin, end, leave, 0)


def terms(sources, part, spot, lists, coup_re, coup_im, states, maps_wide, head_cols, rho):
    modes = maps_wide.shape[0] - 1
    windows, share, lanes = rho.shape
    width = head_cols.shape[0]
    return pl.pallas_call(
        functools.partial(terms_kernel, sources, modes, windows, part),
        in_specs=[SMEM] * 4 + [HBM] * len(sources) + [VMEM] * 3,
        out_specs=[VMEM] * (width // share),
        out_shape=[jax.ShapeDtypeStruct((part[1] - part[0], windows, share, lanes), F32)] * (width // share),
        scratch_shapes=[
            pltpu.VMEM((len(sources) * SPAN, width, lanes), BF16),
            pltpu.VMEM((RINGS * windows + 1, width, lanes), F32),
            pltpu.SemaphoreType.DMA((len(sources),)),
        ],
        compiler_params=pltpu.CompilerParams(vmem_limit_bytes=28 * 2**20),
        cost_estimate=pl.CostEstimate(flops=10**9, bytes_accessed=10 * 2**20, transcendentals=0),
    )(spot, lists, coup_re, coup_im, *[states[n] for n, _, _ in sources], maps_wide, head_cols, rho)


def lists_of(steps, parts, modes, spot_ref, heard_ref, out_ref):
    core, along, across, group = spot_ref[0], spot_ref[1], spot_ref[2], spot_ref[3]
    pairs = heard_ref.shape[1]
    windows = pairs // RINGS

    def locate(places):
        owner = lax.shift_right_logical(places * 171, 9)
        z, y, c = lax.shift_right_logical(owner, 4), lax.shift_right_logical(owner, 1) & 7, owner & 1
        off = (jnp.where(core == 0, z, y) - along) & (RINGS - 1)
        source = jnp.full_like(off, -1)
        for n, (_, _, step) in enumerate(steps):
            source = jnp.where(off == -step % RINGS, n, source)
        mine = (jnp.where(core == 0, y, z) == across) & (source >= 0)
        kind = jnp.where(c == core, 0, 1)
        lanes = lax.broadcasted_iota(jnp.int32, places.shape, 1)
        receiver = lax.shift_right_logical(lanes, windows.bit_length() - 1)
        return mine, ((source * 2 + kind) * CAP + places - owner * CAP) * RINGS + receiver

    def square(n, axis):
        return lax.broadcasted_iota(jnp.int32, (n, n), axis)

    def ones(mask):
        return jnp.where(mask, 1.0, 0.0)

    mine, row = locate(heard_ref[:modes])
    ids = lax.broadcasted_iota(jnp.int32, mine.shape, 0)
    below = ones(square(modes, 0) > square(modes, 1))
    rank = jnp.dot(below, ones(mine), preferred_element_type=F32).astype(jnp.int32)
    rank = jnp.where(mine, rank, -1)
    count = jnp.sum(ones(mine), axis=0, keepdims=True)
    value = (ids * 512 + row - modes * 512).astype(F32)
    for n in range(modes):
        found = jnp.sum(jnp.where(rank == n, value, 0.0), axis=0, keepdims=True)
        out_ref[n:n + 1] = found.astype(jnp.int32) + modes * 512

    mine, row = locate(heard_ref[modes:modes + CAP])
    local = heard_ref[modes + CAP:modes + 2 * CAP] - group * modes
    live = mine & (local >= 0) & (local < modes)
    out_ref[modes:modes + CAP] = jnp.where(live, local * 512 + row, 0)

    first = lax.broadcasted_iota(jnp.int32, (1, pairs), 1)
    flags = []
    for begin, end in parts:
        inside = (first >= begin * windows) & (first < end * windows)
        for n in range(modes // LOT):
            flags.append(ones(inside & (count > n * LOT)))
        for t in range(CAP):
            flags.append(ones(inside & live[t:t + 1]))
    total = len(flags)
    flags = jnp.concatenate(flags + [jnp.zeros((pairs - total, pairs), F32)], axis=0)
    turned = (((1,), (1,)), ((), ()))
    down, over = square(pairs, 0), square(pairs, 1)
    chosen = lax.dot_general(ones(down == over), flags, turned, preferred_element_type=F32)
    order = lax.dot_general(ones(down > over), flags, turned, preferred_element_type=F32)
    order = jnp.where(chosen > 0.5, order, -1.0)
    numbers = (down - pairs).astype(F32)
    lanes = over.astype(F32)
    for n in range(total):
        found = jnp.sum(jnp.where(order[:, n:n + 1] == lanes, numbers, 0.0), axis=0, keepdims=True)
        out_ref[modes + CAP + n:modes + CAP + n + 1] = found.astype(jnp.int32) + pairs
    sums = lax.dot_general(jnp.ones((8, pairs), F32), flags, turned, preferred_element_type=F32)
    last = out_ref.shape[0] - 1
    out_ref[last:last + 1] = sums[:1].astype(jnp.int32)


def lists_kernel(kinds, modes, spot_ref, *refs):
    for (steps, parts), heard_ref, out_ref in zip(kinds, refs[:len(kinds)], refs[len(kinds):], strict=True):
        lists_of(steps, parts, modes, spot_ref, heard_ref, out_ref)


def use_lists(kinds, modes, spot, heard):
    rows = [modes + CAP + len(parts) * (modes // LOT + CAP) + 1 for _, parts in kinds]
    return pl.pallas_call(
        functools.partial(lists_kernel, kinds, modes),
        in_specs=[SMEM] + [VMEM] * len(kinds),
        out_specs=[VMEM] * len(kinds),
        out_shape=[jax.ShapeDtypeStruct((n + -n % 8, heard[0].shape[1]), jnp.int32) for n in rows],
        compiler_params=pltpu.CompilerParams(vmem_limit_bytes=8 * 2**20),
        cost_estimate=pl.CostEstimate(flops=10**7, bytes_accessed=2**18, transcendentals=0),
    )(spot, *heard)


def say_kernel(spot_ref, up_ref, down_ref, tri_ref, out_ref):
    windows, modes = up_ref.shape
    shape = (windows, out_ref.shape[2])
    lanes = lax.broadcasted_iota(jnp.int32, shape, 1)
    row = lax.broadcasted_iota(jnp.int32, shape, 0)
    place = jnp.where(lanes == spot_ref[2] * windows + row, 1.0, 0.0)

    def put(values, axis):
        def half(part):
            return lax.dot_general(
                part.astype(F32), place, (((axis,), (0,)), ((), ())), preferred_element_type=F32
            )

        high = lax.shift_right_logical(values, 5)
        return (half(high) * 32.0 + half(values & 31)).astype(jnp.int32)

    up, down, tri = put(up_ref[...], 0), put(down_ref[...], 1), put(tri_ref[...], 1)
    spare = jnp.zeros((out_ref.shape[1] - modes - 2 * CAP, shape[1]), jnp.int32)
    whole = jnp.concatenate([up, down, tri, spare], axis=0)
    for n in range(RINGS):
        out_ref[n] = whole


def say(spot, use_up, use_down, modes_tri):
    windows, modes = use_up.shape
    rows = modes + 2 * CAP
    return pl.pallas_call(
        say_kernel,
        in_specs=[SMEM, VMEM, VMEM, VMEM],
        out_specs=VMEM,
        out_shape=jax.ShapeDtypeStruct((RINGS, rows + -rows % 8, RINGS * windows), jnp.int32),
        cost_estimate=pl.CostEstimate(flops=10**6, bytes_accessed=2**18, transcendentals=0),
    )(spot, use_up, use_down.T, modes_tri.T)


def over_groups(parts):
    count = len(parts)
    total = parts[0]
    for shift in (2, 1, 3):
        ring = [(i, (i + shift) % count) for i in range(count)]
        total = total + lax.ppermute(parts[shift].astype(LINK), "grp", ring).astype(F32)
    return total


def on_device(
    states, send_slot, window_tier_states, modes_tri, use_up, use_down,
    hamiltonian, coupling, coup_re, coup_im, decay_rate,
):
    width = hamiltonian.shape[0]
    windows, share = window_tier_states.shape[:2]
    modes = coupling.shape[0]
    group = lax.axis_index("grp").astype(jnp.int32)
    index = lax.axis_index("ado").astype(jnp.int32)
    core, z, y = index & 1, index >> 4, (index >> 1) & 7
    along = jnp.where(core == 0, z, y)
    across = jnp.where(core == 0, y, z)

    spot = jnp.stack([core, along, across, group])

    said = say(spot, use_up, use_down, modes_tri)
    said, slots, store = lax.optimization_barrier((said, send_slot[0, 0], states[0, 0]))
    heard = lax.all_to_all(
        said, "ado", split_axis=0, concat_axis=0, tiled=True, axis_index_groups=DELIVER
    )
    slots = jnp.transpose(slots).reshape(-1)
    sib_store = lax.ppermute(store, "ado", SIBLING)
    sib_slots = lax.ppermute(slots, "ado", SIBLING)
    heard, slots = lax.optimization_barrier((jnp.sum(heard, axis=0), slots))
    heard_far = lax.ppermute(heard, "ado", onward(4))
    picked = pick(spot, slots, sib_slots, store, sib_store)
    maps_wide = jnp.concatenate([doubled(coupling), jnp.zeros((1, 2 * width, 2 * width), BF16)], axis=0)
    head_cols = lax.dynamic_slice_in_dim(hamiltonian, group * share, share, 1)
    shared = (maps_wide, head_cols, window_tier_states)
    picked, heard, heard_far, shared = lax.optimization_barrier((picked, heard, heard_far, shared))

    sent = [
        block if step == 0 else lax.ppermute(block, "ado", onward(step))
        for (step, _), block in zip(SENDS, picked, strict=True)
    ]
    kinds = ((FAR, ((0, RINGS),)), (NEAR, ((0, RINGS),)))
    far_lists, near_lists = use_lists(kinds, modes, spot, (heard_far, heard))

    far = terms(FAR, (0, RINGS, 0), spot, far_lists, coup_re, coup_im, sent, *shared)
    far, near_lists = lax.optimization_barrier((far, near_lists))
    far = lax.ppermute(over_groups(far).astype(LINK), "ado", onward(4))
    near = over_groups(terms(NEAR, (0, RINGS, 0), spot, near_lists, coup_re, coup_im, sent, *shared))
    summed = lax.all_to_all(
        (near + far.astype(F32)).astype(LINK), "ado", split_axis=0, concat_axis=0, tiled=True,
        axis_index_groups=DELIVER,
    )

    ham_wide = doubled(hamiltonian)
    right_part = jnp.einsum("wab,bc->wac", window_tier_states, ham_wide, preferred_element_type=F32)
    every_mode = jnp.arange(decay_rate.shape[0], dtype=jnp.int32)
    hits = modes_tri[:, :, None] == every_mode
    damping = jnp.sum(jnp.where(hits, decay_rate, 0.0), axis=(1, 2))
    own = rotate(right_part) + damping[:, None, None] * window_tier_states.astype(F32)
    return STEP_WEIGHT * (jnp.sum(summed.astype(F32), axis=0) - own)


def solution(mesh):
    in_specs = (
        P("grp", "ado", None, None, None),
        P("grp", "ado", None, None),
        P("ado", "grp", None),
        P("ado", None),
        P("ado", "grp"),
        P("ado", None),
        P(),
        P("grp", None, None),
        P("grp"),
        P("grp"),
        P(),
    )
    out_specs = P("ado", "grp", None)
    return jax.shard_map(
        on_device, mesh=mesh, in_specs=in_specs, out_specs=out_specs, check_vma=False
    )
```
